512 devices in a mesh: tm: 16 (over z_hi, y, core), rows: 32 (over x, z_lo).
Axes of the slice: x: 4, y: 4, z: 16 (z_hi: 2, z_lo: 8; z = z_hi * 8 + z_lo), core: 2. Of those that a mesh axis runs over, the one named last changes fastest.
Arguments:
- video_clip: bfloat16 [32, 64, 64, 128], P('tm', 'rows'), may hold values from -6 to 6
- first_kernel: bfloat16 [3, 3, 3, 128, 128], replicated, may hold values from -0.109375 to 0.109375
- second_kernel: bfloat16 [3, 3, 3, 128, 128], replicated, may hold values from -0.109375 to 0.109375
- cotangent: bfloat16 [32, 64, 64, 128], P('tm', 'rows'), may hold values from -6 to 6
Outputs:
- input_grad: bfloat16 [32, 64, 64, 128], P('tm', 'rows')
- weight_grads: float32 [2, 442368], P(None, ('tm', 'rows'))
The draws below stay inside these ranges and needn't reach their ends.
All inputs are finite; a program needn't handle non-finite values.
Results may differ from the reference program's by a relative error of at most 0.0046.
Values may be sent and summed in bfloat16 or wider, within the bound.
No kernel may reach another device: no remote copies, remote signals or barrier semaphores. Data moves between devices by JAX's collectives and lax.ppermute only.
A program may use at most 64 MiB of HBM per device.

```python
import math
import jax
import jax.numpy as jnp
from jax import lax

C = 128
W = 64
NF = 32
H = 64


def block_scale(stream_key, shape, cuts, least, largest):
    gain = 1.0
    for dim, shards_of in cuts:
        steps = jax.random.uniform(jax.random.fold_in(jax.random.fold_in(stream_key, 6), dim), (shards_of,), jnp.float32, least / len(cuts), largest / len(cuts))
        gain = gain * jnp.repeat(jnp.exp(steps), shape[dim] // shards_of).reshape((-1,) + (1,) * (len(shape) - 1 - dim))
    return gain


def scatter_about(own_key, extent, deviation, limit, cuts=(), kind=jnp.bfloat16):
    loudness = block_scale(own_key, extent, cuts, -0.22, 0.18) if cuts else 1.0
    drawn = jax.random.normal(own_key, extent, jnp.float32) * deviation * loudness
    return jnp.minimum(jnp.maximum(drawn, -limit), limit).astype(kind)


def setup_inputs(seed: int = 0) -> dict:
    splits = jax.random.split(jax.random.key(seed), 5)
    video_clip = scatter_about(splits[0], (NF, H, W, C), 1.0, 6.0, ((0, 16), (1, 32)))
    first_kernel = scatter_about(splits[1], (3, 3, 3, C, C), (27 * C) ** -0.5, 0.109375)
    second_kernel = scatter_about(splits[2], (3, 3, 3, C, C), (27 * C) ** -0.5, 0.109375)
    cotangent = scatter_about(splits[3], (NF, H, W, C), 1.0, 6.0, ((0, 16), (1, 32)))
    return {"video_clip": video_clip, "first_kernel": first_kernel, "second_kernel": second_kernel, "cotangent": cotangent}


def pad_past(volume):
    leading = volume[:1]
    volume = jnp.concatenate([leading, leading, volume], axis=0)
    return jnp.pad(volume, ((0, 0), (1, 1), (1, 1), (0, 0)))

def pad_future(volume):
    blanks = jnp.zeros((2,) + volume.shape[1:], volume.dtype)
    volume = jnp.concatenate([volume, blanks], axis=0)
    return jnp.pad(volume, ((0, 0), (1, 1), (1, 1), (0, 0)))

def correlate(source, kernel, frames, row_count):
    columns = source.shape[2] - 2
    time_taps = kernel.shape[0]
    out_chans = kernel.shape[-1]
    running = jnp.zeros((frames * row_count * columns, out_chans), jnp.float32)
    for tap_t in range(time_taps):
        for tap_h in range(3):
            stripe = source[tap_t:tap_t + frames, tap_h:tap_h + row_count]
            triple = jnp.concatenate([stripe[:, :, tap_w:tap_w + columns] for tap_w in range(3)], axis=-1)
            triple = triple.reshape(frames * row_count * columns, -1)
            running = running + jnp.dot(triple, kernel[tap_t, tap_h].reshape(-1, out_chans), preferred_element_type=jnp.float32)
    return running.reshape(frames, row_count, columns, out_chans)

def weight_terms(source, gradient, frames, row_count):
    columns = source.shape[2] - 2
    flat_grad = gradient.reshape(frames * row_count * columns, -1)
    pieces = []
    for tap_t in range(3):
        for tap_h in range(3):
            stripe = source[tap_t:tap_t + frames, tap_h:tap_h + row_count]
            triple = jnp.concatenate([stripe[:, :, tap_w:tap_w + columns] for tap_w in range(3)], axis=-1)
            triple = triple.reshape(frames * row_count * columns, -1)
            pieces.append(lax.dot_general(triple, flat_grad, (((0,), (0,)), ((), ())), preferred_element_type=jnp.float32))
    return jnp.stack(pieces).reshape(-1)

def flipped(kernel):
    return jnp.flip(kernel, (0, 1, 2)).transpose(0, 1, 2, 4, 3)

def fold_first(source, turned, row_count):
    leading = jnp.stack([source[0], source[0], source[1]])
    taps = jnp.stack([turned[2], turned[1], turned[2]])
    return correlate(leading, taps, 1, row_count)[0]

def silu_slope(values):
    sig_value = jax.nn.sigmoid(values)
    return sig_value * (1.0 + values * (1.0 - sig_value))

def transpose_conv(gradient, kernel, frames, row_count):
    source = pad_future(gradient)
    turned = flipped(kernel)
    result = correlate(source, turned, frames, row_count)
    return result.at[0].add(fold_first(source, turned, row_count))

def reference(video_clip, first_kernel, second_kernel, cotangent):
    frames, height, columns, channels = video_clip.shape
    grad_scale = 1.0 / math.sqrt(frames * height * columns)
    clip_ext = pad_past(video_clip)
    pre_act = correlate(clip_ext, first_kernel, frames, height).astype(jnp.bfloat16)
    hidden = jax.nn.silu(pre_act.astype(jnp.float32)).astype(jnp.bfloat16)
    hidden_ext = pad_past(hidden)
    back_grad = transpose_conv(cotangent, second_kernel, frames, height)
    act_grad = (back_grad * silu_slope(pre_act.astype(jnp.float32))).astype(jnp.bfloat16)
    second_terms = weight_terms(hidden_ext, cotangent, frames, height)
    branch_grad = transpose_conv(act_grad, first_kernel, frames, height)
    input_grad = (cotangent.astype(jnp.float32) + branch_grad).astype(jnp.bfloat16)
    first_terms = weight_terms(clip_ext, act_grad, frames, height)
    weight_grads = jnp.stack([first_terms, second_terms]) * grad_scale
    return (input_grad, weight_grads)
```

```python
import math

import jax
import jax.numpy as jnp
import numpy as np
from jax import lax
from jax.experimental import pallas as pl
from jax.experimental.pallas import tpu as pltpu
from jax.sharding import Mesh, PartitionSpec as P

TM = ("zh", "y", "c")
ROWS = ("x", "zl")
VMEM = pl.BlockSpec(memory_space=pltpu.VMEM)
PARAMS = pltpu.CompilerParams(vmem_limit_bytes=48 * 1024 * 1024)


def contract_first(lhs, rhs):
    return lax.dot_general(lhs, rhs, (((0,), (0,)), ((), ())), preferred_element_type=jnp.float32)


def fill_triples(src_ref, up_ref, dn_ref, triples_ref, frames):
    columns = src_ref.shape[2]
    chans = src_ref.shape[3]
    col = lax.broadcasted_iota(jnp.int32, (columns, chans), 0)
    for f in range(frames):
        for r in range(4):
            cells = up_ref[f] if r == 0 else dn_ref[f] if r == 3 else src_ref[f, r - 1]
            wide = cells.astype(jnp.float32)
            before = jnp.where(col == 0, 0.0, pltpu.roll(wide, 1, 0))
            after = jnp.where(col == columns - 1, 0.0, pltpu.roll(wide, columns - 1, 0))
            triples_ref[f, r, :, 0:chans] = before.astype(cells.dtype)
            triples_ref[f, r, :, chans : 2 * chans] = cells
            triples_ref[f, r, :, 2 * chans : 3 * chans] = after.astype(cells.dtype)


def stripe(triples_ref, f, count, b):
    part = triples_ref[f : f + count, b : b + 2]
    return part.reshape(count * 2 * part.shape[2], part.shape[3])


def conv_all(triples_ref, kernel_ref, frames):
    total = None
    for a in range(3):
        for b in range(3):
            term = jnp.dot(
                stripe(triples_ref, a, frames, b),
                kernel_ref[a * 3 + b],
                preferred_element_type=jnp.float32,
            )
            total = term if total is None else total + term
    return total


def fold_all(triples_ref, kernel_ref):
    total = None
    for f, a in ((0, 2), (0, 1), (1, 2)):
        for b in range(3):
            term = jnp.dot(
                stripe(triples_ref, f, 1, b),
                kernel_ref[a * 3 + b],
                preferred_element_type=jnp.float32,
            )
            total = term if total is None else total + term
    return total


def first_conv_kernel(src_ref, up_ref, dn_ref, kernel_ref, out_ref, triples_ref):
    fill_triples(src_ref, up_ref, dn_ref, triples_ref, 6)
    out_ref[...] = conv_all(triples_ref, kernel_ref, 4)

    @pl.when((lax.axis_index("c") == 1) & (lax.axis_index("zh") == 0) & (lax.axis_index("y") == 0))
    def _():
        out_ref[0:128, :] += fold_all(triples_ref, kernel_ref)


def input_conv_kernel(src_ref, up_ref, dn_ref, kernel_ref, cot_ref, out_ref, triples_ref, sum_ref):
    fill_triples(src_ref, up_ref, dn_ref, triples_ref, 4)
    sum_ref[...] = conv_all(triples_ref, kernel_ref, 2)

    @pl.when((lax.axis_index("c") == 0) & (lax.axis_index("zh") == 0) & (lax.axis_index("y") == 0))
    def _():
        sum_ref[0:128, :] += fold_all(triples_ref, kernel_ref)

    cot = cot_ref[...].reshape(256, 128).astype(jnp.float32)
    out_ref[...] = (cot + sum_ref[...]).astype(jnp.bfloat16).reshape(out_ref.shape)


def grads_kernel(own_ref, other_ref, triples_ref, send_ref, act_ref, terms_ref):
    core = lax.axis_index("c")
    own, other = own_ref[...], other_ref[...]
    pre_act = jnp.where(core == 0, own, other).astype(jnp.bfloat16).astype(jnp.float32)
    back_grad = jnp.where(core == 0, other, own)
    sig = 1.0 / (1.0 + jnp.exp(-pre_act))
    act_grad = (back_grad * (sig * (1.0 + pre_act * (1.0 - sig)))).astype(jnp.bfloat16)
    hidden = (pre_act * sig).astype(jnp.bfloat16)
    act_ref[...] = act_grad.reshape(act_ref.shape)

    @pl.when(core == 0)
    def _():
        for a in range(3):
            for b in range(3):
                start = (a * 3 + b) * 384
                terms_ref[start : start + 384, :] = contract_first(stripe(triples_ref, a, 4, b), act_grad)

    @pl.when(core == 1)
    def _():
        for a in range(3):
            for b in range(3):
                part = contract_first(hidden, stripe(triples_ref, a, 4, b))
                for d in range(3):
                    start = ((2 - a) * 9 + (2 - b) * 3 + (2 - d)) * 128
                    terms_ref[start : start + 128, :] = part[:, d * 128 : (d + 1) * 128]

    @pl.when((core == 1) & (lax.axis_index("zh") == 0) & (lax.axis_index("y") == 0))
    def _():
        for f, a in ((0, 2), (0, 1), (1, 2)):
            for b in range(3):
                part = contract_first(hidden[0:128], stripe(triples_ref, f, 1, b))
                for d in range(3):
                    start = ((2 - a) * 9 + (2 - b) * 3 + (2 - d)) * 128
                    terms_ref[start : start + 128, :] += part[:, d * 128 : (d + 1) * 128]

    for y in range(4):
        for x in range(4):
            blocks = []
            for zh in range(2):
                for c in range(2):
                    start = 54 * (((zh * 4 + y) * 2 + c) * 4 + x)
                    blocks.append(terms_ref[start : start + 54, :])
            blocks.append(jnp.zeros((8, 128), jnp.float32))
            send_ref[y * 4 + x] = jnp.concatenate(blocks, axis=0).astype(jnp.bfloat16)


def plane_sum_kernel(got_ref, send_ref, sum_ref):
    total = got_ref[0].astype(jnp.float32)
    for k in range(1, 16):
        total = total + got_ref[k].astype(jnp.float32)
    sum_ref[...] = total
    lane = lax.broadcasted_iota(jnp.int32, (8, 128), 1)
    for zh in range(2):
        for c in range(2):
            for zl in range(8):
                value = (zh * 2 + c) * 54 * 128 + zl * 864
                row, shift = value // 128, value % 128
                piece = sum_ref[row : row + 8, :]
                if shift:
                    after = sum_ref[row + 1 : row + 9, :]
                    piece = jnp.where(
                        lane < 128 - shift,
                        pltpu.roll(piece, 128 - shift, 1),
                        pltpu.roll(after, 128 - shift, 1),
                    )
                send_ref[zh * 8 + zl, c] = piece


def line_sum_kernel(got_ref, own_ref, send_ref):
    core = lax.axis_index("c")
    total = got_ref[0]
    for k in range(1, 16):
        total = total + got_ref[k]
    own_ref[...] = jnp.where(core == 0, total[0], total[1])
    send_ref[...] = jnp.where(core == 0, total[1], total[0])


def place_kernel(scale, own_ref, other_ref, out_ref):
    core = lax.axis_index("c")
    own, other = own_ref[...] * scale, other_ref[...] * scale
    shares = (jnp.where(core == 0, own, other), jnp.where(core == 0, other, own))
    for k in range(2):
        for r in range(7):
            width = min(128, 864 - 128 * r)
            out_ref[k : k + 1, 128 * r : 128 * r + width] = shares[k][r : r + 1, :width]


def call(kernel, out_shape, *args, scratch=()):
    many = isinstance(out_shape, (list, tuple))
    return pl.pallas_call(
        kernel,
        out_shape=out_shape,
        in_specs=[VMEM] * len(args),
        out_specs=[VMEM] * len(out_shape) if many else VMEM,
        scratch_shapes=scratch,
        compiler_params=PARAMS,
    )(*args)


def shaped(shape, dtype):
    return jax.ShapeDtypeStruct(shape, dtype)


def flipped(kernel):
    return jnp.flip(kernel, (0, 1, 2)).transpose(0, 1, 2, 4, 3)


def exchange_rows(source):
    count = lax.axis_size(ROWS)
    up = lax.ppermute(source[:, 1], ROWS, [(i, i + 1) for i in range(count - 1)])
    down = lax.ppermute(source[:, 0], ROWS, [(i + 1, i) for i in range(count - 1)])
    return up, down


SWAP = [(0, 1), (1, 0)]


def per_device(video_clip, first_kernel, second_kernel, cotangent):
    bf16, f32 = jnp.bfloat16, jnp.float32
    core = lax.axis_index("c")
    chip = lax.axis_index(("zh", "y"))
    other_cores = lax.ppermute(jnp.where(core == 0, cotangent, video_clip), "c", SWAP)
    beyond_pairs = [(2 * k + 1, 2 * k + 2) for k in range(7)] + [(2 * k + 2, 2 * k + 1) for k in range(7)]
    beyond = lax.ppermute(jnp.where(core == 0, cotangent, video_clip), TM, beyond_pairs)
    kernel = jnp.where(core == 0, first_kernel, flipped(second_kernel)).reshape(9, 384, 128)
    first_back = flipped(first_kernel).reshape(9, 384, 128)
    repeated = jnp.broadcast_to(video_clip[:1], video_clip.shape)
    beyond = jnp.where((core == 0) & (chip == 0), repeated, beyond)
    source = jnp.where(
        core == 0,
        jnp.concatenate([beyond, video_clip, other_cores], 0),
        jnp.concatenate([other_cores, cotangent, beyond], 0),
    )
    up, down = exchange_rows(source)
    own, triples = call(
        first_conv_kernel,
        (shaped((512, 128), f32), shaped((6, 4, 64, 384), bf16)),
        source, up, down, kernel,
    )
    other = lax.ppermute(own, "c", SWAP)
    send, act_grad = call(
        grads_kernel,
        (shaped((16, 224, 128), bf16), shaped((4, 2, 64, 128), bf16)),
        own, other, triples,
        scratch=[pltpu.VMEM((3456, 128), f32)],
    )
    got = lax.all_to_all(send, ("y", "x"), 0, 0, tiled=True)
    send = call(plane_sum_kernel, shaped((16, 2, 8, 128), f32), got, scratch=[pltpu.VMEM((224, 128), f32)])
    got = lax.all_to_all(send, ("zh", "zl"), 0, 0, tiled=True)
    own_share, send_share = call(line_sum_kernel, (shaped((8, 128), f32),) * 2, got)
    other_share = lax.ppermute(send_share, "c", SWAP)
    scale = 1.0 / math.sqrt(131072)
    weight_grads = call(
        lambda *refs: place_kernel(scale, *refs), shaped((2, 864), f32), own_share, other_share
    )
    later = lax.ppermute(act_grad[:2], TM, [(2 * k + 2, 2 * k + 1) for k in range(7)])
    grad_source = jnp.where(core == 0, act_grad, jnp.concatenate([act_grad[2:], later], 0))
    up, down = exchange_rows(grad_source)
    input_grad = call(
        input_conv_kernel,
        shaped((2, 2, 64, 128), bf16),
        grad_source, up, down, first_back, cotangent,
        scratch=[pltpu.VMEM((4, 4, 64, 384), bf16), pltpu.VMEM((256, 128), f32)],
    )
    return input_grad, weight_grads


def solution(mesh):
    fine = Mesh(np.asarray(mesh.devices).reshape(2, 4, 2, 4, 8), TM + ROWS)
    return jax.shard_map(
        per_device,
        mesh=fine,
        in_specs=(P(TM, ROWS, None, None), P(), P(), P(TM, ROWS, None, None)),
        out_specs=(P(TM, ROWS, None, None), P(None, TM + ROWS)),
        check_vma=False,
    )
```

```python
import math

import jax
import jax.numpy as jnp
import numpy as np
from jax import lax
from jax.experimental import pallas as pl
from jax.experimental.pallas import tpu as pltpu
from jax.sharding import Mesh, PartitionSpec as P

TM = ("zh", "y", "c")
ROWS = ("x", "zl")
VMEM = pl.BlockSpec(memory_space=pltpu.VMEM)
PARAMS = pltpu.CompilerParams(vmem_limit_bytes=48 * 1024 * 1024)


SWAP = [(0, 1), (1, 0)]
NEAR_ROWS = [(r, r ^ 1) for r in range(32)]
FAR_GROUPS = [
    [t * 32 + r for t in (2 * k + 1, (2 * k + 2) % 16) for r in (2 * s + 1, (2 * s + 2) % 32)]
    for k in range(8)
    for s in range(16)
]


def place():
    core = lax.axis_index("c")
    chip = lax.axis_index("zh") * 4 + lax.axis_index("y")
    slab = lax.axis_index("x") * 8 + lax.axis_index("zl")
    odd = slab & 1
    return core, chip, slab, odd, 2 * (1 - core) + (1 - odd)


def contract_first(lhs, rhs):
    return lax.dot_general(lhs, rhs, (((0,), (0,)), ((), ())), preferred_element_type=jnp.float32)


def fill_triples(src_ref, far_ref, near_ref, triples_ref, frames):
    odd = place()[3]
    columns = src_ref.shape[2]
    chans = src_ref.shape[3]
    col = lax.broadcasted_iota(jnp.int32, (columns, chans), 0)
    for f in range(frames):
        for r in range(4):
            if r in (0, 3):
                cells = jnp.where(odd == (r == 3), far_ref[f], near_ref[f])
            else:
                cells = src_ref[f, r - 1]
            wide = cells.astype(jnp.float32)
            before = jnp.where(col == 0, 0.0, pltpu.roll(wide, 1, 0))
            after = jnp.where(col == columns - 1, 0.0, pltpu.roll(wide, columns - 1, 0))
            triples_ref[f, r, :, 0:chans] = before.astype(cells.dtype)
            triples_ref[f, r, :, chans : 2 * chans] = cells
            triples_ref[f, r, :, 2 * chans : 3 * chans] = after.astype(cells.dtype)


def stripe(triples_ref, f, count, b):
    part = triples_ref[f : f + count, b : b + 2]
    return part.reshape(count * 2 * part.shape[2], part.shape[3])


def conv_all(triples_ref, kernel_ref, frames):
    total = None
    for a in range(3):
        for b in range(3):
            term = jnp.dot(
                stripe(triples_ref, a, frames, b),
                kernel_ref[a * 3 + b],
                preferred_element_type=jnp.float32,
            )
            total = term if total is None else total + term
    return total


def fold_all(triples_ref, kernel_ref):
    total = None
    for f, a in ((0, 2), (0, 1), (1, 2)):
        for b in range(3):
            term = jnp.dot(
                stripe(triples_ref, f, 1, b),
                kernel_ref[a * 3 + b],
                preferred_element_type=jnp.float32,
            )
            total = term if total is None else total + term
    return total


def pack_kernel(clip_ref, cot_ref, other_ref, send_ref):
    core, _, _, odd, spot = place()

    def pack(across_ref, first_ref, second_ref):
        send_ref[spot ^ 2] = across_ref[...].reshape(4, 64, 128)
        send_ref[spot ^ 1, 0:2] = first_ref[:, odd]
        send_ref[spot ^ 1, 2:4] = second_ref[:, odd]
        send_ref[spot ^ 3, 0:2] = across_ref[:, odd]

    @pl.when(core == 0)
    def _():
        pack(cot_ref, clip_ref, other_ref)

    @pl.when(core == 1)
    def _():
        pack(clip_ref, other_ref, cot_ref)


def unpack_kernel(clip_ref, cot_ref, other_ref, got_ref, src_ref, far_ref, inner_ref):
    core, chip, slab, odd, spot = place()

    @pl.when(core == 0)
    def _():
        src_ref[0:2] = got_ref[spot ^ 2].reshape(2, 2, 64, 128)
        src_ref[2:4] = clip_ref[...]
        src_ref[4:6] = other_ref[...]
        far_ref[0:2] = got_ref[spot ^ 3, 0:2]
        far_ref[2:6] = got_ref[spot ^ 1]

        @pl.when(chip == 0)
        def _():
            for f in range(2):
                src_ref[f] = clip_ref[0]
                far_ref[f] = got_ref[spot ^ 1, 0]

    @pl.when(core == 1)
    def _():
        src_ref[0:2] = other_ref[...]
        src_ref[2:4] = cot_ref[...]
        src_ref[4:6] = got_ref[spot ^ 2].reshape(2, 2, 64, 128)
        far_ref[0:4] = got_ref[spot ^ 1]
        far_ref[4:6] = got_ref[spot ^ 3, 0:2]

        @pl.when(chip == 7)
        def _():
            src_ref[4:6] = jnp.zeros((2, 2, 64, 128), jnp.bfloat16)
            far_ref[4:6] = jnp.zeros((2, 64, 128), jnp.bfloat16)

    @pl.when((slab == 0) | (slab == 31))
    def _():
        far_ref[...] = jnp.zeros(far_ref.shape, jnp.bfloat16)

    inner_ref[...] = src_ref[:, 1 - odd]


def unpack_grad_kernel(act_ref, got_ref, src_ref, far_ref, inner_ref):
    core, chip, slab, odd, spot = place()
    far_ref[...] = got_ref[spot ^ 1]

    @pl.when(core == 0)
    def _():
        src_ref[...] = act_ref[...]

    @pl.when(core == 1)
    def _():
        src_ref[0:2] = act_ref[2:4]
        src_ref[2:4] = got_ref[spot ^ 2].reshape(2, 2, 64, 128)
        far_ref[2:4] = got_ref[spot ^ 3, 0:2]

        @pl.when(chip == 7)
        def _():
            src_ref[2:4] = jnp.zeros((2, 2, 64, 128), jnp.bfloat16)
            far_ref[2:4] = jnp.zeros((2, 64, 128), jnp.bfloat16)

    @pl.when((slab == 0) | (slab == 31))
    def _():
        far_ref[...] = jnp.zeros(far_ref.shape, jnp.bfloat16)

    inner_ref[...] = src_ref[:, 1 - odd]


def first_conv_kernel(src_ref, far_ref, near_ref, kernel_ref, out_ref, triples_ref):
    fill_triples(src_ref, far_ref, near_ref, triples_ref, 6)
    out_ref[...] = conv_all(triples_ref, kernel_ref, 4)

    @pl.when((lax.axis_index("c") == 1) & (lax.axis_index("zh") == 0) & (lax.axis_index("y") == 0))
    def _():
        out_ref[0:128, :] += fold_all(triples_ref, kernel_ref)


def input_conv_kernel(src_ref, far_ref, near_ref, kernel_ref, cot_ref, out_ref, triples_ref, sum_ref):
    fill_triples(src_ref, far_ref, near_ref, triples_ref, 4)
    sum_ref[...] = conv_all(triples_ref, kernel_ref, 2)

    @pl.when((lax.axis_index("c") == 0) & (lax.axis_index("zh") == 0) & (lax.axis_index("y") == 0))
    def _():
        sum_ref[0:128, :] += fold_all(triples_ref, kernel_ref)

    cot = cot_ref[...].reshape(256, 128).astype(jnp.float32)
    out_ref[...] = (cot + sum_ref[...]).astype(jnp.bfloat16).reshape(out_ref.shape)


def grads_kernel(own_ref, other_ref, triples_ref, send_ref, act_ref, halo_ref, terms_ref):
    core, _, _, odd, spot = place()
    own, other = own_ref[...], other_ref[...]
    pre_act = jnp.where(core == 0, own, other).astype(jnp.bfloat16).astype(jnp.float32)
    back_grad = jnp.where(core == 0, other, own)
    sig = 1.0 / (1.0 + jnp.exp(-pre_act))
    act_grad = (back_grad * (sig * (1.0 + pre_act * (1.0 - sig)))).astype(jnp.bfloat16)
    hidden = (pre_act * sig).astype(jnp.bfloat16)
    act_ref[...] = act_grad.reshape(act_ref.shape)
    halo_ref[spot ^ 2] = act_ref[0:2].reshape(4, 64, 128)
    halo_ref[spot ^ 3, 0:2] = act_ref[0:2, odd]
    halo_ref[spot ^ 1, 0:2] = act_ref[pl.ds(2 * core, 2), odd]
    halo_ref[spot ^ 1, 2:4] = act_ref[2:4, odd]

    @pl.when(core == 0)
    def _():
        for a in range(3):
            for b in range(3):
                start = (a * 3 + b) * 384
                terms_ref[start : start + 384, :] = contract_first(stripe(triples_ref, a, 4, b), act_grad)

    @pl.when(core == 1)
    def _():
        for a in range(3):
            for b in range(3):
                part = contract_first(hidden, stripe(triples_ref, a, 4, b))
                for d in range(3):
                    start = ((2 - a) * 9 + (2 - b) * 3 + (2 - d)) * 128
                    terms_ref[start : start + 128, :] = part[:, d * 128 : (d + 1) * 128]

    @pl.when((core == 1) & (lax.axis_index("zh") == 0) & (lax.axis_index("y") == 0))
    def _():
        for f, a in ((0, 2), (0, 1), (1, 2)):
            for b in range(3):
                part = contract_first(hidden[0:128], stripe(triples_ref, f, 1, b))
                for d in range(3):
                    start = ((2 - a) * 9 + (2 - b) * 3 + (2 - d)) * 128
                    terms_ref[start : start + 128, :] += part[:, d * 128 : (d + 1) * 128]

    for y in range(4):
        for x in range(4):
            blocks = []
            for zh in range(2):
                for c in range(2):
                    start = 54 * (((zh * 4 + y) * 2 + c) * 4 + x)
                    blocks.append(terms_ref[start : start + 54, :])
            blocks.append(jnp.zeros((8, 128), jnp.float32))
            send_ref[y * 4 + x] = jnp.concatenate(blocks, axis=0).astype(jnp.bfloat16)


def plane_sum_kernel(got_ref, send_ref, sum_ref):
    total = got_ref[0].astype(jnp.float32)
    for k in range(1, 16):
        total = total + got_ref[k].astype(jnp.float32)
    sum_ref[...] = total
    lane = lax.broadcasted_iota(jnp.int32, (8, 128), 1)
    for zh in range(2):
        for c in range(2):
            for zl in range(8):
                value = (zh * 2 + c) * 54 * 128 + zl * 864
                row, shift = value // 128, value % 128
                piece = sum_ref[row : row + 8, :]
                if shift:
                    after = sum_ref[row + 1 : row + 9, :]
                    piece = jnp.where(
                        lane < 128 - shift,
                        pltpu.roll(piece, 128 - shift, 1),
                        pltpu.roll(after, 128 - shift, 1),
                    )
                send_ref[zh * 8 + zl, c] = piece


def line_sum_kernel(got_ref, own_ref, send_ref):
    core = lax.axis_index("c")
    total = got_ref[0]
    for k in range(1, 16):
        total = total + got_ref[k]
    own_ref[...] = jnp.where(core == 0, total[0], total[1])
    send_ref[...] = jnp.where(core == 0, total[1], total[0])


def place_kernel(scale, own_ref, other_ref, out_ref):
    core = lax.axis_index("c")
    own, other = own_ref[...] * scale, other_ref[...] * scale
    shares = (jnp.where(core == 0, own, other), jnp.where(core == 0, other, own))
    for k in range(2):
        for r in range(7):
            width = min(128, 864 - 128 * r)
            out_ref[k : k + 1, 128 * r : 128 * r + width] = shares[k][r : r + 1, :width]


def call(kernel, out_shape, *args, scratch=()):
    many = isinstance(out_shape, (list, tuple))
    return pl.pallas_call(
        kernel,
        out_shape=out_shape,
        in_specs=[VMEM] * len(args),
        out_specs=[VMEM] * len(out_shape) if many else VMEM,
        scratch_shapes=scratch,
        compiler_params=PARAMS,
    )(*args)


def shaped(shape, dtype):
    return jax.ShapeDtypeStruct(shape, dtype)


def flipped(kernel):
    return jnp.flip(kernel, (0, 1, 2)).transpose(0, 1, 2, 4, 3)


def far_exchange(blocks):
    return lax.all_to_all(blocks, TM + ROWS, 0, 0, axis_index_groups=FAR_GROUPS, tiled=True)


def per_device(video_clip, first_kernel, second_kernel, cotangent):
    bf16, f32 = jnp.bfloat16, jnp.float32
    core = lax.axis_index("c")
    other_frames = lax.ppermute(jnp.where(core == 0, cotangent, video_clip), "c", SWAP)
    blocks = call(pack_kernel, shaped((4, 4, 64, 128), bf16), video_clip, cotangent, other_frames)
    got = far_exchange(blocks)
    kernel = jnp.where(core == 0, first_kernel, flipped(second_kernel)).reshape(9, 384, 128)
    first_back = flipped(first_kernel).reshape(9, 384, 128)
    kernel, first_back = lax.optimization_barrier((kernel, first_back))
    source, far, inner = call(
        unpack_kernel,
        (shaped((6, 2, 64, 128), bf16), shaped((6, 64, 128), bf16), shaped((6, 64, 128), bf16)),
        video_clip, cotangent, other_frames, got,
    )
    near = lax.ppermute(inner, ROWS, NEAR_ROWS)
    own, triples = call(
        first_conv_kernel,
        (shaped((512, 128), f32), shaped((6, 4, 64, 384), bf16)),
        source, far, near, kernel,
    )
    other = lax.ppermute(own, "c", SWAP)
    send, act_grad, blocks = call(
        grads_kernel,
        (shaped((16, 224, 128), bf16), shaped((4, 2, 64, 128), bf16), shaped((4, 4, 64, 128), bf16)),
        own, other, triples,
        scratch=[pltpu.VMEM((3456, 128), f32)],
    )
    got = lax.all_to_all(send, ("y", "x"), 0, 0, tiled=True)
    got_grad = far_exchange(blocks)
    send = call(plane_sum_kernel, shaped((16, 2, 8, 128), f32), got, scratch=[pltpu.VMEM((224, 128), f32)])
    got = lax.all_to_all(send, ("zh", "zl"), 0, 0, tiled=True)
    source, far, inner = call(
        unpack_grad_kernel,
        (shaped((4, 2, 64, 128), bf16), shaped((4, 64, 128), bf16), shaped((4, 64, 128), bf16)),
        act_grad, got_grad,
    )
    near = lax.ppermute(inner, ROWS, NEAR_ROWS)
    input_grad = call(
        input_conv_kernel,
        shaped((2, 2, 64, 128), bf16),
        source, far, near, first_back, cotangent,
        scratch=[pltpu.VMEM((4, 4, 64, 384), bf16), pltpu.VMEM((256, 128), f32)],
    )
    got, input_grad = lax.optimization_barrier((got, input_grad))
    own_share, send_share = call(line_sum_kernel, (shaped((8, 128), f32),) * 2, got)
    other_share = lax.ppermute(send_share, "c", SWAP)
    scale = 1.0 / math.sqrt(131072)
    weight_grads = call(
        lambda *refs: place_kernel(scale, *refs), shaped((2, 864), f32), own_share, other_share
    )
    return input_grad, weight_grads


def solution(mesh):
    fine = Mesh(np.asarray(mesh.devices).reshape(2, 4, 2, 4, 8), TM + ROWS)
    return jax.shard_map(
        per_device,
        mesh=fine,
        in_specs=(P(TM, ROWS, None, None), P(), P(), P(TM, ROWS, None, None)),
        out_specs=(P(TM, ROWS, None, None), P(None, TM + ROWS)),
        check_vma=False,
    )
```

```python
import math

import jax
import jax.numpy as jnp
import numpy as np
from jax import lax
from jax.experimental import pallas as pl
from jax.experimental.pallas import tpu as pltpu
from jax.sharding import Mesh, PartitionSpec as P

TM = ("zh", "y", "c")
ROWS = ("x", "zl")
VMEM = pl.BlockSpec(memory_space=pltpu.VMEM)
PARAMS = pltpu.CompilerParams(vmem_limit_bytes=48 * 1024 * 1024)


SWAP = [(0, 1), (1, 0)]
NEAR_ROWS = [(r, r ^ 1) for r in range(32)]
FAR_ROWS = [(r, r + 1) for r in range(1, 31, 2)] + [(r + 1, r) for r in range(1, 31, 2)]
BEYOND = [(2 * k + 1, 2 * k + 2) for k in range(7)] + [(2 * k + 2, 2 * k + 1) for k in range(7)]
BEFORE = [((2 * k + 2) * 32 + r, (2 * k + 1) * 32 + r) for k in range(7) for r in range(32)] + [
    ((2 * k + 3) * 32 + r, 2 * k * 32 + q) for k in range(7) for r, q in FAR_ROWS
]


def place():
    core = lax.axis_index("c")
    chip = lax.axis_index("zh") * 4 + lax.axis_index("y")
    slab = lax.axis_index("x") * 8 + lax.axis_index("zl")
    odd = slab & 1
    return core, chip, slab, odd


def contract_first(lhs, rhs):
    return lax.dot_general(lhs, rhs, (((0,), (0,)), ((), ())), preferred_element_type=jnp.float32)


def fill_triples(src_ref, far_ref, near_ref, triples_ref, frames):
    odd = place()[3]
    columns = src_ref.shape[2]
    chans = src_ref.shape[3]
    col = lax.broadcasted_iota(jnp.int32, (columns, chans), 0)
    for f in range(frames):
        for r in range(4):
            if r in (0, 3):
                cells = jnp.where(odd == (r == 3), far_ref[f], near_ref[f])
            else:
                cells = src_ref[f, r - 1]
            wide = cells.astype(jnp.float32)
            before = jnp.where(col == 0, 0.0, pltpu.roll(wide, 1, 0))
            after = jnp.where(col == columns - 1, 0.0, pltpu.roll(wide, columns - 1, 0))
            triples_ref[f, r, :, 0:chans] = before.astype(cells.dtype)
            triples_ref[f, r, :, chans : 2 * chans] = cells
            triples_ref[f, r, :, 2 * chans : 3 * chans] = after.astype(cells.dtype)


def stripe(triples_ref, f, count, b):
    part = triples_ref[f : f + count, b : b + 2]
    return part.reshape(count * 2 * part.shape[2], part.shape[3])


def conv_all(triples_ref, kernel_ref, frames):
    total = None
    for a in range(3):
        for b in range(3):
            term = jnp.dot(
                stripe(triples_ref, a, frames, b),
                kernel_ref[a * 3 + b],
                preferred_element_type=jnp.float32,
            )
            total = term if total is None else total + term
    return total


def fold_all(triples_ref, kernel_ref):
    total = None
    for f, a in ((0, 2), (0, 1), (1, 2)):
        for b in range(3):
            term = jnp.dot(
                stripe(triples_ref, f, 1, b),
                kernel_ref[a * 3 + b],
                preferred_element_type=jnp.float32,
            )
            total = term if total is None else total + term
    return total


def assemble_kernel(clip_ref, cot_ref, other_ref, beyond_ref, src_ref, edge_ref, inner_ref):
    core, chip, _, odd = place()

    @pl.when(core == 0)
    def _():
        src_ref[0:2] = beyond_ref[...]
        src_ref[2:4] = clip_ref[...]
        src_ref[4:6] = other_ref[...]

        @pl.when(chip == 0)
        def _():
            src_ref[0] = clip_ref[0]
            src_ref[1] = clip_ref[0]

    @pl.when(core == 1)
    def _():
        src_ref[0:2] = other_ref[...]
        src_ref[2:4] = cot_ref[...]
        src_ref[4:6] = beyond_ref[...]

    edge_ref[...] = src_ref[:, odd]
    inner_ref[...] = src_ref[:, 1 - odd]


def assemble_grad_kernel(act_ref, before_ref, src_ref, inner_ref, corner_ref):
    core, _, _, odd = place()
    corner_ref[...] = before_ref[:, 0]

    @pl.when(core == 0)
    def _():
        src_ref[...] = act_ref[...]

    @pl.when(core == 1)
    def _():
        src_ref[0:2] = act_ref[2:4]
        src_ref[2:4] = before_ref[...]

    inner_ref[...] = src_ref[:, 1 - odd]


def first_conv_kernel(src_ref, far_ref, near_ref, kernel_ref, out_ref, triples_ref):
    fill_triples(src_ref, far_ref, near_ref, triples_ref, 6)
    out_ref[...] = conv_all(triples_ref, kernel_ref, 4)

    @pl.when((lax.axis_index("c") == 1) & (lax.axis_index("zh") == 0) & (lax.axis_index("y") == 0))
    def _():
        out_ref[0:128, :] += fold_all(triples_ref, kernel_ref)


def input_conv_kernel(
    src_ref, edge_ref, corner_ref, near_ref, kernel_ref, cot_ref, out_ref, far_ref, triples_ref, sum_ref
):
    far_ref[...] = edge_ref[...]

    @pl.when(lax.axis_index("c") == 1)
    def _():
        far_ref[2:4] = corner_ref[...]

    fill_triples(src_ref, far_ref, near_ref, triples_ref, 4)
    sum_ref[...] = conv_all(triples_ref, kernel_ref, 2)

    @pl.when((lax.axis_index("c") == 0) & (lax.axis_index("zh") == 0) & (lax.axis_index("y") == 0))
    def _():
        sum_ref[0:128, :] += fold_all(triples_ref, kernel_ref)

    cot = cot_ref[...].reshape(256, 128).astype(jnp.float32)
    out_ref[...] = (cot + sum_ref[...]).astype(jnp.bfloat16).reshape(out_ref.shape)


def grads_kernel(own_ref, other_ref, triples_ref, send_ref, act_ref, edge_ref, before_ref, terms_ref):
    core, _, _, odd = place()
    own, other = own_ref[...], other_ref[...]
    pre_act = jnp.where(core == 0, own, other).astype(jnp.bfloat16).astype(jnp.float32)
    back_grad = jnp.where(core == 0, other, own)
    sig = 1.0 / (1.0 + jnp.exp(-pre_act))
    act_grad = (back_grad * (sig * (1.0 + pre_act * (1.0 - sig)))).astype(jnp.bfloat16)
    hidden = (pre_act * sig).astype(jnp.bfloat16)
    act_ref[...] = act_grad.reshape(act_ref.shape)
    edge_ref[0:2] = act_ref[pl.ds(2 * core, 2), odd]
    edge_ref[2:4] = act_ref[2:4, odd]

    @pl.when(core == 0)
    def _():
        before_ref[...] = act_ref[0:2]

    @pl.when(core == 1)
    def _():
        before_ref[:, 0] = act_ref[0:2, odd]
        before_ref[:, 1] = act_ref[0:2, odd]

    @pl.when(core == 0)
    def _():
        for a in range(3):
            for b in range(3):
                start = (a * 3 + b) * 384
                terms_ref[start : start + 384, :] = contract_first(stripe(triples_ref, a, 4, b), act_grad)

    @pl.when(core == 1)
    def _():
        for a in range(3):
            for b in range(3):
                part = contract_first(hidden, stripe(triples_ref, a, 4, b))
                for d in range(3):
                    start = ((2 - a) * 9 + (2 - b) * 3 + (2 - d)) * 128
                    terms_ref[start : start + 128, :] = part[:, d * 128 : (d + 1) * 128]

    @pl.when((core == 1) & (lax.axis_index("zh") == 0) & (lax.axis_index("y") == 0))
    def _():
        for f, a in ((0, 2), (0, 1), (1, 2)):
            for b in range(3):
                part = contract_first(hidden[0:128], stripe(triples_ref, f, 1, b))
                for d in range(3):
                    start = ((2 - a) * 9 + (2 - b) * 3 + (2 - d)) * 128
                    terms_ref[start : start + 128, :] += part[:, d * 128 : (d + 1) * 128]

    for y in range(4):
        for x in range(4):
            blocks = []
            for zh in range(2):
                for c in range(2):
                    start = 54 * (((zh * 4 + y) * 2 + c) * 4 + x)
                    blocks.append(terms_ref[start : start + 54, :])
            blocks.append(jnp.zeros((8, 128), jnp.float32))
            send_ref[y * 4 + x] = jnp.concatenate(blocks, axis=0).astype(jnp.bfloat16)


def plane_sum_kernel(got_ref, send_ref, sum_ref):
    total = got_ref[0].astype(jnp.float32)
    for k in range(1, 16):
        total = total + got_ref[k].astype(jnp.float32)
    sum_ref[...] = total
    lane = lax.broadcasted_iota(jnp.int32, (8, 128), 1)
    for zh in range(2):
        for c in range(2):
            for zl in range(8):
                value = (zh * 2 + c) * 54 * 128 + zl * 864
                row, shift = value // 128, value % 128
                piece = sum_ref[row : row + 8, :]
                if shift:
                    after = sum_ref[row + 1 : row + 9, :]
                    piece = jnp.where(
                        lane < 128 - shift,
                        pltpu.roll(piece, 128 - shift, 1),
                        pltpu.roll(after, 128 - shift, 1),
                    )
                send_ref[zh * 16 + c * 8 + zl] = piece


def line_sum_kernel(scale, got_ref, out_ref):
    for k in range(2):
        total = None
        for zh in range(2):
            for zl in range(8):
                term = got_ref[zh * 16 + k * 8 + zl]
                total = term if total is None else total + term
        total = total * scale
        for r in range(7):
            width = min(128, 864 - 128 * r)
            out_ref[k : k + 1, 128 * r : 128 * r + width] = total[r : r + 1, :width]


def call(kernel, out_shape, *args, scratch=()):
    many = isinstance(out_shape, (list, tuple))
    return pl.pallas_call(
        kernel,
        out_shape=out_shape,
        in_specs=[VMEM] * len(args),
        out_specs=[VMEM] * len(out_shape) if many else VMEM,
        scratch_shapes=scratch,
        compiler_params=PARAMS,
    )(*args)


def shaped(shape, dtype):
    return jax.ShapeDtypeStruct(shape, dtype)


def flipped(kernel):
    return jnp.flip(kernel, (0, 1, 2)).transpose(0, 1, 2, 4, 3)


def per_device(video_clip, first_kernel, second_kernel, cotangent):
    bf16, f32 = jnp.bfloat16, jnp.float32
    core = lax.axis_index("c")
    given = jnp.where(core == 0, cotangent, video_clip)
    beyond = lax.ppermute(given, TM, BEYOND)
    other_frames = lax.ppermute(given, "c", SWAP)
    kernel = jnp.where(core == 0, first_kernel, flipped(second_kernel)).reshape(9, 384, 128)
    first_back = flipped(first_kernel).reshape(9, 384, 128)
    kernel, first_back = lax.optimization_barrier((kernel, first_back))
    source, edge, inner = call(
        assemble_kernel,
        (shaped((6, 2, 64, 128), bf16), shaped((6, 64, 128), bf16), shaped((6, 64, 128), bf16)),
        video_clip, cotangent, other_frames, beyond,
    )
    far = lax.ppermute(edge, ROWS, FAR_ROWS)
    near = lax.ppermute(inner, ROWS, NEAR_ROWS)
    own, triples = call(
        first_conv_kernel,
        (shaped((512, 128), f32), shaped((6, 4, 64, 384), bf16)),
        source, far, near, kernel,
    )
    other = lax.ppermute(own, "c", SWAP)
    send, act_grad, edge, before = call(
        grads_kernel,
        (
            shaped((16, 224, 128), bf16), shaped((4, 2, 64, 128), bf16),
            shaped((4, 64, 128), bf16), shaped((2, 2, 64, 128), bf16),
        ),
        own, other, triples,
        scratch=[pltpu.VMEM((3456, 128), f32)],
    )
    got = lax.all_to_all(send, ("y", "x"), 0, 0, tiled=True)
    before = lax.ppermute(before, TM + ROWS, BEFORE)
    far = lax.ppermute(edge, ROWS, FAR_ROWS)
    send = call(plane_sum_kernel, shaped((32, 8, 128), f32), got, scratch=[pltpu.VMEM((224, 128), f32)])
    got = lax.all_to_all(send, ("zh", "c", "zl"), 0, 0, tiled=True)
    source, inner, corner = call(
        assemble_grad_kernel,
        (shaped((4, 2, 64, 128), bf16), shaped((4, 64, 128), bf16), shaped((2, 64, 128), bf16)),
        act_grad, before,
    )
    near = lax.ppermute(inner, ROWS, NEAR_ROWS)
    corner = lax.ppermute(corner, "c", [(0, 1)])
    input_grad = call(
        input_conv_kernel,
        shaped((2, 2, 64, 128), bf16),
        source, far, corner, near, first_back, cotangent,
        scratch=[
            pltpu.VMEM((4, 64, 128), bf16), pltpu.VMEM((4, 4, 64, 384), bf16), pltpu.VMEM((256, 128), f32)
        ],
    )
    got, input_grad = lax.optimization_barrier((got, input_grad))
    scale = 1.0 / math.sqrt(131072)
    weight_grads = call(lambda *refs: line_sum_kernel(scale, *refs), shaped((2, 864), f32), got)
    return input_grad, weight_grads


def solution(mesh):
    fine = Mesh(np.asarray(mesh.devices).reshape(2, 4, 2, 4, 8), TM + ROWS)
    return jax.shard_map(
        per_device,
        mesh=fine,
        in_specs=(P(TM, ROWS, None, None), P(), P(), P(TM, ROWS, None, None)),
        out_specs=(P(TM, ROWS, None, None), P(None, TM + ROWS)),
        check_vma=False,
    )
```

```python
import math

import jax
import jax.numpy as jnp
import numpy as np
from jax import lax
from jax.experimental import pallas as pl
from jax.experimental.pallas import tpu as pltpu
from jax.sharding import Mesh, PartitionSpec as P

TM = ("zh", "y", "c")
ROWS = ("x", "zl")
VMEM = pl.BlockSpec(memory_space=pltpu.VMEM)
PARAMS = pltpu.CompilerParams(vmem_limit_bytes=48 * 1024 * 1024)


SWAP = [(0, 1), (1, 0)]
NEAR_ROWS = [(r, r ^ 1) for r in range(32)]
FAR_ROWS = [(r, r + 1) for r in range(1, 31, 2)] + [(r + 1, r) for r in range(1, 31, 2)]
BEYOND = [(2 * k + 1, 2 * k + 2) for k in range(7)] + [(2 * k + 2, 2 * k + 1) for k in range(7)]
BEFORE = [((2 * k + 2) * 32 + r, (2 * k + 1) * 32 + r) for k in range(7) for r in range(32)] + [
    ((2 * k + 3) * 32 + r, 2 * k * 32 + q) for k in range(7) for r, q in FAR_ROWS
]


def place():
    core = lax.axis_index("c")
    chip = lax.axis_index("zh") * 4 + lax.axis_index("y")
    slab = lax.axis_index("x") * 8 + lax.axis_index("zl")
    odd = slab & 1
    return core, chip, slab, odd


def contract_first(lhs, rhs):
    return lax.dot_general(lhs, rhs, (((0,), (0,)), ((), ())), preferred_element_type=jnp.float32)


def fill_triples(src_ref, far_ref, near_ref, triples_ref, frames):
    odd = place()[3]
    columns = src_ref.shape[2]
    chans = src_ref.shape[3]
    col = lax.broadcasted_iota(jnp.int32, (columns, chans), 0)
    for f in range(frames):
        for r in range(4):
            if r in (0, 3):
                cells = jnp.where(odd == (r == 3), far_ref[f], near_ref[f])
            else:
                cells = src_ref[f, r - 1]
            wide = cells.astype(jnp.float32)
            before = jnp.where(col == 0, 0.0, pltpu.roll(wide, 1, 0))
            after = jnp.where(col == columns - 1, 0.0, pltpu.roll(wide, columns - 1, 0))
            triples_ref[f, r, :, 0:chans] = before.astype(cells.dtype)
            triples_ref[f, r, :, chans : 2 * chans] = cells
            triples_ref[f, r, :, 2 * chans : 3 * chans] = after.astype(cells.dtype)


def stripe(triples_ref, f, count, b):
    part = triples_ref[f : f + count, b : b + 2]
    return part.reshape(count * 2 * part.shape[2], part.shape[3])


def conv_all(triples_ref, kernel_ref, frames):
    total = None
    for a in range(3):
        for b in range(3):
            term = jnp.dot(
                stripe(triples_ref, a, frames, b),
                kernel_ref[a * 3 + b],
                preferred_element_type=jnp.float32,
            )
            total = term if total is None else total + term
    return total


def fold_all(triples_ref, kernel_ref):
    total = None
    for f, a in ((0, 2), (0, 1), (1, 2)):
        for b in range(3):
            term = jnp.dot(
                stripe(triples_ref, f, 1, b),
                kernel_ref[a * 3 + b],
                preferred_element_type=jnp.float32,
            )
            total = term if total is None else total + term
    return total


def assemble_kernel(clip_ref, cot_ref, other_ref, beyond_ref, src_ref, edge_ref, inner_ref):
    core, chip, _, odd = place()

    @pl.when(core == 0)
    def _():
        src_ref[0:2] = beyond_ref[...]
        src_ref[2:4] = clip_ref[...]
        src_ref[4:6] = other_ref[...]

        @pl.when(chip == 0)
        def _():
            src_ref[0] = clip_ref[0]
            src_ref[1] = clip_ref[0]

    @pl.when(core == 1)
    def _():
        src_ref[0:2] = other_ref[...]
        src_ref[2:4] = cot_ref[...]
        src_ref[4:6] = beyond_ref[...]

    edge_ref[...] = src_ref[:, odd]
    inner_ref[...] = src_ref[:, 1 - odd]


def assemble_grad_kernel(act_ref, before_ref, src_ref, inner_ref, corner_ref):
    core, _, _, odd = place()
    corner_ref[...] = before_ref[:, 0]

    @pl.when(core == 0)
    def _():
        src_ref[...] = act_ref[...]

    @pl.when(core == 1)
    def _():
        src_ref[0:2] = act_ref[2:4]
        src_ref[2:4] = before_ref[...]

    inner_ref[...] = src_ref[:, 1 - odd]


def first_conv_kernel(src_ref, far_ref, near_ref, kernel_ref, out_ref, triples_ref):
    fill_triples(src_ref, far_ref, near_ref, triples_ref, 6)
    out_ref[...] = conv_all(triples_ref, kernel_ref, 4)

    @pl.when((lax.axis_index("c") == 1) & (lax.axis_index("zh") == 0) & (lax.axis_index("y") == 0))
    def _():
        out_ref[0:128, :] += fold_all(triples_ref, kernel_ref)


def input_conv_kernel(
    src_ref, edge_ref, corner_ref, near_ref, kernel_ref, cot_ref, out_ref, far_ref, triples_ref, sum_ref
):
    far_ref[...] = edge_ref[...]

    @pl.when(lax.axis_index("c") == 1)
    def _():
        far_ref[2:4] = corner_ref[...]

    fill_triples(src_ref, far_ref, near_ref, triples_ref, 4)
    sum_ref[...] = conv_all(triples_ref, kernel_ref, 2)

    @pl.when((lax.axis_index("c") == 0) & (lax.axis_index("zh") == 0) & (lax.axis_index("y") == 0))
    def _():
        sum_ref[0:128, :] += fold_all(triples_ref, kernel_ref)

    cot = cot_ref[...].reshape(256, 128).astype(jnp.float32)
    out_ref[...] = (cot + sum_ref[...]).astype(jnp.bfloat16).reshape(out_ref.shape)


def grads_kernel(own_ref, other_ref, triples_ref, send_ref, act_ref, edge_ref, before_ref, terms_ref):
    core, _, _, odd = place()
    own, other = own_ref[...], other_ref[...]
    pre_act = jnp.where(core == 0, own, other).astype(jnp.bfloat16).astype(jnp.float32)
    back_grad = jnp.where(core == 0, other, own)
    sig = 1.0 / (1.0 + jnp.exp(-pre_act))
    act_grad = (back_grad * (sig * (1.0 + pre_act * (1.0 - sig)))).astype(jnp.bfloat16)
    hidden = (pre_act * sig).astype(jnp.bfloat16)
    act_ref[...] = act_grad.reshape(act_ref.shape)
    edge_ref[0:2] = act_ref[pl.ds(2 * core, 2), odd]
    edge_ref[2:4] = act_ref[2:4, odd]

    @pl.when(core == 0)
    def _():
        before_ref[...] = act_ref[0:2]

    @pl.when(core == 1)
    def _():
        before_ref[:, 0] = act_ref[0:2, odd]
        before_ref[:, 1] = act_ref[0:2, odd]

    @pl.when(core == 0)
    def _():
        for a in range(3):
            for b in range(3):
                start = (a * 3 + b) * 384
                terms_ref[start : start + 384, :] = contract_first(stripe(triples_ref, a, 4, b), act_grad)

    @pl.when(core == 1)
    def _():
        for a in range(3):
            for b in range(3):
                part = contract_first(hidden, stripe(triples_ref, a, 4, b))
                for d in range(3):
                    start = ((2 - a) * 9 + (2 - b) * 3 + (2 - d)) * 128
                    terms_ref[start : start + 128, :] = part[:, d * 128 : (d + 1) * 128]

    @pl.when((core == 1) & (lax.axis_index("zh") == 0) & (lax.axis_index("y") == 0))
    def _():
        for f, a in ((0, 2), (0, 1), (1, 2)):
            for b in range(3):
                part = contract_first(hidden[0:128], stripe(triples_ref, f, 1, b))
                for d in range(3):
                    start = ((2 - a) * 9 + (2 - b) * 3 + (2 - d)) * 128
                    terms_ref[start : start + 128, :] += part[:, d * 128 : (d + 1) * 128]

    for y in range(4):
        for x in range(4):
            blocks = []
            for zh in range(2):
                for c in range(2):
                    start = 54 * (((zh * 4 + y) * 2 + c) * 4 + x)
                    blocks.append(terms_ref[start : start + 54, :])
            blocks.append(jnp.zeros((8, 128), jnp.float32))
            send_ref[y * 4 + x] = jnp.concatenate(blocks, axis=0).astype(jnp.bfloat16)


def plane_sum_kernel(got_ref, send_ref, sum_ref):
    total = got_ref[0].astype(jnp.float32)
    for k in range(1, 16):
        total = total + got_ref[k].astype(jnp.float32)
    sum_ref[...] = total
    lane = lax.broadcasted_iota(jnp.int32, (8, 128), 1)
    for zh in range(2):
        for zl in range(8):
            pieces = []
            for c in range(2):
                value = (zh * 2 + c) * 54 * 128 + zl * 864
                row, shift = value // 128, value % 128
                piece = sum_ref[row : row + 8, :]
                if shift:
                    after = sum_ref[row + 1 : row + 9, :]
                    piece = jnp.where(
                        lane < 128 - shift,
                        pltpu.roll(piece, 128 - shift, 1),
                        pltpu.roll(after, 128 - shift, 1),
                    )
                pieces.append(piece)
            send_ref[zh * 8 + zl] = jnp.concatenate(pieces, axis=0).astype(jnp.bfloat16)


def line_sum_kernel(got_ref, own_ref, send_ref):
    core = lax.axis_index("c")
    total = got_ref[0].astype(jnp.float32)
    for k in range(1, 16):
        total = total + got_ref[k].astype(jnp.float32)
    own_ref[...] = jnp.where(core == 0, total[0:8], total[8:16])
    send_ref[...] = jnp.where(core == 0, total[8:16], total[0:8])


def place_kernel(scale, own_ref, other_ref, out_ref):
    core = lax.axis_index("c")
    own, other = own_ref[...] * scale, other_ref[...] * scale
    shares = (jnp.where(core == 0, own, other), jnp.where(core == 0, other, own))
    for k in range(2):
        for r in range(7):
            width = min(128, 864 - 128 * r)
            out_ref[k : k + 1, 128 * r : 128 * r + width] = shares[k][r : r + 1, :width]


def call(kernel, out_shape, *args, scratch=(), flops=0):
    many = isinstance(out_shape, (list, tuple))
    return pl.pallas_call(
        kernel,
        out_shape=out_shape,
        in_specs=[VMEM] * len(args),
        out_specs=[VMEM] * len(out_shape) if many else VMEM,
        scratch_shapes=scratch,
        compiler_params=PARAMS,
        cost_estimate=pl.CostEstimate(flops=flops, bytes_accessed=0, transcendentals=0) if flops else None,
    )(*args)


def shaped(shape, dtype):
    return jax.ShapeDtypeStruct(shape, dtype)


def flipped(kernel):
    return jnp.flip(kernel, (0, 1, 2)).transpose(0, 1, 2, 4, 3)


def per_device(video_clip, first_kernel, second_kernel, cotangent):
    bf16, f32 = jnp.bfloat16, jnp.float32
    core = lax.axis_index("c")
    given = jnp.where(core == 0, cotangent, video_clip)
    beyond = lax.ppermute(given, TM, BEYOND)
    other_frames = lax.ppermute(given, "c", SWAP)
    kernel = jnp.where(core == 0, first_kernel, flipped(second_kernel)).reshape(9, 384, 128)
    first_back = flipped(first_kernel).reshape(9, 384, 128)
    kernel, first_back = lax.optimization_barrier((kernel, first_back))
    source, edge, inner = call(
        assemble_kernel,
        (shaped((6, 2, 64, 128), bf16), shaped((6, 64, 128), bf16), shaped((6, 64, 128), bf16)),
        video_clip, cotangent, other_frames, beyond,
    )
    far = lax.ppermute(edge, ROWS, FAR_ROWS)
    near = lax.ppermute(inner, ROWS, NEAR_ROWS)
    own, triples = call(
        first_conv_kernel,
        (shaped((512, 128), f32), shaped((6, 4, 64, 384), bf16)),
        source, far, near, kernel,
    )
    other = lax.ppermute(own, "c", SWAP)
    send, act_grad, edge, before = call(
        grads_kernel,
        (
            shaped((16, 224, 128), bf16), shaped((4, 2, 64, 128), bf16),
            shaped((4, 64, 128), bf16), shaped((2, 2, 64, 128), bf16),
        ),
        own, other, triples,
        scratch=[pltpu.VMEM((3456, 128), f32)],
    )
    got = lax.all_to_all(send, ("y", "x"), 0, 0, tiled=True)
    before = lax.ppermute(before, TM + ROWS, BEFORE)
    far = lax.ppermute(edge, ROWS, FAR_ROWS)
    got, before = lax.optimization_barrier((got, before))
    send = call(plane_sum_kernel, shaped((16, 16, 128), bf16), got, scratch=[pltpu.VMEM((224, 128), f32)])
    got = lax.all_to_all(send, ("zh", "zl"), 0, 0, tiled=True)
    _, before, far = lax.optimization_barrier((send, before, far))
    source, inner, corner = call(
        assemble_grad_kernel,
        (shaped((4, 2, 64, 128), bf16), shaped((4, 64, 128), bf16), shaped((2, 64, 128), bf16)),
        act_grad, before,
    )
    near = lax.ppermute(inner, ROWS, NEAR_ROWS)
    corner = lax.ppermute(corner, "c", [(0, 1)])
    input_grad = call(
        input_conv_kernel,
        shaped((2, 2, 64, 128), bf16),
        source, far, corner, near, first_back, cotangent,
        scratch=[
            pltpu.VMEM((4, 64, 128), bf16), pltpu.VMEM((4, 4, 64, 384), bf16), pltpu.VMEM((256, 128), f32)
        ],
        flops=1_600_000_000,
    )
    got, input_grad = lax.optimization_barrier((got, input_grad))
    scale = 1.0 / math.sqrt(131072)
    own_share, send_share = call(line_sum_kernel, (shaped((8, 128), f32),) * 2, got)
    other_share = lax.ppermute(send_share, "c", SWAP)
    weight_grads = call(
        lambda *refs: place_kernel(scale, *refs), shaped((2, 864), f32), own_share, other_share
    )
    return input_grad, weight_grads


def solution(mesh):
    fine = Mesh(np.asarray(mesh.devices).reshape(2, 4, 2, 4, 8), TM + ROWS)
    return jax.shard_map(
        per_device,
        mesh=fine,
        in_specs=(P(TM, ROWS, None, None), P(), P(), P(TM, ROWS, None, None)),
        out_specs=(P(TM, ROWS, None, None), P(None, TM + ROWS)),
        check_vma=False,
    )
```

```python
import math

import jax
import jax.numpy as jnp
import numpy as np
from jax import lax
from jax.experimental import pallas as pl
from jax.experimental.pallas import tpu as pltpu
from jax.sharding import Mesh, PartitionSpec as P

TM = ("zh", "y", "c")
ROWS = ("x", "zl")
VMEM = pl.BlockSpec(memory_space=pltpu.VMEM)


SWAP = [(0, 1), (1, 0)]
NEAR_ROWS = [(r, r ^ 1) for r in range(32)]
FAR_ROWS = [(r, r + 1) for r in range(1, 31, 2)] + [(r + 1, r) for r in range(1, 31, 2)]
ENDS = [(r, q) for r, q in FAR_ROWS if r // 8 != q // 8]
MIDDLES = [(r, q) for r, q in FAR_ROWS if r // 8 == q // 8]
ENDS_OF = [r for r, _ in ENDS]


PLANES = [list(range(15, -1, -1)), list(range(16, 32))]


def device(chip, core, slab):
    return (2 * chip + core) * 32 + slab


BEYOND = [pair for k in (0, 1, 2, 4, 5, 6) for pair in ((2 * k + 1, 2 * k + 2), (2 * k + 2, 2 * k + 1))]
BEYOND_FAR = [(7, 8), (8, 7)]
CORNER_FREE = [(device(3, 0, r), device(4, 1, q)) for r, q in ENDS] + [
    (device(4, 1, r), device(3, 0, q)) for r, q in ENDS
]
CORNER_ROWS = [(device(k, c, r), device(k, c, q)) for k, c in ((3, 1), (4, 0)) for r, q in MIDDLES] + [
    (device(k, c, r), device(k, 1 - c, r)) for k, c in ((3, 0), (4, 1)) for r in ENDS_OF
]
BEFORE = [(device(k + 1, 0, r), device(k, 1, r)) for k in range(7) for r in range(32)] + [
    (device(4, 1, r), device(3, 0, q)) for r, q in ENDS
]
CORNER_GRAD = (
    [(device(k, 1, r), device(k, 1, q)) for k in range(7) for r, q in MIDDLES]
    + [(device(k + 1, 1, r), device(k, 1, r)) for k in (0, 1, 2, 4, 5, 6) for r in ENDS_OF]
    + [(device(3, 0, r), device(3, 1, r)) for r in ENDS_OF]
)


def place():
    core = lax.axis_index("c")
    chip = lax.axis_index("zh") * 4 + lax.axis_index("y")
    odd = lax.axis_index("zl") & 1
    end = (lax.axis_index("zl") == 0) | (lax.axis_index("zl") == 7)
    return core, chip, end, odd


def contract_first(lhs, rhs):
    return lax.dot_general(lhs, rhs, (((0,), (0,)), ((), ())), preferred_element_type=jnp.float32)


def fill_triples(src_ref, far_ref, near_ref, triples_ref, frames):
    odd = place()[3]
    columns = src_ref.shape[2]
    chans = src_ref.shape[3]
    col = lax.broadcasted_iota(jnp.int32, (columns, chans), 0)
    for f in range(frames):
        for r in range(4):
            if r in (0, 3):
                cells = jnp.where(odd == (r == 3), far_ref[f], near_ref[f])
            else:
                cells = src_ref[f, r - 1]
            wide = cells.astype(jnp.float32)
            before = jnp.where(col == 0, 0.0, pltpu.roll(wide, 1, 0))
            after = jnp.where(col == columns - 1, 0.0, pltpu.roll(wide, columns - 1, 0))
            triples_ref[f, r, :, 0:chans] = before.astype(cells.dtype)
            triples_ref[f, r, :, chans : 2 * chans] = cells
            triples_ref[f, r, :, 2 * chans : 3 * chans] = after.astype(cells.dtype)


def stripe(triples_ref, f, count, b):
    part = triples_ref[f : f + count, b : b + 2]
    return part.reshape(count * 2 * part.shape[2], part.shape[3])


def conv(triples_ref, kernel_ref, frames):
    total = None
    for a in range(3):
        for b in range(3):
            start = (a * 3 + b) * 384
            term = jnp.dot(
                stripe(triples_ref, a, frames, b),
                kernel_ref[start : start + 384, :],
                preferred_element_type=jnp.float32,
            )
            total = term if total is None else total + term
    return total


def back_terms(triples_ref, kernel_ref, frames, taps):
    total = None
    for f, a in taps:
        for b in range(3):
            part = stripe(triples_ref, f, frames, b)
            starts = [((2 - a) * 9 + (2 - b) * 3 + (2 - d)) * 128 for d in range(3)]
            turned = jnp.concatenate([kernel_ref[start : start + 128, :] for start in starts], axis=1)
            term = lax.dot_general(part, turned, (((1,), (1,)), ((), ())), preferred_element_type=jnp.float32)
            total = term if total is None else total + term
    return total


TAPS = ((0, 0), (1, 1), (2, 2))
FOLD = ((0, 2), (0, 1), (1, 2))


def edge_kernel(mine_ref, both_ref, beyond_ref, edge_ref, corner_ref):
    core, chip, _, odd = place()
    other_ref = both_ref.at[pl.ds(2 - 2 * core, 2)]
    corner_ref[...] = other_ref[:, odd]
    edge_ref[pl.ds(4 * core, 2)] = beyond_ref[:, odd]
    edge_ref[2:4] = mine_ref[:, odd]
    edge_ref[pl.ds(4 - 4 * core, 2)] = other_ref[:, odd]

    @pl.when((core == 0) & (chip == 0))
    def _():
        edge_ref[0] = mine_ref[0, odd]
        edge_ref[1] = mine_ref[0, odd]


def assemble_kernel(mine_ref, both_ref, beyond_ref, beyond_far_ref, free_ref, src_ref, inner_ref, corner_ref):
    core, chip, end, odd = place()
    src_ref[pl.ds(4 * core, 2)] = beyond_ref[...] + beyond_far_ref[...]
    src_ref[2:4] = mine_ref[...]
    src_ref[pl.ds(4 - 4 * core, 2)] = both_ref[pl.ds(2 - 2 * core, 2)]

    @pl.when((core == 0) & (chip == 0))
    def _():
        src_ref[0] = mine_ref[0]
        src_ref[1] = mine_ref[0]

    inner_ref[...] = src_ref[:, 1 - odd]
    corner_ref[...] = jnp.where(end, free_ref[...], beyond_far_ref[:, odd])


def first_conv_kernel(
    src_ref, far_ref, near_ref, corner_ref, kernel_ref, out_ref, triples_ref, outer_ref
):
    core, chip, _, _ = place()
    outer_ref[...] = far_ref[...]
    outer_ref[pl.ds(4 * core, 2)] += corner_ref[...]
    fill_triples(src_ref, outer_ref, near_ref, triples_ref, 6)

    @pl.when(core == 0)
    def _():
        out_ref[...] = conv(triples_ref, kernel_ref, 4)

    @pl.when(core == 1)
    def _():
        out_ref[...] = back_terms(triples_ref, kernel_ref, 4, TAPS)

    @pl.when((core == 1) & (chip == 0))
    def _():
        out_ref[0:128, :] += back_terms(triples_ref, kernel_ref, 1, FOLD)


def assemble_grad_kernel(act_ref, before_ref, far_ref, src_ref, inner_ref, corner_ref):
    core, _, end, odd = place()

    @pl.when(core == 0)
    def _():
        src_ref[...] = act_ref[...]
        corner_ref[...] = before_ref[:, 0]

    @pl.when(core == 1)
    def _():
        src_ref[0:2] = act_ref[2:4]
        src_ref[2:4] = before_ref[...]
        corner_ref[...] = jnp.where(end, far_ref[2:4], before_ref[:, odd])

    inner_ref[...] = src_ref[:, 1 - odd]


def input_conv_kernel(
    src_ref, far_ref, corner_ref, near_ref, kernel_ref, cot_ref, out_ref, outer_ref, triples_ref, sum_ref
):
    core, chip, _, _ = place()
    outer_ref[...] = far_ref[...]

    @pl.when(core == 1)
    def _():
        outer_ref[2:4] = corner_ref[...]

    fill_triples(src_ref, outer_ref, near_ref, triples_ref, 4)
    sum_ref[...] = back_terms(triples_ref, kernel_ref, 2, TAPS)

    @pl.when((core == 0) & (chip == 0))
    def _():
        sum_ref[0:128, :] += back_terms(triples_ref, kernel_ref, 1, FOLD)

    cot = cot_ref[...].reshape(256, 128).astype(jnp.float32)
    out_ref[...] = (cot + sum_ref[...]).astype(jnp.bfloat16).reshape(out_ref.shape)


def grads_kernel(own_ref, other_ref, triples_ref, send_ref, act_ref, edge_ref, before_ref, terms_ref):
    core, _, _, odd = place()
    own, other = own_ref[...], other_ref[...]
    pre_act = jnp.where(core == 0, own, other).astype(jnp.bfloat16).astype(jnp.float32)
    back_grad = jnp.where(core == 0, other, own)
    sig = 1.0 / (1.0 + jnp.exp(-pre_act))
    act_grad = (back_grad * (sig * (1.0 + pre_act * (1.0 - sig)))).astype(jnp.bfloat16)
    hidden = (pre_act * sig).astype(jnp.bfloat16)
    act_ref[...] = act_grad.reshape(act_ref.shape)
    edge_ref[0:2] = act_ref[pl.ds(2 * core, 2), odd]
    edge_ref[2:4] = act_ref[pl.ds(2 - 2 * core, 2), odd]

    @pl.when(core == 0)
    def _():
        before_ref[...] = act_ref[0:2]

    @pl.when(core == 1)
    def _():
        before_ref[:, 0] = act_ref[0:2, odd]
        before_ref[:, 1] = act_ref[0:2, odd]

    @pl.when(core == 0)
    def _():
        for a in range(3):
            for b in range(3):
                start = (a * 3 + b) * 384
                terms_ref[start : start + 384, :] = contract_first(stripe(triples_ref, a, 4, b), act_grad)

    @pl.when(core == 1)
    def _():
        for a in range(3):
            for b in range(3):
                part = contract_first(hidden, stripe(triples_ref, a, 4, b))
                for d in range(3):
                    start = ((2 - a) * 9 + (2 - b) * 3 + (2 - d)) * 128
                    terms_ref[start : start + 128, :] = part[:, d * 128 : (d + 1) * 128]

    @pl.when((core == 1) & (lax.axis_index("zh") == 0) & (lax.axis_index("y") == 0))
    def _():
        for f, a in ((0, 2), (0, 1), (1, 2)):
            for b in range(3):
                part = contract_first(hidden[0:128], stripe(triples_ref, f, 1, b))
                for d in range(3):
                    start = ((2 - a) * 9 + (2 - b) * 3 + (2 - d)) * 128
                    terms_ref[start : start + 128, :] += part[:, d * 128 : (d + 1) * 128]

    for y in range(4):
        for x in range(4):
            blocks = []
            for zh in range(2):
                for c in range(2):
                    start = 54 * (((zh * 4 + y) * 2 + c) * 4 + x)
                    blocks.append(terms_ref[start : start + 54, :])
            blocks.append(jnp.zeros((8, 128), jnp.float32))
            rank = y * 4 + x
            rank = jnp.where(lax.axis_index("zh") == 0, 15 - rank, rank)
            send_ref[rank] = jnp.concatenate(blocks, axis=0).astype(jnp.bfloat16)


def plane_sum_kernel(got_ref, send_ref, sum_ref):
    total = got_ref[0].astype(jnp.float32)
    for k in range(1, 16):
        total = total + got_ref[k].astype(jnp.float32)
    sum_ref[...] = total
    lane = lax.broadcasted_iota(jnp.int32, (8, 128), 1)
    for zh in range(2):
        for zl in range(8):
            pieces = []
            for c in range(2):
                value = (zh * 2 + c) * 54 * 128 + zl * 864
                row, shift = value // 128, value % 128
                piece = sum_ref[row : row + 8, :]
                if shift:
                    after = sum_ref[row + 1 : row + 9, :]
                    piece = jnp.where(
                        lane < 128 - shift,
                        pltpu.roll(piece, 128 - shift, 1),
                        pltpu.roll(after, 128 - shift, 1),
                    )
                pieces.append(piece)
            send_ref[zh * 8 + zl] = jnp.concatenate(pieces, axis=0).astype(jnp.bfloat16)


def line_sum_kernel(got_ref, own_ref, send_ref):
    core = lax.axis_index("c")
    total = got_ref[0].astype(jnp.float32)
    for k in range(1, 16):
        total = total + got_ref[k].astype(jnp.float32)
    own_ref[...] = jnp.where(core == 0, total[0:8], total[8:16])
    send_ref[...] = jnp.where(core == 0, total[8:16], total[0:8])


def place_kernel(scale, own_ref, other_ref, out_ref):
    core = lax.axis_index("c")
    own, other = own_ref[...] * scale, other_ref[...] * scale
    shares = (jnp.where(core == 0, own, other), jnp.where(core == 0, other, own))
    for k in range(2):
        for r in range(7):
            width = min(128, 864 - 128 * r)
            out_ref[k : k + 1, 128 * r : 128 * r + width] = shares[k][r : r + 1, :width]


def call(kernel, out_shape, *args, scratch=(), flops=0):
    many = isinstance(out_shape, (list, tuple))
    return pl.pallas_call(
        kernel,
        out_shape=out_shape,
        in_specs=[VMEM] * len(args),
        out_specs=[VMEM] * len(out_shape) if many else VMEM,
        scratch_shapes=scratch,
        compiler_params=pltpu.CompilerParams(vmem_limit_bytes=32 * 1024 * 1024),
        cost_estimate=pl.CostEstimate(flops=flops, bytes_accessed=0, transcendentals=0) if flops else None,
    )(*args)


def shaped(shape, dtype):
    return jax.ShapeDtypeStruct(shape, dtype)


def per_device(video_clip, first_kernel, second_kernel, cotangent):
    bf16, f32 = jnp.bfloat16, jnp.float32
    core = lax.axis_index("c")
    everywhere = TM + ROWS
    first_kernel, second_kernel = first_kernel.reshape(3456, 128), second_kernel.reshape(3456, 128)
    given = jnp.where(core == 0, cotangent, video_clip)
    mine = jnp.where(core == 0, video_clip, cotangent)
    given, mine = lax.optimization_barrier((given, mine))
    both = lax.all_gather(given, "c", tiled=True)
    both, given = lax.optimization_barrier((both, given))
    beyond_far = lax.ppermute(given, TM, BEYOND_FAR)
    beyond = lax.ppermute(given, TM, BEYOND)
    edge, corner = call(
        edge_kernel,
        (shaped((6, 64, 128), bf16), shaped((2, 64, 128), bf16)),
        mine, both, beyond,
    )
    far = lax.ppermute(edge, ROWS, FAR_ROWS)
    free = lax.ppermute(corner, everywhere, CORNER_FREE)
    source, inner, corner = call(
        assemble_kernel,
        (shaped((6, 2, 64, 128), bf16), shaped((6, 64, 128), bf16), shaped((2, 64, 128), bf16)),
        mine, both, beyond, beyond_far, free,
    )
    inner, corner, second = lax.optimization_barrier((inner, corner, second_kernel))
    kernel = jnp.where(core == 0, first_kernel, second)
    near = lax.ppermute(inner, ROWS, NEAR_ROWS)
    corner = lax.ppermute(corner, everywhere, CORNER_ROWS)
    own, triples = call(
        first_conv_kernel,
        (shaped((512, 128), f32), shaped((6, 4, 64, 384), bf16)),
        source, far, near, corner, kernel,
        scratch=[pltpu.VMEM((6, 64, 128), bf16)],
    )
    other = lax.ppermute(own, "c", SWAP)
    send, act_grad, edge, before = call(
        grads_kernel,
        (
            shaped((16, 224, 128), bf16), shaped((4, 2, 64, 128), bf16),
            shaped((4, 64, 128), bf16), shaped((2, 2, 64, 128), bf16),
        ),
        own, other, triples,
        scratch=[pltpu.VMEM((3456, 128), f32)],
    )
    got = lax.all_to_all(send, ("zh", "y", "x"), 0, 0, axis_index_groups=PLANES, tiled=True)
    before = lax.ppermute(before, everywhere, BEFORE)
    far = lax.ppermute(edge, ROWS, FAR_ROWS)
    send = call(plane_sum_kernel, shaped((16, 16, 128), bf16), got, scratch=[pltpu.VMEM((224, 128), f32)])
    got = lax.all_to_all(send, ("zh", "zl"), 0, 0, tiled=True)
    _, before, far = lax.optimization_barrier((send, before, far))
    source, inner, corner = call(
        assemble_grad_kernel,
        (shaped((4, 2, 64, 128), bf16), shaped((4, 64, 128), bf16), shaped((2, 64, 128), bf16)),
        act_grad, before, far,
    )
    near = lax.ppermute(inner, ROWS, NEAR_ROWS)
    corner = lax.ppermute(corner, everywhere, CORNER_GRAD)
    input_grad = call(
        input_conv_kernel,
        shaped((2, 2, 64, 128), bf16),
        source, far, corner, near, first_kernel, cotangent,
        scratch=[
            pltpu.VMEM((4, 64, 128), bf16), pltpu.VMEM((4, 4, 64, 384), bf16), pltpu.VMEM((256, 128), f32),
        ],
        flops=1_600_000_000,
    )
    got, input_grad = lax.optimization_barrier((got, input_grad))
    scale = 1.0 / math.sqrt(131072)
    own_share, send_share = call(line_sum_kernel, (shaped((8, 128), f32),) * 2, got)
    other_share = lax.ppermute(send_share, "c", SWAP)
    weight_grads = call(
        lambda *refs: place_kernel(scale, *refs), shaped((2, 864), f32), own_share, other_share
    )
    return input_grad, weight_grads


def solution(mesh):
    fine = Mesh(np.asarray(mesh.devices).reshape(2, 4, 2, 4, 8), TM + ROWS)
    return jax.shard_map(
        per_device,
        mesh=fine,
        in_specs=(P(TM, ROWS, None, None), P(), P(), P(TM, ROWS, None, None)),
        out_specs=(P(TM, ROWS, None, None), P(None, TM + ROWS)),
        check_vma=False,
    )
```

```python
import math

import jax
import jax.numpy as jnp
import numpy as np
from jax import lax
from jax.experimental import pallas as pl
from jax.experimental.pallas import tpu as pltpu
from jax.sharding import Mesh, PartitionSpec as P

TM = ("zh", "y", "c")
ROWS = ("x", "zl")
VMEM = pl.BlockSpec(memory_space=pltpu.VMEM)


NEAR_ROWS = [(r, r ^ 1) for r in range(32)]
FAR_ROWS = [(r, r + 1) for r in range(1, 31, 2)] + [(r + 1, r) for r in range(1, 31, 2)]
ENDS = [(r, q) for r, q in FAR_ROWS if r // 8 != q // 8]
MIDDLES = [(r, q) for r, q in FAR_ROWS if r // 8 == q // 8]
ENDS_OF = [r for r, _ in ENDS]


PLANES = [list(range(12, 16)) + list(range(12)), list(range(16, 32))]


LINES = [[(12 - z) % 16 for z in range(16)]]


def device(chip, core, slab):
    return (2 * chip + core) * 32 + slab


BEYOND = [pair for k in (0, 1, 2, 4, 5, 6) for pair in ((2 * k + 1, 2 * k + 2), (2 * k + 2, 2 * k + 1))]
BEYOND_FAR = [(7, 8), (8, 7)]
CORNER_FREE = [(device(3, 0, r), device(4, 1, q)) for r, q in ENDS] + [
    (device(4, 1, r), device(3, 0, q)) for r, q in ENDS
]
CORNER_ROWS = [(device(k, c, r), device(k, c, q)) for k, c in ((3, 1), (4, 0)) for r, q in MIDDLES] + [
    (device(k, c, r), device(k, 1 - c, r)) for k, c in ((3, 0), (4, 1)) for r in ENDS_OF
]
BEFORE = [(device(k + 1, 0, r), device(k, 1, r)) for k in range(7) for r in range(32)] + [
    (device(4, 1, r), device(3, 0, q)) for r, q in ENDS
]
CORNER_GRAD = (
    [(device(k, 1, r), device(k, 1, q)) for k in range(7) for r, q in MIDDLES]
    + [(device(k + 1, 1, r), device(k, 1, r)) for k in (0, 1, 2, 4, 5, 6) for r in ENDS_OF]
    + [(device(3, 0, r), device(3, 1, r)) for r in ENDS_OF]
)


def place():
    core = lax.axis_index("c")
    chip = lax.axis_index("zh") * 4 + lax.axis_index("y")
    odd = lax.axis_index("zl") & 1
    end = (lax.axis_index("zl") == 0) | (lax.axis_index("zl") == 7)
    return core, chip, end, odd


def contract_first(lhs, rhs):
    return lax.dot_general(lhs, rhs, (((0,), (0,)), ((), ())), preferred_element_type=jnp.float32)


def fill_triples(src_ref, far_ref, near_ref, triples_ref, frames):
    odd = place()[3]
    columns = src_ref.shape[2]
    chans = src_ref.shape[3]
    col = lax.broadcasted_iota(jnp.int32, (columns, chans), 0)
    for f in range(frames):
        for r in range(4):
            if r in (0, 3):
                cells = jnp.where(odd == (r == 3), far_ref[f], near_ref[f])
            else:
                cells = src_ref[f, r - 1]
            wide = cells.astype(jnp.float32)
            before = jnp.where(col == 0, 0.0, pltpu.roll(wide, 1, 0))
            after = jnp.where(col == columns - 1, 0.0, pltpu.roll(wide, columns - 1, 0))
            triples_ref[f, r, :, 0:chans] = before.astype(cells.dtype)
            triples_ref[f, r, :, chans : 2 * chans] = cells
            triples_ref[f, r, :, 2 * chans : 3 * chans] = after.astype(cells.dtype)


def stripe(triples_ref, f, count, b):
    part = triples_ref[f : f + count, b : b + 2]
    return part.reshape(count * 2 * part.shape[2], part.shape[3])


def conv(triples_ref, kernel_ref, frames):
    total = None
    for a in range(3):
        for b in range(3):
            start = (a * 3 + b) * 384
            term = jnp.dot(
                stripe(triples_ref, a, frames, b),
                kernel_ref[start : start + 384, :],
                preferred_element_type=jnp.float32,
            )
            total = term if total is None else total + term
    return total


def back_terms(triples_ref, kernel_ref, frames, taps):
    total = None
    for f, a in taps:
        for b in range(3):
            part = stripe(triples_ref, f, frames, b)
            starts = [((2 - a) * 9 + (2 - b) * 3 + (2 - d)) * 128 for d in range(3)]
            turned = jnp.concatenate([kernel_ref[start : start + 128, :] for start in starts], axis=1)
            term = lax.dot_general(part, turned, (((1,), (1,)), ((), ())), preferred_element_type=jnp.float32)
            total = term if total is None else total + term
    return total


TAPS = ((0, 0), (1, 1), (2, 2))
FOLD = ((0, 2), (0, 1), (1, 2))


def edge_kernel(mine_ref, both_ref, beyond_ref, edge_ref, corner_ref):
    core, chip, _, odd = place()
    other_ref = both_ref.at[pl.ds(2 - 2 * core, 2)]
    corner_ref[...] = other_ref[:, odd]
    edge_ref[pl.ds(4 * core, 2)] = beyond_ref[:, odd]
    edge_ref[2:4] = mine_ref[:, odd]
    edge_ref[pl.ds(4 - 4 * core, 2)] = other_ref[:, odd]

    @pl.when((core == 0) & (chip == 0))
    def _():
        edge_ref[0] = mine_ref[0, odd]
        edge_ref[1] = mine_ref[0, odd]


def assemble_kernel(mine_ref, both_ref, beyond_ref, beyond_far_ref, free_ref, src_ref, inner_ref, corner_ref):
    core, chip, end, odd = place()
    src_ref[pl.ds(4 * core, 2)] = beyond_ref[...] + beyond_far_ref[...]
    src_ref[2:4] = mine_ref[...]
    src_ref[pl.ds(4 - 4 * core, 2)] = both_ref[pl.ds(2 - 2 * core, 2)]

    @pl.when((core == 0) & (chip == 0))
    def _():
        src_ref[0] = mine_ref[0]
        src_ref[1] = mine_ref[0]

    inner_ref[...] = src_ref[:, 1 - odd]
    corner_ref[...] = jnp.where(end, free_ref[...], beyond_far_ref[:, odd])


def first_conv_kernel(
    src_ref, far_ref, near_ref, corner_ref, kernel_ref, out_ref, triples_ref, outer_ref
):
    core, chip, _, _ = place()
    outer_ref[...] = far_ref[...]
    outer_ref[pl.ds(4 * core, 2)] += corner_ref[...]
    fill_triples(src_ref, outer_ref, near_ref, triples_ref, 6)

    @pl.when(core == 0)
    def _():
        out_ref[...] = conv(triples_ref, kernel_ref, 4)

    @pl.when(core == 1)
    def _():
        out_ref[...] = back_terms(triples_ref, kernel_ref, 4, TAPS)

    @pl.when((core == 1) & (chip == 0))
    def _():
        out_ref[0:128, :] += back_terms(triples_ref, kernel_ref, 1, FOLD)


def assemble_grad_kernel(act_ref, before_ref, far_ref, src_ref, inner_ref, corner_ref):
    core, _, end, odd = place()

    @pl.when(core == 0)
    def _():
        src_ref[...] = act_ref[...]
        corner_ref[...] = before_ref[:, 0]

    @pl.when(core == 1)
    def _():
        src_ref[0:2] = act_ref[2:4]
        src_ref[2:4] = before_ref[...]
        corner_ref[...] = jnp.where(end, far_ref[2:4], before_ref[:, odd])

    inner_ref[...] = src_ref[:, 1 - odd]


def input_conv_kernel(
    src_ref, far_ref, corner_ref, near_ref, kernel_ref, cot_ref, out_ref, outer_ref, triples_ref, sum_ref
):
    core, chip, _, _ = place()
    outer_ref[...] = far_ref[...]

    @pl.when(core == 1)
    def _():
        outer_ref[2:4] = corner_ref[...]

    fill_triples(src_ref, outer_ref, near_ref, triples_ref, 4)
    sum_ref[...] = back_terms(triples_ref, kernel_ref, 2, TAPS)

    @pl.when((core == 0) & (chip == 0))
    def _():
        sum_ref[0:128, :] += back_terms(triples_ref, kernel_ref, 1, FOLD)

    cot = cot_ref[...].reshape(256, 128).astype(jnp.float32)
    out_ref[...] = (cot + sum_ref[...]).astype(jnp.bfloat16).reshape(out_ref.shape)


def grads_kernel(both_ref, triples_ref, send_ref, act_ref, edge_ref, before_ref, terms_ref):
    core, _, _, odd = place()
    pre_act = both_ref[0:512, :].astype(jnp.bfloat16).astype(jnp.float32)
    back_grad = both_ref[512:1024, :]
    sig = 1.0 / (1.0 + jnp.exp(-pre_act))
    act_grad = (back_grad * (sig * (1.0 + pre_act * (1.0 - sig)))).astype(jnp.bfloat16)
    hidden = (pre_act * sig).astype(jnp.bfloat16)
    act_ref[...] = act_grad.reshape(act_ref.shape)
    edge_ref[0:2] = act_ref[pl.ds(2 * core, 2), odd]
    edge_ref[2:4] = act_ref[pl.ds(2 - 2 * core, 2), odd]

    @pl.when(core == 0)
    def _():
        before_ref[...] = act_ref[0:2]

    @pl.when(core == 1)
    def _():
        before_ref[:, 0] = act_ref[0:2, odd]
        before_ref[:, 1] = act_ref[0:2, odd]

    @pl.when(core == 0)
    def _():
        for a in range(3):
            for b in range(3):
                start = (a * 3 + b) * 384
                terms_ref[start : start + 384, :] = contract_first(stripe(triples_ref, a, 4, b), act_grad)

    @pl.when(core == 1)
    def _():
        for a in range(3):
            for b in range(3):
                part = contract_first(hidden, stripe(triples_ref, a, 4, b))
                for d in range(3):
                    start = ((2 - a) * 9 + (2 - b) * 3 + (2 - d)) * 128
                    terms_ref[start : start + 128, :] = part[:, d * 128 : (d + 1) * 128]

    @pl.when((core == 1) & (lax.axis_index("zh") == 0) & (lax.axis_index("y") == 0))
    def _():
        for f, a in ((0, 2), (0, 1), (1, 2)):
            for b in range(3):
                part = contract_first(hidden[0:128], stripe(triples_ref, f, 1, b))
                for d in range(3):
                    start = ((2 - a) * 9 + (2 - b) * 3 + (2 - d)) * 128
                    terms_ref[start : start + 128, :] += part[:, d * 128 : (d + 1) * 128]

    for y in range(4):
        for x in range(4):
            blocks = []
            for zh in range(2):
                for c in range(2):
                    start = 54 * (((zh * 4 + y) * 2 + c) * 4 + x)
                    blocks.append(terms_ref[start : start + 54, :])
            blocks.append(jnp.zeros((8, 128), jnp.float32))
            rank = y * 4 + x
            rank = jnp.where(lax.axis_index("zh") == 0, (rank + 4) % 16, rank)
            send_ref[rank] = jnp.concatenate(blocks, axis=0).astype(jnp.bfloat16)


def plane_sum_kernel(got_ref, send_ref, sum_ref):
    total = got_ref[0].astype(jnp.float32)
    for k in range(1, 16):
        total = total + got_ref[k].astype(jnp.float32)
    sum_ref[...] = total
    lane = lax.broadcasted_iota(jnp.int32, (8, 128), 1)
    for zh in range(2):
        for zl in range(8):
            pieces = []
            for c in range(2):
                value = (zh * 2 + c) * 54 * 128 + zl * 864
                row, shift = value // 128, value % 128
                piece = sum_ref[row : row + 8, :]
                if shift:
                    after = sum_ref[row + 1 : row + 9, :]
                    piece = jnp.where(
                        lane < 128 - shift,
                        pltpu.roll(piece, 128 - shift, 1),
                        pltpu.roll(after, 128 - shift, 1),
                    )
                pieces.append(piece)
            send_ref[LINES[0].index(zh * 8 + zl)] = jnp.concatenate(pieces, axis=0).astype(jnp.bfloat16)


def line_sum_kernel(got_ref, sum_ref):
    total = got_ref[0].astype(jnp.float32)
    for k in range(1, 16):
        total = total + got_ref[k].astype(jnp.float32)
    sum_ref[...] = total


def place_kernel(scale, shares_ref, out_ref):
    for k in range(2):
        start = pl.multiple_of(16 * k + 8 * lax.axis_index("c"), 8)
        share = shares_ref[pl.ds(start, 8), :] * scale
        for r in range(7):
            width = min(128, 864 - 128 * r)
            out_ref[k : k + 1, 128 * r : 128 * r + width] = share[r : r + 1, :width]


def call(kernel, out_shape, *args, scratch=(), flops=0):
    many = isinstance(out_shape, (list, tuple))
    return pl.pallas_call(
        kernel,
        out_shape=out_shape,
        in_specs=[VMEM] * len(args),
        out_specs=[VMEM] * len(out_shape) if many else VMEM,
        scratch_shapes=scratch,
        compiler_params=pltpu.CompilerParams(vmem_limit_bytes=32 * 1024 * 1024),
        cost_estimate=pl.CostEstimate(flops=flops, bytes_accessed=0, transcendentals=0) if flops else None,
    )(*args)


def shaped(shape, dtype):
    return jax.ShapeDtypeStruct(shape, dtype)


def per_device(video_clip, first_kernel, second_kernel, cotangent):
    bf16, f32 = jnp.bfloat16, jnp.float32
    core = lax.axis_index("c")
    everywhere = TM + ROWS
    first_kernel, second_kernel = first_kernel.reshape(3456, 128), second_kernel.reshape(3456, 128)
    given = jnp.where(core == 0, cotangent, video_clip)
    mine = jnp.where(core == 0, video_clip, cotangent)
    given, mine = lax.optimization_barrier((given, mine))
    both = lax.all_gather(given, "c", tiled=True)
    both, given = lax.optimization_barrier((both, given))
    beyond_far = lax.ppermute(given, TM, BEYOND_FAR)
    beyond = lax.ppermute(given, TM, BEYOND)
    edge, corner = call(
        edge_kernel,
        (shaped((6, 64, 128), bf16), shaped((2, 64, 128), bf16)),
        mine, both, beyond,
    )
    far = lax.ppermute(edge, ROWS, FAR_ROWS)
    free = lax.ppermute(corner, everywhere, CORNER_FREE)
    source, inner, corner = call(
        assemble_kernel,
        (shaped((6, 2, 64, 128), bf16), shaped((6, 64, 128), bf16), shaped((2, 64, 128), bf16)),
        mine, both, beyond, beyond_far, free,
    )
    inner, corner, second = lax.optimization_barrier((inner, corner, second_kernel))
    kernel = jnp.where(core == 0, first_kernel, second)
    near = lax.ppermute(inner, ROWS, NEAR_ROWS)
    corner = lax.ppermute(corner, everywhere, CORNER_ROWS)
    own, triples = call(
        first_conv_kernel,
        (shaped((512, 128), f32), shaped((6, 4, 64, 384), bf16)),
        source, far, near, corner, kernel,
        scratch=[pltpu.VMEM((6, 64, 128), bf16)],
    )
    both = lax.all_gather(own, "c", tiled=True)
    send, act_grad, edge, before = call(
        grads_kernel,
        (
            shaped((16, 224, 128), bf16), shaped((4, 2, 64, 128), bf16),
            shaped((4, 64, 128), bf16), shaped((2, 2, 64, 128), bf16),
        ),
        both, triples,
        scratch=[pltpu.VMEM((3456, 128), f32)],
    )
    got = lax.all_to_all(send, ("zh", "y", "x"), 0, 0, axis_index_groups=PLANES, tiled=True)
    before = lax.ppermute(before, everywhere, BEFORE)
    far = lax.ppermute(edge, ROWS, FAR_ROWS)
    send = call(plane_sum_kernel, shaped((16, 16, 128), bf16), got, scratch=[pltpu.VMEM((224, 128), f32)])
    got = lax.all_to_all(send, ("zh", "zl"), 0, 0, axis_index_groups=LINES, tiled=True)
    _, before, far = lax.optimization_barrier((send, before, far))
    source, inner, corner = call(
        assemble_grad_kernel,
        (shaped((4, 2, 64, 128), bf16), shaped((4, 64, 128), bf16), shaped((2, 64, 128), bf16)),
        act_grad, before, far,
    )
    near = lax.ppermute(inner, ROWS, NEAR_ROWS)
    corner = lax.ppermute(corner, everywhere, CORNER_GRAD)
    input_grad = call(
        input_conv_kernel,
        shaped((2, 2, 64, 128), bf16),
        source, far, corner, near, first_kernel, cotangent,
        scratch=[
            pltpu.VMEM((4, 64, 128), bf16), pltpu.VMEM((4, 4, 64, 384), bf16), pltpu.VMEM((256, 128), f32),
        ],
        flops=1_600_000_000,
    )
    got, input_grad = lax.optimization_barrier((got, input_grad))
    scale = 1.0 / math.sqrt(131072)
    shares = call(line_sum_kernel, shaped((16, 128), f32), got)
    shares = lax.all_gather(shares, "c", tiled=True)
    weight_grads = call(lambda *refs: place_kernel(scale, *refs), shaped((2, 864), f32), shares)
    return input_grad, weight_grads


def solution(mesh):
    fine = Mesh(np.asarray(mesh.devices).reshape(2, 4, 2, 4, 8), TM + ROWS)
    return jax.shard_map(
        per_device,
        mesh=fine,
        in_specs=(P(TM, ROWS, None, None), P(), P(), P(TM, ROWS, None, None)),
        out_specs=(P(TM, ROWS, None, None), P(None, TM + ROWS)),
        check_vma=False,
    )
```

```python
import math

import jax
import jax.numpy as jnp
import numpy as np
from jax import lax
from jax.experimental import pallas as pl
from jax.experimental.pallas import tpu as pltpu
from jax.sharding import Mesh, PartitionSpec as P

TM = ("zh", "y", "c")
ROWS = ("x", "zl")
VMEM = pl.BlockSpec(memory_space=pltpu.VMEM)


NEAR_ROWS = [(r, r ^ 1) for r in range(32)]
FAR_ROWS = [(r, r + 1) for r in range(1, 31, 2)] + [(r + 1, r) for r in range(1, 31, 2)]
ENDS = [(r, q) for r, q in FAR_ROWS if r // 8 != q // 8]
MIDDLES = [(r, q) for r, q in FAR_ROWS if r // 8 == q // 8]
ENDS_OF = [r for r, _ in ENDS]


PLANES = [[12, 13, 14, 15, 8, 9, 10, 11, 4, 5, 6, 7, 0, 1, 2, 3], [16 + i for i in [0, 1, 2, 3, 12, 13, 14, 15, 8, 9, 10, 11, 4, 5, 6, 7]]]


LINES = [[(12 - z) % 16 for z in range(16)]]


def device(chip, core, slab):
    return (2 * chip + core) * 32 + slab


BEYOND = [pair for k in (0, 1, 2, 4, 5, 6) for pair in ((2 * k + 1, 2 * k + 2), (2 * k + 2, 2 * k + 1))]
BEYOND_FAR = [(7, 8), (8, 7)]
CORNER_FREE = [(device(3, 0, r), device(4, 1, q)) for r, q in ENDS] + [
    (device(4, 1, r), device(3, 0, q)) for r, q in ENDS
]
CORNER_ROWS = [(device(k, c, r), device(k, c, q)) for k, c in ((3, 1), (4, 0)) for r, q in MIDDLES] + [
    (device(k, c, r), device(k, 1 - c, r)) for k, c in ((3, 0), (4, 1)) for r in ENDS_OF
]
BEFORE = [(device(k + 1, 0, r), device(k, 1, r)) for k in range(7) for r in range(32)] + [
    (device(4, 1, r), device(3, 0, q)) for r, q in ENDS
]
CORNER_GRAD = (
    [(device(k, 1, r), device(k, 1, q)) for k in range(7) for r, q in MIDDLES]
    + [(device(k + 1, 1, r), device(k, 1, r)) for k in (0, 1, 2, 4, 5, 6) for r in ENDS_OF]
    + [(device(3, 0, r), device(3, 1, r)) for r in ENDS_OF]
)


def place():
    core = lax.axis_index("c")
    chip = lax.axis_index("zh") * 4 + lax.axis_index("y")
    odd = lax.axis_index("zl") & 1
    end = (lax.axis_index("zl") == 0) | (lax.axis_index("zl") == 7)
    return core, chip, end, odd


def contract_first(lhs, rhs):
    return lax.dot_general(lhs, rhs, (((0,), (0,)), ((), ())), preferred_element_type=jnp.float32)


def side_by_side(cells):
    columns, chans = cells.shape
    col = lax.broadcasted_iota(jnp.int32, (columns, chans), 0)
    wide = cells.astype(jnp.float32)
    before = jnp.where(col == 0, 0.0, pltpu.roll(wide, 1, 0)).astype(cells.dtype)
    after = jnp.where(col == columns - 1, 0.0, pltpu.roll(wide, columns - 1, 0)).astype(cells.dtype)
    return jnp.concatenate([before, cells, after], axis=1)


def fill_inner(src_ref, triples_ref, frames):
    for f in range(frames):
        for r in range(2):
            triples_ref[f, r + 1] = side_by_side(src_ref[f, r])


def fill_outer(far_ref, near_ref, triples_ref, frames):
    odd = place()[3]
    for f in range(frames):
        triples_ref[f, 0] = side_by_side(jnp.where(odd == 0, far_ref[f], near_ref[f]))
        triples_ref[f, 3] = side_by_side(jnp.where(odd == 1, far_ref[f], near_ref[f]))


def stripe(triples_ref, f, count, b):
    part = triples_ref[f : f + count, b : b + 2]
    return part.reshape(count * 2 * part.shape[2], part.shape[3])


def turned(kernel_ref, a, b):
    starts = [((2 - a) * 9 + (2 - b) * 3 + (2 - d)) * 128 for d in range(3)]
    return jnp.concatenate([kernel_ref[start : start + 128, :] for start in starts], axis=1)


def stage_taps(kernel_ref, taps_ref, back):
    for a in range(3):
        for b in range(3):
            if back:
                taps_ref[a * 3 + b] = turned(kernel_ref, a, b).T
            else:
                taps_ref[a * 3 + b] = kernel_ref[(a * 3 + b) * 384 : (a * 3 + b + 1) * 384, :]


INNER = (((1, 1), (2, 2)), ((0, 1), (1, 2)))
OUTER = (((0, 0),), ((2, 3),))
TAPS = ((0, 0), (1, 1), (2, 2))
FOLD = ((0, 2), (0, 1), (1, 2))


def row_terms(triples_ref, taps_ref, frames, pairs, times):
    total = None
    for f, a in times:
        for b, row in pairs:
            part = triples_ref[f : f + frames, row].reshape(frames * 64, 384)
            term = jnp.dot(part, taps_ref[a * 3 + b], preferred_element_type=jnp.float32)
            total = term if total is None else total + term
    return total


def add_rows(triples_ref, taps_ref, sum_ref, frames, rows, fresh, fold):
    for row in range(2):
        term = row_terms(triples_ref, taps_ref, frames, rows[row], TAPS)
        sum_ref[row] = term if fresh else sum_ref[row] + term

    @pl.when(fold)
    def _():
        for row in range(2):
            sum_ref[row, 0:64, :] += row_terms(triples_ref, taps_ref, 1, rows[row], FOLD)


def interleaved(sum_ref, frames):
    rows = [sum_ref[r, f * 64 : (f + 1) * 64, :] for f in range(frames) for r in range(2)]
    return jnp.concatenate(rows, axis=0)


def edge_kernel(mine_ref, both_ref, beyond_ref, edge_ref, corner_ref):
    core, chip, _, odd = place()
    other_ref = both_ref.at[pl.ds(2 - 2 * core, 2)]
    corner_ref[...] = other_ref[:, odd]
    edge_ref[pl.ds(4 * core, 2)] = beyond_ref[:, odd]
    edge_ref[2:4] = mine_ref[:, odd]
    edge_ref[pl.ds(4 - 4 * core, 2)] = other_ref[:, odd]

    @pl.when((core == 0) & (chip == 0))
    def _():
        edge_ref[0] = mine_ref[0, odd]
        edge_ref[1] = mine_ref[0, odd]


def assemble_kernel(mine_ref, both_ref, beyond_ref, beyond_far_ref, free_ref, src_ref, inner_ref, corner_ref):
    core, chip, end, odd = place()
    src_ref[pl.ds(4 * core, 2)] = beyond_ref[...] + beyond_far_ref[...]
    src_ref[2:4] = mine_ref[...]
    src_ref[pl.ds(4 - 4 * core, 2)] = both_ref[pl.ds(2 - 2 * core, 2)]

    @pl.when((core == 0) & (chip == 0))
    def _():
        src_ref[0] = mine_ref[0]
        src_ref[1] = mine_ref[0]

    inner_ref[...] = src_ref[:, 1 - odd]
    corner_ref[...] = jnp.where(end, free_ref[...], beyond_far_ref[:, odd])


def first_inner_kernel(src_ref, kernel_ref, sum_ref, triples_ref, taps_ref):
    core, chip, _, _ = place()
    fill_inner(src_ref, triples_ref, 6)

    @pl.when(core == 0)
    def _():
        stage_taps(kernel_ref, taps_ref, False)

    @pl.when(core == 1)
    def _():
        stage_taps(kernel_ref, taps_ref, True)

    add_rows(triples_ref, taps_ref, sum_ref, 4, INNER, True, (core == 1) & (chip == 0))


def first_outer_kernel(
    inner_ref, triples_in_ref, taps_ref, far_ref, near_ref, corner_ref, out_ref, triples_ref, outer_ref, sum_ref
):
    core, chip, _, _ = place()
    outer_ref[...] = far_ref[...]
    outer_ref[pl.ds(4 * core, 2)] += corner_ref[...]
    fill_outer(outer_ref, near_ref, triples_ref, 6)
    sum_ref[...] = inner_ref[...]
    add_rows(triples_ref, taps_ref, sum_ref, 4, OUTER, False, (core == 1) & (chip == 0))
    out_ref[...] = interleaved(sum_ref, 4)


def assemble_grad_kernel(act_ref, before_ref, far_ref, src_ref, inner_ref, corner_ref):
    core, _, end, odd = place()

    @pl.when(core == 0)
    def _():
        src_ref[...] = act_ref[...]
        corner_ref[...] = before_ref[:, 0]

    @pl.when(core == 1)
    def _():
        src_ref[0:2] = act_ref[2:4]
        src_ref[2:4] = before_ref[...]
        corner_ref[...] = jnp.where(end, far_ref[2:4], before_ref[:, odd])

    inner_ref[...] = src_ref[:, 1 - odd]


def input_inner_kernel(src_ref, kernel_ref, sum_ref, triples_ref, taps_ref):
    core, chip, _, _ = place()
    fill_inner(src_ref, triples_ref, 4)
    stage_taps(kernel_ref, taps_ref, True)
    add_rows(triples_ref, taps_ref, sum_ref, 2, INNER, True, (core == 0) & (chip == 0))


def input_outer_kernel(
    inner_ref, taps_ref, far_ref, corner_ref, near_ref, cot_ref, triples_in_ref, out_ref, triples_ref, outer_ref,
    sum_ref
):
    core, chip, _, _ = place()
    outer_ref[...] = far_ref[...]

    @pl.when(core == 1)
    def _():
        outer_ref[2:4] = corner_ref[...]

    fill_outer(outer_ref, near_ref, triples_ref, 4)
    sum_ref[...] = inner_ref[...]
    add_rows(triples_ref, taps_ref, sum_ref, 2, OUTER, False, (core == 0) & (chip == 0))
    cot = cot_ref[...].reshape(256, 128).astype(jnp.float32)
    out_ref[...] = (cot + interleaved(sum_ref, 2)).astype(jnp.bfloat16).reshape(out_ref.shape)


def grads_kernel(both_ref, triples_ref, send_ref, act_ref, edge_ref, before_ref, terms_ref):
    core, _, _, odd = place()
    pre_act = both_ref[0:512, :].astype(jnp.bfloat16).astype(jnp.float32)
    back_grad = both_ref[512:1024, :]
    sig = 1.0 / (1.0 + jnp.exp(-pre_act))
    act_grad = (back_grad * (sig * (1.0 + pre_act * (1.0 - sig)))).astype(jnp.bfloat16)
    hidden = (pre_act * sig).astype(jnp.bfloat16)
    act_ref[...] = act_grad.reshape(act_ref.shape)
    edge_ref[0:2] = act_ref[pl.ds(2 * core, 2), odd]
    edge_ref[2:4] = act_ref[pl.ds(2 - 2 * core, 2), odd]

    @pl.when(core == 0)
    def _():
        before_ref[...] = act_ref[0:2]

    @pl.when(core == 1)
    def _():
        before_ref[:, 0] = act_ref[0:2, odd]
        before_ref[:, 1] = act_ref[0:2, odd]

    @pl.when(core == 0)
    def _():
        for a in range(3):
            for b in range(3):
                start = (a * 3 + b) * 384
                terms_ref[start : start + 384, :] = contract_first(stripe(triples_ref, a, 4, b), act_grad)

    @pl.when(core == 1)
    def _():
        for a in range(3):
            for b in range(3):
                part = contract_first(hidden, stripe(triples_ref, a, 4, b))
                for d in range(3):
                    start = ((2 - a) * 9 + (2 - b) * 3 + (2 - d)) * 128
                    terms_ref[start : start + 128, :] = part[:, d * 128 : (d + 1) * 128]

    @pl.when((core == 1) & (lax.axis_index("zh") == 0) & (lax.axis_index("y") == 0))
    def _():
        for f, a in ((0, 2), (0, 1), (1, 2)):
            for b in range(3):
                part = contract_first(hidden[0:128], stripe(triples_ref, f, 1, b))
                for d in range(3):
                    start = ((2 - a) * 9 + (2 - b) * 3 + (2 - d)) * 128
                    terms_ref[start : start + 128, :] += part[:, d * 128 : (d + 1) * 128]

    for y in range(4):
        for x in range(4):
            blocks = []
            for zh in range(2):
                for c in range(2):
                    start = 54 * (((zh * 4 + y) * 2 + c) * 4 + x)
                    blocks.append(terms_ref[start : start + 54, :])
            place0, place1 = PLANES[0].index(y * 4 + x), PLANES[1].index(16 + y * 4 + x)
            rank = jnp.where(lax.axis_index("zh") == 0, place0, place1)
            send_ref[rank] = jnp.concatenate(blocks, axis=0).astype(jnp.bfloat16)


def plane_sum_kernel(got_ref, send_ref, sum_ref):
    total = got_ref[0].astype(jnp.float32)
    for k in range(1, 16):
        total = total + got_ref[k].astype(jnp.float32)
    sum_ref[0:216] = total
    sum_ref[216:224] = jnp.zeros((8, 128), jnp.float32)
    lane = lax.broadcasted_iota(jnp.int32, (8, 128), 1)
    for zh in range(2):
        for zl in range(8):
            pieces = []
            for c in range(2):
                value = (zh * 2 + c) * 54 * 128 + zl * 864
                row, shift = value // 128, value % 128
                piece = sum_ref[row : row + 8, :]
                if shift:
                    after = sum_ref[row + 1 : row + 9, :]
                    piece = jnp.where(
                        lane < 128 - shift,
                        pltpu.roll(piece, 128 - shift, 1),
                        pltpu.roll(after, 128 - shift, 1),
                    )
                pieces.append(piece)
            send_ref[LINES[0].index(zh * 8 + zl)] = jnp.concatenate(pieces, axis=0).astype(jnp.bfloat16)


def line_sum_kernel(got_ref, sum_ref):
    total = got_ref[0].astype(jnp.float32)
    for k in range(1, 16):
        total = total + got_ref[k].astype(jnp.float32)
    sum_ref[...] = total


def place_kernel(scale, shares_ref, out_ref):
    for k in range(2):
        start = pl.multiple_of(16 * k + 8 * lax.axis_index("c"), 8)
        share = shares_ref[pl.ds(start, 8), :] * scale
        for r in range(7):
            width = min(128, 864 - 128 * r)
            out_ref[k : k + 1, 128 * r : 128 * r + width] = share[r : r + 1, :width]


def call(kernel, out_shape, *args, scratch=(), flops=0, aliases=None):
    many = isinstance(out_shape, (list, tuple))
    return pl.pallas_call(
        kernel,
        out_shape=out_shape,
        in_specs=[VMEM] * len(args),
        out_specs=[VMEM] * len(out_shape) if many else VMEM,
        scratch_shapes=scratch,
        input_output_aliases=aliases or {},
        compiler_params=pltpu.CompilerParams(vmem_limit_bytes=32 * 1024 * 1024),
        cost_estimate=pl.CostEstimate(flops=flops, bytes_accessed=0, transcendentals=0) if flops else None,
    )(*args)


def shaped(shape, dtype):
    return jax.ShapeDtypeStruct(shape, dtype)


def per_device(video_clip, first_kernel, second_kernel, cotangent):
    bf16, f32 = jnp.bfloat16, jnp.float32
    core = lax.axis_index("c")
    everywhere = TM + ROWS
    first_kernel, second_kernel = first_kernel.reshape(3456, 128), second_kernel.reshape(3456, 128)
    given = jnp.where(core == 0, cotangent, video_clip)
    mine = jnp.where(core == 0, video_clip, cotangent)
    given, mine = lax.optimization_barrier((given, mine))
    both = lax.all_gather(given, "c", tiled=True)
    both, given = lax.optimization_barrier((both, given))
    beyond_far = lax.ppermute(given, TM, BEYOND_FAR)
    beyond = lax.ppermute(given, TM, BEYOND)
    edge, corner = call(
        edge_kernel,
        (shaped((6, 64, 128), bf16), shaped((2, 64, 128), bf16)),
        mine, both, beyond,
    )
    far = lax.ppermute(edge, ROWS, FAR_ROWS)
    free = lax.ppermute(corner, everywhere, CORNER_FREE)
    source, inner, corner = call(
        assemble_kernel,
        (shaped((6, 2, 64, 128), bf16), shaped((6, 64, 128), bf16), shaped((2, 64, 128), bf16)),
        mine, both, beyond, beyond_far, free,
    )
    inner, corner, second = lax.optimization_barrier((inner, corner, second_kernel))
    kernel = jnp.where(core == 0, first_kernel, second)
    near = lax.ppermute(inner, ROWS, NEAR_ROWS)
    corner = lax.ppermute(corner, everywhere, CORNER_ROWS)
    inner, triples, taps = call(
        first_inner_kernel,
        (shaped((2, 256, 128), f32), shaped((6, 4, 64, 384), bf16), shaped((9, 384, 128), bf16)),
        source, kernel,
        flops=300_000_000,
    )
    own, triples = call(
        first_outer_kernel,
        (shaped((512, 128), f32), shaped((6, 4, 64, 384), bf16)),
        inner, triples, taps, far, near, corner,
        scratch=[pltpu.VMEM((6, 64, 128), bf16), pltpu.VMEM((2, 256, 128), f32)],
        aliases={1: 1},
    )
    both = lax.all_gather(own, "c", tiled=True)
    send, act_grad, edge, before = call(
        grads_kernel,
        (
            shaped((16, 216, 128), bf16), shaped((4, 2, 64, 128), bf16),
            shaped((4, 64, 128), bf16), shaped((2, 2, 64, 128), bf16),
        ),
        both, triples,
        scratch=[pltpu.VMEM((3456, 128), f32)],
    )
    got = lax.all_to_all(send, ("zh", "y", "x"), 0, 0, axis_index_groups=PLANES, tiled=True)
    before = lax.ppermute(before, everywhere, BEFORE)
    far = lax.ppermute(edge, ROWS, FAR_ROWS)
    send = call(plane_sum_kernel, shaped((16, 16, 128), bf16), got, scratch=[pltpu.VMEM((224, 128), f32)])
    got = lax.all_to_all(send, ("zh", "zl"), 0, 0, axis_index_groups=LINES, tiled=True)
    _, before, far = lax.optimization_barrier((send, before, far))
    source, inner, corner = call(
        assemble_grad_kernel,
        (shaped((4, 2, 64, 128), bf16), shaped((4, 64, 128), bf16), shaped((2, 64, 128), bf16)),
        act_grad, before, far,
    )
    near = lax.ppermute(inner, ROWS, NEAR_ROWS)
    corner = lax.ppermute(corner, everywhere, CORNER_GRAD)
    inner, triples, taps = call(
        input_inner_kernel,
        (shaped((2, 128, 128), f32), shaped((4, 4, 64, 384), bf16), shaped((9, 384, 128), bf16)),
        source, first_kernel,
        flops=150_000_000,
    )
    input_grad, _ = call(
        input_outer_kernel,
        (shaped((2, 2, 64, 128), bf16), shaped((4, 4, 64, 384), bf16)),
        inner, taps, far, corner, near, cotangent, triples,
        scratch=[pltpu.VMEM((4, 64, 128), bf16), pltpu.VMEM((2, 128, 128), f32)],
        aliases={6: 1},
        flops=1_600_000_000,
    )
    got, input_grad = lax.optimization_barrier((got, input_grad))
    scale = 1.0 / math.sqrt(131072)
    shares = call(line_sum_kernel, shaped((16, 128), f32), got)
    shares = lax.all_gather(shares, "c", tiled=True)
    weight_grads = call(lambda *refs: place_kernel(scale, *refs), shaped((2, 864), f32), shares)
    return input_grad, weight_grads


def solution(mesh):
    fine = Mesh(np.asarray(mesh.devices).reshape(2, 4, 2, 4, 8), TM + ROWS)
    return jax.shard_map(
        per_device,
        mesh=fine,
        in_specs=(P(TM, ROWS, None, None), P(), P(), P(TM, ROWS, None, None)),
        out_specs=(P(TM, ROWS, None, None), P(None, TM + ROWS)),
        check_vma=False,
    )
```

```python
import math

import jax
import jax.numpy as jnp
import numpy as np
from jax import lax
from jax.experimental import pallas as pl
from jax.experimental.pallas import tpu as pltpu
from jax.sharding import Mesh, PartitionSpec as P

TM = ("zh", "y", "c")
ROWS = ("x", "zl")
VMEM = pl.BlockSpec(memory_space=pltpu.VMEM)


NEAR_ROWS = [(r, r ^ 1) for r in range(32)]
FAR_ROWS = [(r, r + 1) for r in range(1, 31, 2)] + [(r + 1, r) for r in range(1, 31, 2)]
ENDS = [(r, q) for r, q in FAR_ROWS if r // 8 != q // 8]
MIDDLES = [(r, q) for r, q in FAR_ROWS if r // 8 == q // 8]
ENDS_OF = [r for r, _ in ENDS]


PLANES = [[12, 13, 14, 15, 8, 9, 10, 11, 4, 5, 6, 7, 0, 1, 2, 3], [16 + i for i in [0, 1, 2, 3, 12, 13, 14, 15, 8, 9, 10, 11, 4, 5, 6, 7]]]


LINES = [[11, 10, 9, 8, 7, 6, 5, 4, 3, 2, 1, 0, 15, 14, 13, 12]]


def device(chip, core, slab):
    return (2 * chip + core) * 32 + slab


BEYOND = [pair for k in (0, 1, 2, 4, 5, 6) for pair in ((2 * k + 1, 2 * k + 2), (2 * k + 2, 2 * k + 1))]
BEYOND_FAR = [(7, 8), (8, 7)]
CORNER_FREE = [(device(3, 0, r), device(4, 1, q)) for r, q in ENDS] + [
    (device(4, 1, r), device(3, 0, q)) for r, q in ENDS
]
CORNER_ROWS = [(device(k, c, r), device(k, c, q)) for k, c in ((3, 1), (4, 0)) for r, q in MIDDLES] + [
    (device(k, c, r), device(k, 1 - c, r)) for k, c in ((3, 0), (4, 1)) for r in ENDS_OF
]
BEFORE = [(device(k + 1, 0, r), device(k, 1, r)) for k in range(7) for r in range(32)] + [
    (device(4, 1, r), device(3, 0, q)) for r, q in ENDS
]
CORNER_GRAD = (
    [(device(k, 1, r), device(k, 1, q)) for k in range(7) for r, q in MIDDLES]
    + [(device(k + 1, 1, r), device(k, 1, r)) for k in (0, 1, 2, 4, 5, 6) for r in ENDS_OF]
    + [(device(3, 0, r), device(3, 1, r)) for r in ENDS_OF]
)


def place():
    core = lax.axis_index("c")
    chip = lax.axis_index("zh") * 4 + lax.axis_index("y")
    odd = lax.axis_index("zl") & 1
    end = (lax.axis_index("zl") == 0) | (lax.axis_index("zl") == 7)
    return core, chip, end, odd


def contract_first(lhs, rhs):
    return lax.dot_general(lhs, rhs, (((0,), (0,)), ((), ())), preferred_element_type=jnp.float32)


def side_by_side(cells):
    columns, chans = cells.shape
    col = lax.broadcasted_iota(jnp.int32, (columns, chans), 0)
    wide = cells.astype(jnp.float32)
    before = jnp.where(col == 0, 0.0, pltpu.roll(wide, 1, 0)).astype(cells.dtype)
    after = jnp.where(col == columns - 1, 0.0, pltpu.roll(wide, columns - 1, 0)).astype(cells.dtype)
    return jnp.concatenate([before, cells, after], axis=1)


def fill_inner(src_ref, triples_ref, frames):
    for f in range(frames):
        for r in range(2):
            triples_ref[f, r + 1] = side_by_side(src_ref[f, r])


def fill_outer(far_ref, near_ref, triples_ref, frames):
    odd = place()[3]
    for f in range(frames):
        triples_ref[f, 0] = side_by_side(jnp.where(odd == 0, far_ref[f], near_ref[f]))
        triples_ref[f, 3] = side_by_side(jnp.where(odd == 1, far_ref[f], near_ref[f]))


def stripe(triples_ref, f, count, b):
    part = triples_ref[f : f + count, b : b + 2]
    return part.reshape(count * 2 * part.shape[2], part.shape[3])


def turned(kernel_ref, a, b):
    starts = [((2 - a) * 9 + (2 - b) * 3 + (2 - d)) * 128 for d in range(3)]
    return jnp.concatenate([kernel_ref[start : start + 128, :] for start in starts], axis=1)


def stage_taps(kernel_ref, taps_ref, back):
    for a in range(3):
        for b in range(3):
            if back:
                taps_ref[a * 3 + b] = turned(kernel_ref, a, b).T
            else:
                taps_ref[a * 3 + b] = kernel_ref[(a * 3 + b) * 384 : (a * 3 + b + 1) * 384, :]


INNER = (((1, 1), (2, 2)), ((0, 1), (1, 2)))
OUTER = (((0, 0),), ((2, 3),))
TAPS = ((0, 0), (1, 1), (2, 2))
FOLD = ((0, 2), (0, 1), (1, 2))


def row_terms(triples_ref, taps_ref, frames, pairs, times):
    total = None
    for f, a in times:
        for b, row in pairs:
            part = triples_ref[f : f + frames, row].reshape(frames * 64, 384)
            term = jnp.dot(part, taps_ref[a * 3 + b], preferred_element_type=jnp.float32)
            total = term if total is None else total + term
    return total


def add_rows(triples_ref, taps_ref, sum_ref, frames, rows, fresh, fold):
    for row in range(2):
        term = row_terms(triples_ref, taps_ref, frames, rows[row], TAPS)
        sum_ref[row] = term if fresh else sum_ref[row] + term

    @pl.when(fold)
    def _():
        for row in range(2):
            sum_ref[row, 0:64, :] += row_terms(triples_ref, taps_ref, 1, rows[row], FOLD)


def interleaved(sum_ref, frames):
    rows = [sum_ref[r, f * 64 : (f + 1) * 64, :] for f in range(frames) for r in range(2)]
    return jnp.concatenate(rows, axis=0)


def edge_kernel(mine_ref, both_ref, beyond_ref, edge_ref, corner_ref):
    core, chip, _, odd = place()
    other_ref = both_ref.at[pl.ds(2 - 2 * core, 2)]
    corner_ref[...] = other_ref[:, odd]
    edge_ref[pl.ds(4 * core, 2)] = beyond_ref[:, odd]
    edge_ref[2:4] = mine_ref[:, odd]
    edge_ref[pl.ds(4 - 4 * core, 2)] = other_ref[:, odd]

    @pl.when((core == 0) & (chip == 0))
    def _():
        edge_ref[0] = mine_ref[0, odd]
        edge_ref[1] = mine_ref[0, odd]


def assemble_kernel(mine_ref, both_ref, beyond_ref, beyond_far_ref, free_ref, src_ref, inner_ref, corner_ref):
    core, chip, end, odd = place()
    src_ref[pl.ds(4 * core, 2)] = beyond_ref[...] + beyond_far_ref[...]
    src_ref[2:4] = mine_ref[...]
    src_ref[pl.ds(4 - 4 * core, 2)] = both_ref[pl.ds(2 - 2 * core, 2)]

    @pl.when((core == 0) & (chip == 0))
    def _():
        src_ref[0] = mine_ref[0]
        src_ref[1] = mine_ref[0]

    inner_ref[...] = src_ref[:, 1 - odd]
    corner_ref[...] = jnp.where(end, free_ref[...], beyond_far_ref[:, odd])


def first_inner_kernel(src_ref, kernel_ref, sum_ref, triples_ref, taps_ref):
    core, chip, _, _ = place()
    fill_inner(src_ref, triples_ref, 6)

    @pl.when(core == 0)
    def _():
        stage_taps(kernel_ref, taps_ref, False)

    @pl.when(core == 1)
    def _():
        stage_taps(kernel_ref, taps_ref, True)

    add_rows(triples_ref, taps_ref, sum_ref, 4, INNER, True, (core == 1) & (chip == 0))


def first_outer_kernel(
    inner_ref, triples_in_ref, taps_ref, far_ref, near_ref, corner_ref, out_ref, triples_ref, outer_ref, sum_ref
):
    core, chip, _, _ = place()
    outer_ref[...] = far_ref[...]
    outer_ref[pl.ds(4 * core, 2)] += corner_ref[...]
    fill_outer(outer_ref, near_ref, triples_ref, 6)
    sum_ref[...] = inner_ref[...]
    add_rows(triples_ref, taps_ref, sum_ref, 4, OUTER, False, (core == 1) & (chip == 0))
    out_ref[...] = interleaved(sum_ref, 4)


def assemble_grad_kernel(act_ref, before_ref, far_ref, src_ref, inner_ref, corner_ref):
    core, _, end, odd = place()

    @pl.when(core == 0)
    def _():
        src_ref[...] = act_ref[...]
        corner_ref[...] = before_ref[:, 0]

    @pl.when(core == 1)
    def _():
        src_ref[0:2] = act_ref[2:4]
        src_ref[2:4] = before_ref[...]
        corner_ref[...] = jnp.where(end, far_ref[2:4], before_ref[:, odd])

    inner_ref[...] = src_ref[:, 1 - odd]


def input_inner_kernel(src_ref, kernel_ref, sum_ref, triples_ref, taps_ref):
    core, chip, _, _ = place()
    fill_inner(src_ref, triples_ref, 4)
    stage_taps(kernel_ref, taps_ref, True)
    add_rows(triples_ref, taps_ref, sum_ref, 2, INNER, True, (core == 0) & (chip == 0))


def input_outer_kernel(
    inner_ref, taps_ref, far_ref, corner_ref, near_ref, cot_ref, triples_in_ref, out_ref, triples_ref, outer_ref,
    sum_ref
):
    core, chip, _, _ = place()
    outer_ref[...] = far_ref[...]

    @pl.when(core == 1)
    def _():
        outer_ref[2:4] = corner_ref[...]

    fill_outer(outer_ref, near_ref, triples_ref, 4)
    sum_ref[...] = inner_ref[...]
    add_rows(triples_ref, taps_ref, sum_ref, 2, OUTER, False, (core == 0) & (chip == 0))
    cot = cot_ref[...].reshape(256, 128).astype(jnp.float32)
    out_ref[...] = (cot + interleaved(sum_ref, 2)).astype(jnp.bfloat16).reshape(out_ref.shape)


def grads_kernel(both_ref, triples_ref, send_ref, act_ref, edge_ref, before_ref, terms_ref):
    core, _, _, odd = place()
    pre_act = both_ref[0:512, :].astype(jnp.bfloat16).astype(jnp.float32)
    back_grad = both_ref[512:1024, :]
    sig = 1.0 / (1.0 + jnp.exp(-pre_act))
    act_grad = (back_grad * (sig * (1.0 + pre_act * (1.0 - sig)))).astype(jnp.bfloat16)
    hidden = (pre_act * sig).astype(jnp.bfloat16)
    act_ref[...] = act_grad.reshape(act_ref.shape)
    edge_ref[0:2] = act_ref[pl.ds(2 * core, 2), odd]
    edge_ref[2:4] = act_ref[pl.ds(2 - 2 * core, 2), odd]

    @pl.when(core == 0)
    def _():
        before_ref[...] = act_ref[0:2]

    @pl.when(core == 1)
    def _():
        before_ref[:, 0] = act_ref[0:2, odd]
        before_ref[:, 1] = act_ref[0:2, odd]

    @pl.when(core == 0)
    def _():
        for a in range(3):
            for b in range(3):
                start = (a * 3 + b) * 384
                terms_ref[start : start + 384, :] = contract_first(stripe(triples_ref, a, 4, b), act_grad)

    @pl.when(core == 1)
    def _():
        for a in range(3):
            for b in range(3):
                part = contract_first(hidden, stripe(triples_ref, a, 4, b))
                for d in range(3):
                    start = ((2 - a) * 9 + (2 - b) * 3 + (2 - d)) * 128
                    terms_ref[start : start + 128, :] = part[:, d * 128 : (d + 1) * 128]

    @pl.when((core == 1) & (lax.axis_index("zh") == 0) & (lax.axis_index("y") == 0))
    def _():
        for f, a in ((0, 2), (0, 1), (1, 2)):
            for b in range(3):
                part = contract_first(hidden[0:128], stripe(triples_ref, f, 1, b))
                for d in range(3):
                    start = ((2 - a) * 9 + (2 - b) * 3 + (2 - d)) * 128
                    terms_ref[start : start + 128, :] += part[:, d * 128 : (d + 1) * 128]

    for y in range(4):
        for x in range(4):
            blocks = []
            for zh in range(2):
                for c in range(2):
                    start = 54 * (((zh * 4 + y) * 2 + c) * 4 + x)
                    blocks.append(terms_ref[start : start + 54, :])
            place0, place1 = PLANES[0].index(y * 4 + x), PLANES[1].index(16 + y * 4 + x)
            rank = jnp.where(lax.axis_index("zh") == 0, place0, place1)
            send_ref[rank] = jnp.concatenate(blocks, axis=0).astype(jnp.bfloat16)


def plane_sum_kernel(got_ref, send_ref, sum_ref):
    total = got_ref[0].astype(jnp.float32)
    for k in range(1, 16):
        total = total + got_ref[k].astype(jnp.float32)
    sum_ref[0:216] = total
    sum_ref[216:224] = jnp.zeros((8, 128), jnp.float32)
    lane = lax.broadcasted_iota(jnp.int32, (8, 128), 1)
    for zh in range(2):
        for zl in range(8):
            pieces = []
            for c in range(2):
                value = (zh * 2 + c) * 54 * 128 + zl * 864
                row, shift = value // 128, value % 128
                piece = sum_ref[row : row + 8, :]
                if shift:
                    after = sum_ref[row + 1 : row + 9, :]
                    piece = jnp.where(
                        lane < 128 - shift,
                        pltpu.roll(piece, 128 - shift, 1),
                        pltpu.roll(after, 128 - shift, 1),
                    )
                pieces.append(piece)
            send_ref[LINES[0].index(zh * 8 + zl)] = jnp.concatenate(pieces, axis=0).astype(jnp.bfloat16)


def line_sum_kernel(got_ref, sum_ref):
    total = got_ref[0].astype(jnp.float32)
    for k in range(1, 16):
        total = total + got_ref[k].astype(jnp.float32)
    sum_ref[...] = total


def place_kernel(scale, shares_ref, out_ref):
    for k in range(2):
        start = pl.multiple_of(16 * k + 8 * lax.axis_index("c"), 8)
        share = shares_ref[pl.ds(start, 8), :] * scale
        for r in range(7):
            width = min(128, 864 - 128 * r)
            out_ref[k : k + 1, 128 * r : 128 * r + width] = share[r : r + 1, :width]


def call(kernel, out_shape, *args, scratch=(), flops=0, aliases=None):
    many = isinstance(out_shape, (list, tuple))
    return pl.pallas_call(
        kernel,
        out_shape=out_shape,
        in_specs=[VMEM] * len(args),
        out_specs=[VMEM] * len(out_shape) if many else VMEM,
        scratch_shapes=scratch,
        input_output_aliases=aliases or {},
        compiler_params=pltpu.CompilerParams(vmem_limit_bytes=32 * 1024 * 1024),
        cost_estimate=pl.CostEstimate(flops=flops, bytes_accessed=0, transcendentals=0) if flops else None,
    )(*args)


def shaped(shape, dtype):
    return jax.ShapeDtypeStruct(shape, dtype)


def per_device(video_clip, first_kernel, second_kernel, cotangent):
    bf16, f32 = jnp.bfloat16, jnp.float32
    core = lax.axis_index("c")
    everywhere = TM + ROWS
    first_kernel, second_kernel = first_kernel.reshape(3456, 128), second_kernel.reshape(3456, 128)
    given = jnp.where(core == 0, cotangent, video_clip)
    mine = jnp.where(core == 0, video_clip, cotangent)
    given, mine = lax.optimization_barrier((given, mine))
    both = lax.all_gather(given, "c", tiled=True)
    both, given = lax.optimization_barrier((both, given))
    beyond_far = lax.ppermute(given, TM, BEYOND_FAR)
    beyond = lax.ppermute(given, TM, BEYOND)
    edge, corner = call(
        edge_kernel,
        (shaped((6, 64, 128), bf16), shaped((2, 64, 128), bf16)),
        mine, both, beyond,
    )
    far = lax.ppermute(edge, ROWS, FAR_ROWS)
    free = lax.ppermute(corner, everywhere, CORNER_FREE)
    source, inner, corner = call(
        assemble_kernel,
        (shaped((6, 2, 64, 128), bf16), shaped((6, 64, 128), bf16), shaped((2, 64, 128), bf16)),
        mine, both, beyond, beyond_far, free,
    )
    inner, corner, second = lax.optimization_barrier((inner, corner, second_kernel))
    kernel = jnp.where(core == 0, first_kernel, second)
    near = lax.ppermute(inner, ROWS, NEAR_ROWS)
    corner = lax.ppermute(corner, everywhere, CORNER_ROWS)
    inner, triples, taps = call(
        first_inner_kernel,
        (shaped((2, 256, 128), f32), shaped((6, 4, 64, 384), bf16), shaped((9, 384, 128), bf16)),
        source, kernel,
        flops=300_000_000,
    )
    own, triples = call(
        first_outer_kernel,
        (shaped((512, 128), f32), shaped((6, 4, 64, 384), bf16)),
        inner, triples, taps, far, near, corner,
        scratch=[pltpu.VMEM((6, 64, 128), bf16), pltpu.VMEM((2, 256, 128), f32)],
        aliases={1: 1},
    )
    both = lax.all_gather(own, "c", tiled=True)
    send, act_grad, edge, before = call(
        grads_kernel,
        (
            shaped((16, 216, 128), bf16), shaped((4, 2, 64, 128), bf16),
            shaped((4, 64, 128), bf16), shaped((2, 2, 64, 128), bf16),
        ),
        both, triples,
        scratch=[pltpu.VMEM((3456, 128), f32)],
    )
    got = lax.all_to_all(send, ("zh", "y", "x"), 0, 0, axis_index_groups=PLANES, tiled=True)
    before = lax.ppermute(before, everywhere, BEFORE)
    far = lax.ppermute(edge, ROWS, FAR_ROWS)
    send = call(plane_sum_kernel, shaped((16, 16, 128), bf16), got, scratch=[pltpu.VMEM((224, 128), f32)])
    got = lax.all_to_all(send, ("zh", "zl"), 0, 0, axis_index_groups=LINES, tiled=True)
    _, before, far = lax.optimization_barrier((send, before, far))
    source, inner, corner = call(
        assemble_grad_kernel,
        (shaped((4, 2, 64, 128), bf16), shaped((4, 64, 128), bf16), shaped((2, 64, 128), bf16)),
        act_grad, before, far,
    )
    near = lax.ppermute(inner, ROWS, NEAR_ROWS)
    corner = lax.ppermute(corner, everywhere, CORNER_GRAD)
    inner, triples, taps = call(
        input_inner_kernel,
        (shaped((2, 128, 128), f32), shaped((4, 4, 64, 384), bf16), shaped((9, 384, 128), bf16)),
        source, first_kernel,
        flops=150_000_000,
    )
    input_grad, _ = call(
        input_outer_kernel,
        (shaped((2, 2, 64, 128), bf16), shaped((4, 4, 64, 384), bf16)),
        inner, taps, far, corner, near, cotangent, triples,
        scratch=[pltpu.VMEM((4, 64, 128), bf16), pltpu.VMEM((2, 128, 128), f32)],
        aliases={6: 1},
        flops=1_600_000_000,
    )
    got, input_grad = lax.optimization_barrier((got, input_grad))
    scale = 1.0 / math.sqrt(131072)
    shares = call(line_sum_kernel, shaped((16, 128), f32), got)
    shares = lax.all_gather(shares, "c", tiled=True)
    weight_grads = call(lambda *refs: place_kernel(scale, *refs), shaped((2, 864), f32), shares)
    return input_grad, weight_grads


def solution(mesh):
    fine = Mesh(np.asarray(mesh.devices).reshape(2, 4, 2, 4, 8), TM + ROWS)
    return jax.shard_map(
        per_device,
        mesh=fine,
        in_specs=(P(TM, ROWS, None, None), P(), P(), P(TM, ROWS, None, None)),
        out_specs=(P(TM, ROWS, None, None), P(None, TM + ROWS)),
        check_vma=False,
    )
```

```python
import math

import jax
import jax.numpy as jnp
import numpy as np
from jax import lax
from jax.experimental import pallas as pl
from jax.experimental.pallas import tpu as pltpu
from jax.sharding import Mesh, PartitionSpec as P

TM = ("zh", "y", "c")
ROWS = ("x", "zl")
VMEM = pl.BlockSpec(memory_space=pltpu.VMEM)


NEAR_ROWS = [(r, r ^ 1) for r in range(32)]
FAR_ROWS = [(r, r + 1) for r in range(1, 31, 2)] + [(r + 1, r) for r in range(1, 31, 2)]
ENDS = [(r, q) for r, q in FAR_ROWS if r // 8 != q // 8]
MIDDLES = [(r, q) for r, q in FAR_ROWS if r // 8 == q // 8]
ENDS_OF = [r for r, _ in ENDS]


PLANES = [
    [half * 16 + (y + 2) % 4 * 4 + (x + 2) % 4 for y in range(4) for x in range(4)] for half in range(2)
]


LINES = [[(12 + z) % 16 for z in range(16)]]


def device(chip, core, slab):
    return (2 * chip + core) * 32 + slab


BEYOND = [pair for k in (0, 1, 2, 4, 5, 6) for pair in ((2 * k + 1, 2 * k + 2), (2 * k + 2, 2 * k + 1))]
BEYOND_FAR = [(7, 8), (8, 7)]
CORNER_FREE = [(device(3, 0, r), device(4, 1, q)) for r, q in ENDS] + [
    (device(4, 1, r), device(3, 0, q)) for r, q in ENDS
]
CORNER_ROWS = [(device(k, c, r), device(k, c, q)) for k, c in ((3, 1), (4, 0)) for r, q in MIDDLES] + [
    (device(k, c, r), device(k, 1 - c, r)) for k, c in ((3, 0), (4, 1)) for r in ENDS_OF
]
BEFORE = [(device(k + 1, 0, r), device(k, 1, r)) for k in range(7) for r in range(32)] + [
    (device(4, 1, r), device(3, 0, q)) for r, q in ENDS
]
CORNER_GRAD = (
    [(device(k, 1, r), device(k, 1, q)) for k in range(7) for r, q in MIDDLES]
    + [(device(k + 1, 1, r), device(k, 1, r)) for k in (0, 1, 2, 4, 5, 6) for r in ENDS_OF]
    + [(device(3, 0, r), device(3, 1, r)) for r in ENDS_OF]
)


def place():
    core = lax.axis_index("c")
    chip = lax.axis_index("zh") * 4 + lax.axis_index("y")
    odd = lax.axis_index("zl") & 1
    end = (lax.axis_index("zl") == 0) | (lax.axis_index("zl") == 7)
    return core, chip, end, odd


def contract_first(lhs, rhs):
    return lax.dot_general(lhs, rhs, (((0,), (0,)), ((), ())), preferred_element_type=jnp.float32)


def side_by_side(cells):
    columns, chans = cells.shape
    col = lax.broadcasted_iota(jnp.int32, (columns, chans), 0)
    wide = cells.astype(jnp.float32)
    before = jnp.where(col == 0, 0.0, pltpu.roll(wide, 1, 0)).astype(cells.dtype)
    after = jnp.where(col == columns - 1, 0.0, pltpu.roll(wide, columns - 1, 0)).astype(cells.dtype)
    return jnp.concatenate([before, cells, after], axis=1)


def fill_inner(src_ref, triples_ref, frames):
    for f in range(frames):
        for r in range(2):
            triples_ref[f, r + 1] = side_by_side(src_ref[f, r])


def fill_outer(far_ref, near_ref, triples_ref, frames):
    odd = place()[3]
    for f in range(frames):
        triples_ref[f, 0] = side_by_side(jnp.where(odd == 0, far_ref[f], near_ref[f]))
        triples_ref[f, 3] = side_by_side(jnp.where(odd == 1, far_ref[f], near_ref[f]))


def stripe(triples_ref, f, count, b):
    part = triples_ref[f : f + count, b : b + 2]
    return part.reshape(count * 2 * part.shape[2], part.shape[3])


def turned(kernel_ref, a, b):
    starts = [((2 - a) * 9 + (2 - b) * 3 + (2 - d)) * 128 for d in range(3)]
    return jnp.concatenate([kernel_ref[start : start + 128, :] for start in starts], axis=1)


def stage_taps(kernel_ref, taps_ref, back):
    for a in range(3):
        for b in range(3):
            if back:
                taps_ref[a * 3 + b] = turned(kernel_ref, a, b).T
            else:
                taps_ref[a * 3 + b] = kernel_ref[(a * 3 + b) * 384 : (a * 3 + b + 1) * 384, :]


INNER = (((1, 1), (2, 2)), ((0, 1), (1, 2)))
OUTER = (((0, 0),), ((2, 3),))
TAPS = ((0, 0), (1, 1), (2, 2))
FOLD = ((0, 2), (0, 1), (1, 2))


def row_terms(triples_ref, taps_ref, frames, pairs, times):
    total = None
    for f, a in times:
        for b, row in pairs:
            part = triples_ref[f : f + frames, row].reshape(frames * 64, 384)
            term = jnp.dot(part, taps_ref[a * 3 + b], preferred_element_type=jnp.float32)
            total = term if total is None else total + term
    return total


def add_rows(triples_ref, taps_ref, sum_ref, frames, rows, fresh, fold):
    for row in range(2):
        term = row_terms(triples_ref, taps_ref, frames, rows[row], TAPS)
        sum_ref[row] = term if fresh else sum_ref[row] + term

    @pl.when(fold)
    def _():
        for row in range(2):
            sum_ref[row, 0:64, :] += row_terms(triples_ref, taps_ref, 1, rows[row], FOLD)


def interleaved(sum_ref, frames):
    rows = [sum_ref[r, f * 64 : (f + 1) * 64, :] for f in range(frames) for r in range(2)]
    return jnp.concatenate(rows, axis=0)


def edge_kernel(mine_ref, both_ref, beyond_ref, edge_ref, corner_ref):
    core, chip, _, odd = place()
    other_ref = both_ref.at[pl.ds(2 - 2 * core, 2)]
    corner_ref[...] = other_ref[:, odd]
    edge_ref[pl.ds(4 * core, 2)] = beyond_ref[:, odd]
    edge_ref[2:4] = mine_ref[:, odd]
    edge_ref[pl.ds(4 - 4 * core, 2)] = other_ref[:, odd]

    @pl.when((core == 0) & (chip == 0))
    def _():
        edge_ref[0] = mine_ref[0, odd]
        edge_ref[1] = mine_ref[0, odd]


def assemble_kernel(mine_ref, both_ref, beyond_ref, beyond_far_ref, free_ref, src_ref, inner_ref, corner_ref):
    core, chip, end, odd = place()
    src_ref[pl.ds(4 * core, 2)] = beyond_ref[...] + beyond_far_ref[...]
    src_ref[2:4] = mine_ref[...]
    src_ref[pl.ds(4 - 4 * core, 2)] = both_ref[pl.ds(2 - 2 * core, 2)]

    @pl.when((core == 0) & (chip == 0))
    def _():
        src_ref[0] = mine_ref[0]
        src_ref[1] = mine_ref[0]

    inner_ref[...] = src_ref[:, 1 - odd]
    corner_ref[...] = jnp.where(end, free_ref[...], beyond_far_ref[:, odd])


def first_inner_kernel(src_ref, kernel_ref, sum_ref, triples_ref, taps_ref):
    core, chip, _, _ = place()
    fill_inner(src_ref, triples_ref, 6)

    @pl.when(core == 0)
    def _():
        stage_taps(kernel_ref, taps_ref, False)

    @pl.when(core == 1)
    def _():
        stage_taps(kernel_ref, taps_ref, True)

    add_rows(triples_ref, taps_ref, sum_ref, 4, INNER, True, (core == 1) & (chip == 0))


def first_outer_kernel(
    inner_ref, triples_in_ref, taps_ref, far_ref, near_ref, corner_ref, out_ref, triples_ref, outer_ref, sum_ref
):
    core, chip, _, _ = place()
    outer_ref[...] = far_ref[...]
    outer_ref[pl.ds(4 * core, 2)] += corner_ref[...]
    fill_outer(outer_ref, near_ref, triples_ref, 6)
    sum_ref[...] = inner_ref[...]
    add_rows(triples_ref, taps_ref, sum_ref, 4, OUTER, False, (core == 1) & (chip == 0))
    out_ref[...] = interleaved(sum_ref, 4)


def assemble_grad_kernel(act_ref, before_ref, far_ref, src_ref, inner_ref, corner_ref):
    core, _, end, odd = place()

    @pl.when(core == 0)
    def _():
        src_ref[...] = act_ref[...]
        corner_ref[...] = before_ref[:, 0]

    @pl.when(core == 1)
    def _():
        src_ref[0:2] = act_ref[2:4]
        src_ref[2:4] = before_ref[...]
        corner_ref[...] = jnp.where(end, far_ref[2:4], before_ref[:, odd])

    inner_ref[...] = src_ref[:, 1 - odd]


def input_inner_kernel(src_ref, kernel_ref, sum_ref, triples_ref, taps_ref):
    core, chip, _, _ = place()
    fill_inner(src_ref, triples_ref, 4)
    stage_taps(kernel_ref, taps_ref, True)
    add_rows(triples_ref, taps_ref, sum_ref, 2, INNER, True, (core == 0) & (chip == 0))


def input_outer_kernel(
    inner_ref, taps_ref, far_ref, corner_ref, near_ref, cot_ref, triples_in_ref, out_ref, triples_ref, outer_ref,
    sum_ref
):
    core, chip, _, _ = place()
    outer_ref[...] = far_ref[...]

    @pl.when(core == 1)
    def _():
        outer_ref[2:4] = corner_ref[...]

    fill_outer(outer_ref, near_ref, triples_ref, 4)
    sum_ref[...] = inner_ref[...]
    add_rows(triples_ref, taps_ref, sum_ref, 2, OUTER, False, (core == 0) & (chip == 0))
    cot = cot_ref[...].reshape(256, 128).astype(jnp.float32)
    out_ref[...] = (cot + interleaved(sum_ref, 2)).astype(jnp.bfloat16).reshape(out_ref.shape)


def grads_kernel(both_ref, triples_ref, send_ref, act_ref, edge_ref, before_ref, terms_ref):
    core, _, _, odd = place()
    pre_act = both_ref[0:512, :].astype(jnp.bfloat16).astype(jnp.float32)
    back_grad = both_ref[512:1024, :]
    sig = 1.0 / (1.0 + jnp.exp(-pre_act))
    act_grad = (back_grad * (sig * (1.0 + pre_act * (1.0 - sig)))).astype(jnp.bfloat16)
    hidden = (pre_act * sig).astype(jnp.bfloat16)
    act_ref[...] = act_grad.reshape(act_ref.shape)
    edge_ref[0:2] = act_ref[pl.ds(2 * core, 2), odd]
    edge_ref[2:4] = act_ref[pl.ds(2 - 2 * core, 2), odd]

    @pl.when(core == 0)
    def _():
        before_ref[...] = act_ref[0:2]

    @pl.when(core == 1)
    def _():
        before_ref[:, 0] = act_ref[0:2, odd]
        before_ref[:, 1] = act_ref[0:2, odd]

    @pl.when(core == 0)
    def _():
        for a in range(3):
            for b in range(3):
                start = (a * 3 + b) * 384
                terms_ref[start : start + 384, :] = contract_first(stripe(triples_ref, a, 4, b), act_grad)

    @pl.when(core == 1)
    def _():
        for a in range(3):
            for b in range(3):
                part = contract_first(hidden, stripe(triples_ref, a, 4, b))
                for d in range(3):
                    start = ((2 - a) * 9 + (2 - b) * 3 + (2 - d)) * 128
                    terms_ref[start : start + 128, :] = part[:, d * 128 : (d + 1) * 128]

    @pl.when((core == 1) & (lax.axis_index("zh") == 0) & (lax.axis_index("y") == 0))
    def _():
        for f, a in ((0, 2), (0, 1), (1, 2)):
            for b in range(3):
                part = contract_first(hidden[0:128], stripe(triples_ref, f, 1, b))
                for d in range(3):
                    start = ((2 - a) * 9 + (2 - b) * 3 + (2 - d)) * 128
                    terms_ref[start : start + 128, :] += part[:, d * 128 : (d + 1) * 128]

    for y in range(4):
        for x in range(4):
            blocks = []
            for zh in range(2):
                for c in range(2):
                    start = 54 * (((zh * 4 + y) * 2 + c) * 4 + x)
                    blocks.append(terms_ref[start : start + 54, :])
            place0, place1 = PLANES[0].index(y * 4 + x), PLANES[1].index(16 + y * 4 + x)
            rank = jnp.where(lax.axis_index("zh") == 0, place0, place1)
            send_ref[rank] = jnp.concatenate(blocks, axis=0).astype(jnp.bfloat16)


def plane_sum_kernel(got_ref, send_ref, sum_ref):
    total = got_ref[0].astype(jnp.float32)
    for k in range(1, 16):
        total = total + got_ref[k].astype(jnp.float32)
    sum_ref[0:216] = total
    sum_ref[216:224] = jnp.zeros((8, 128), jnp.float32)
    lane = lax.broadcasted_iota(jnp.int32, (8, 128), 1)
    for zh in range(2):
        for zl in range(8):
            pieces = []
            for c in range(2):
                value = (zh * 2 + c) * 54 * 128 + zl * 864
                row, shift = value // 128, value % 128
                piece = sum_ref[row : row + 8, :]
                if shift:
                    after = sum_ref[row + 1 : row + 9, :]
                    piece = jnp.where(
                        lane < 128 - shift,
                        pltpu.roll(piece, 128 - shift, 1),
                        pltpu.roll(after, 128 - shift, 1),
                    )
                pieces.append(piece)
            send_ref[LINES[0].index(zh * 8 + zl)] = jnp.concatenate(pieces, axis=0).astype(jnp.bfloat16)


def line_sum_kernel(got_ref, sum_ref):
    total = got_ref[0].astype(jnp.float32)
    for k in range(1, 16):
        total = total + got_ref[k].astype(jnp.float32)
    sum_ref[...] = total


def place_kernel(scale, shares_ref, out_ref):
    for k in range(2):
        start = pl.multiple_of(16 * k + 8 * lax.axis_index("c"), 8)
        share = shares_ref[pl.ds(start, 8), :] * scale
        for r in range(7):
            width = min(128, 864 - 128 * r)
            out_ref[k : k + 1, 128 * r : 128 * r + width] = share[r : r + 1, :width]


def call(kernel, out_shape, *args, scratch=(), flops=0, aliases=None):
    many = isinstance(out_shape, (list, tuple))
    return pl.pallas_call(
        kernel,
        out_shape=out_shape,
        in_specs=[VMEM] * len(args),
        out_specs=[VMEM] * len(out_shape) if many else VMEM,
        scratch_shapes=scratch,
        input_output_aliases=aliases or {},
        compiler_params=pltpu.CompilerParams(vmem_limit_bytes=32 * 1024 * 1024),
        cost_estimate=pl.CostEstimate(flops=flops, bytes_accessed=0, transcendentals=0) if flops else None,
    )(*args)


def shaped(shape, dtype):
    return jax.ShapeDtypeStruct(shape, dtype)


def per_device(video_clip, first_kernel, second_kernel, cotangent):
    bf16, f32 = jnp.bfloat16, jnp.float32
    core = lax.axis_index("c")
    everywhere = TM + ROWS
    first_kernel, second_kernel = first_kernel.reshape(3456, 128), second_kernel.reshape(3456, 128)
    given = jnp.where(core == 0, cotangent, video_clip)
    mine = jnp.where(core == 0, video_clip, cotangent)
    given, mine = lax.optimization_barrier((given, mine))
    both = lax.all_gather(given, "c", tiled=True)
    both, given = lax.optimization_barrier((both, given))
    beyond_far = lax.ppermute(given, TM, BEYOND_FAR)
    beyond = lax.ppermute(given, TM, BEYOND)
    edge, corner = call(
        edge_kernel,
        (shaped((6, 64, 128), bf16), shaped((2, 64, 128), bf16)),
        mine, both, beyond,
    )
    far = lax.ppermute(edge, ROWS, FAR_ROWS)
    free = lax.ppermute(corner, everywhere, CORNER_FREE)
    source, inner, corner = call(
        assemble_kernel,
        (shaped((6, 2, 64, 128), bf16), shaped((6, 64, 128), bf16), shaped((2, 64, 128), bf16)),
        mine, both, beyond, beyond_far, free,
    )
    inner, corner, second = lax.optimization_barrier((inner, corner, second_kernel))
    kernel = jnp.where(core == 0, first_kernel, second)
    near = lax.ppermute(inner, ROWS, NEAR_ROWS)
    corner = lax.ppermute(corner, everywhere, CORNER_ROWS)
    inner, triples, taps = call(
        first_inner_kernel,
        (shaped((2, 256, 128), f32), shaped((6, 4, 64, 384), bf16), shaped((9, 384, 128), bf16)),
        source, kernel,
        flops=300_000_000,
    )
    own, triples = call(
        first_outer_kernel,
        (shaped((512, 128), f32), shaped((6, 4, 64, 384), bf16)),
        inner, triples, taps, far, near, corner,
        scratch=[pltpu.VMEM((6, 64, 128), bf16), pltpu.VMEM((2, 256, 128), f32)],
        aliases={1: 1},
    )
    both = lax.all_gather(own, "c", tiled=True)
    send, act_grad, edge, before = call(
        grads_kernel,
        (
            shaped((16, 216, 128), bf16), shaped((4, 2, 64, 128), bf16),
            shaped((4, 64, 128), bf16), shaped((2, 2, 64, 128), bf16),
        ),
        both, triples,
        scratch=[pltpu.VMEM((3456, 128), f32)],
    )
    got = lax.all_to_all(send, ("zh", "y", "x"), 0, 0, axis_index_groups=PLANES, tiled=True)
    before = lax.ppermute(before, everywhere, BEFORE)
    far = lax.ppermute(edge, ROWS, FAR_ROWS)
    send = call(plane_sum_kernel, shaped((16, 16, 128), bf16), got, scratch=[pltpu.VMEM((224, 128), f32)])
    got = lax.all_to_all(send, ("zh", "zl"), 0, 0, axis_index_groups=LINES, tiled=True)
    _, before, far = lax.optimization_barrier((send, before, far))
    source, inner, corner = call(
        assemble_grad_kernel,
        (shaped((4, 2, 64, 128), bf16), shaped((4, 64, 128), bf16), shaped((2, 64, 128), bf16)),
        act_grad, before, far,
    )
    near = lax.ppermute(inner, ROWS, NEAR_ROWS)
    corner = lax.ppermute(corner, everywhere, CORNER_GRAD)
    inner, triples, taps = call(
        input_inner_kernel,
        (shaped((2, 128, 128), f32), shaped((4, 4, 64, 384), bf16), shaped((9, 384, 128), bf16)),
        source, first_kernel,
        flops=150_000_000,
    )
    input_grad, _ = call(
        input_outer_kernel,
        (shaped((2, 2, 64, 128), bf16), shaped((4, 4, 64, 384), bf16)),
        inner, taps, far, corner, near, cotangent, triples,
        scratch=[pltpu.VMEM((4, 64, 128), bf16), pltpu.VMEM((2, 128, 128), f32)],
        aliases={6: 1},
        flops=1_600_000_000,
    )
    got, input_grad = lax.optimization_barrier((got, input_grad))
    scale = 1.0 / math.sqrt(131072)
    shares = call(line_sum_kernel, shaped((16, 128), f32), got)
    shares = lax.all_gather(shares, "c", tiled=True)
    weight_grads = call(lambda *refs: place_kernel(scale, *refs), shaped((2, 864), f32), shares)
    return input_grad, weight_grads


def solution(mesh):
    fine = Mesh(np.asarray(mesh.devices).reshape(2, 4, 2, 4, 8), TM + ROWS)
    return jax.shard_map(
        per_device,
        mesh=fine,
        in_specs=(P(TM, ROWS, None, None), P(), P(), P(TM, ROWS, None, None)),
        out_specs=(P(TM, ROWS, None, None), P(None, TM + ROWS)),
        check_vma=False,
    )
```

```python
import math

import jax
import jax.numpy as jnp
import numpy as np
from jax import lax
from jax.experimental import pallas as pl
from jax.experimental.pallas import tpu as pltpu
from jax.sharding import Mesh, PartitionSpec as P

TM = ("zh", "y", "c")
ROWS = ("x", "zl")
VMEM = pl.BlockSpec(memory_space=pltpu.VMEM)


NEAR_ROWS = [(r, r ^ 1) for r in range(32)]
FAR_ROWS = [(r, r + 1) for r in range(1, 31, 2)] + [(r + 1, r) for r in range(1, 31, 2)]
ENDS = [(r, q) for r, q in FAR_ROWS if r // 8 != q // 8]
MIDDLES = [(r, q) for r, q in FAR_ROWS if r // 8 == q // 8]
ENDS_OF = [r for r, _ in ENDS]


PLANES = [
    [half * 16 + (2 - y) % 4 * 4 + (2 - x) % 4 for y in range(4) for x in range(4)] for half in range(2)
]


LINES = [[(12 + z) % 16 for z in range(16)]]


def device(chip, core, slab):
    return (2 * chip + core) * 32 + slab


BEYOND = [pair for k in (0, 1, 2, 4, 5, 6) for pair in ((2 * k + 1, 2 * k + 2), (2 * k + 2, 2 * k + 1))]
BEYOND_FAR = [(7, 8), (8, 7)]
CORNER_FREE = [(device(3, 0, r), device(4, 1, q)) for r, q in ENDS] + [
    (device(4, 1, r), device(3, 0, q)) for r, q in ENDS
]
CORNER_ROWS = [(device(k, c, r), device(k, c, q)) for k, c in ((3, 1), (4, 0)) for r, q in MIDDLES] + [
    (device(k, c, r), device(k, 1 - c, r)) for k, c in ((3, 0), (4, 1)) for r in ENDS_OF
]
BEFORE = [(device(k + 1, 0, r), device(k, 1, r)) for k in range(7) for r in range(32)] + [
    (device(4, 1, r), device(3, 0, q)) for r, q in ENDS
]
CORNER_GRAD = (
    [(device(k, 1, r), device(k, 1, q)) for k in range(7) for r, q in MIDDLES]
    + [(device(k + 1, 1, r), device(k, 1, r)) for k in (0, 1, 2, 4, 5, 6) for r in ENDS_OF]
    + [(device(3, 0, r), device(3, 1, r)) for r in ENDS_OF]
)


def place():
    core = lax.axis_index("c")
    chip = lax.axis_index("zh") * 4 + lax.axis_index("y")
    odd = lax.axis_index("zl") & 1
    end = (lax.axis_index("zl") == 0) | (lax.axis_index("zl") == 7)
    return core, chip, end, odd


def contract_first(lhs, rhs):
    return lax.dot_general(lhs, rhs, (((0,), (0,)), ((), ())), preferred_element_type=jnp.float32)


def side_by_side(cells):
    columns, chans = cells.shape
    col = lax.broadcasted_iota(jnp.int32, (columns, chans), 0)
    wide = cells.astype(jnp.float32)
    before = jnp.where(col == 0, 0.0, pltpu.roll(wide, 1, 0)).astype(cells.dtype)
    after = jnp.where(col == columns - 1, 0.0, pltpu.roll(wide, columns - 1, 0)).astype(cells.dtype)
    return jnp.concatenate([before, cells, after], axis=1)


def fill_inner(src_ref, triples_ref, frames):
    for f in range(frames):
        for r in range(2):
            triples_ref[f, r + 1] = side_by_side(src_ref[f, r])


def fill_outer(far_ref, near_ref, triples_ref, frames):
    odd = place()[3]
    for f in range(frames):
        triples_ref[f, 0] = side_by_side(jnp.where(odd == 0, far_ref[f], near_ref[f]))
        triples_ref[f, 3] = side_by_side(jnp.where(odd == 1, far_ref[f], near_ref[f]))


def stripe(triples_ref, f, count, b):
    part = triples_ref[f : f + count, b : b + 2]
    return part.reshape(count * 2 * part.shape[2], part.shape[3])


def turned(kernel_ref, a, b):
    starts = [((2 - a) * 9 + (2 - b) * 3 + (2 - d)) * 128 for d in range(3)]
    return jnp.concatenate([kernel_ref[start : start + 128, :] for start in starts], axis=1)


def stage_taps(kernel_ref, taps_ref, back):
    for a in range(3):
        for b in range(3):
            if back:
                taps_ref[a * 3 + b] = turned(kernel_ref, a, b).T
            else:
                taps_ref[a * 3 + b] = kernel_ref[(a * 3 + b) * 384 : (a * 3 + b + 1) * 384, :]


INNER = (((1, 1), (2, 2)), ((0, 1), (1, 2)))
OUTER = (((0, 0),), ((2, 3),))
TAPS = ((0, 0), (1, 1), (2, 2))
FOLD = ((0, 2), (0, 1), (1, 2))


def row_terms(triples_ref, taps_ref, frames, pairs, times):
    total = None
    for f, a in times:
        for b, row in pairs:
            part = triples_ref[f : f + frames, row].reshape(frames * 64, 384)
            term = jnp.dot(part, taps_ref[a * 3 + b], preferred_element_type=jnp.float32)
            total = term if total is None else total + term
    return total


def add_rows(triples_ref, taps_ref, sum_ref, frames, rows, fresh, fold):
    for row in range(2):
        term = row_terms(triples_ref, taps_ref, frames, rows[row], TAPS)
        sum_ref[row] = term if fresh else sum_ref[row] + term

    @pl.when(fold)
    def _():
        for row in range(2):
            sum_ref[row, 0:64, :] += row_terms(triples_ref, taps_ref, 1, rows[row], FOLD)


def interleaved(sum_ref, frames):
    rows = [sum_ref[r, f * 64 : (f + 1) * 64, :] for f in range(frames) for r in range(2)]
    return jnp.concatenate(rows, axis=0)


def edge_kernel(mine_ref, both_ref, beyond_ref, edge_ref, corner_ref):
    core, chip, _, odd = place()
    other_ref = both_ref.at[pl.ds(2 - 2 * core, 2)]
    corner_ref[...] = other_ref[:, odd]
    edge_ref[pl.ds(4 * core, 2)] = beyond_ref[:, odd]
    edge_ref[2:4] = mine_ref[:, odd]
    edge_ref[pl.ds(4 - 4 * core, 2)] = other_ref[:, odd]

    @pl.when((core == 0) & (chip == 0))
    def _():
        edge_ref[0] = mine_ref[0, odd]
        edge_ref[1] = mine_ref[0, odd]


def assemble_kernel(mine_ref, both_ref, beyond_ref, beyond_far_ref, free_ref, src_ref, inner_ref, corner_ref):
    core, chip, end, odd = place()
    src_ref[pl.ds(4 * core, 2)] = beyond_ref[...] + beyond_far_ref[...]
    src_ref[2:4] = mine_ref[...]
    src_ref[pl.ds(4 - 4 * core, 2)] = both_ref[pl.ds(2 - 2 * core, 2)]

    @pl.when((core == 0) & (chip == 0))
    def _():
        src_ref[0] = mine_ref[0]
        src_ref[1] = mine_ref[0]

    inner_ref[...] = src_ref[:, 1 - odd]
    corner_ref[...] = jnp.where(end, free_ref[...], beyond_far_ref[:, odd])


def first_inner_kernel(src_ref, kernel_ref, sum_ref, triples_ref, taps_ref):
    core, chip, _, _ = place()
    fill_inner(src_ref, triples_ref, 6)

    @pl.when(core == 0)
    def _():
        stage_taps(kernel_ref, taps_ref, False)

    @pl.when(core == 1)
    def _():
        stage_taps(kernel_ref, taps_ref, True)

    add_rows(triples_ref, taps_ref, sum_ref, 4, INNER, True, (core == 1) & (chip == 0))


def first_outer_kernel(
    inner_ref, triples_in_ref, taps_ref, far_ref, near_ref, corner_ref, out_ref, triples_ref, outer_ref, sum_ref
):
    core, chip, _, _ = place()
    outer_ref[...] = far_ref[...]
    outer_ref[pl.ds(4 * core, 2)] += corner_ref[...]
    fill_outer(outer_ref, near_ref, triples_ref, 6)
    sum_ref[...] = inner_ref[...]
    add_rows(triples_ref, taps_ref, sum_ref, 4, OUTER, False, (core == 1) & (chip == 0))
    out_ref[...] = interleaved(sum_ref, 4)


def assemble_grad_kernel(act_ref, before_ref, far_ref, src_ref, inner_ref, corner_ref):
    core, _, end, odd = place()

    @pl.when(core == 0)
    def _():
        src_ref[...] = act_ref[...]
        corner_ref[...] = before_ref[:, 0]

    @pl.when(core == 1)
    def _():
        src_ref[0:2] = act_ref[2:4]
        src_ref[2:4] = before_ref[...]
        corner_ref[...] = jnp.where(end, far_ref[2:4], before_ref[:, odd])

    inner_ref[...] = src_ref[:, 1 - odd]


def input_inner_kernel(src_ref, kernel_ref, sum_ref, triples_ref, taps_ref):
    core, chip, _, _ = place()
    fill_inner(src_ref, triples_ref, 4)
    stage_taps(kernel_ref, taps_ref, True)
    add_rows(triples_ref, taps_ref, sum_ref, 2, INNER, True, (core == 0) & (chip == 0))


def input_outer_kernel(
    inner_ref, taps_ref, far_ref, corner_ref, near_ref, cot_ref, triples_in_ref, out_ref, triples_ref, outer_ref,
    sum_ref
):
    core, chip, _, _ = place()
    outer_ref[...] = far_ref[...]

    @pl.when(core == 1)
    def _():
        outer_ref[2:4] = corner_ref[...]

    fill_outer(outer_ref, near_ref, triples_ref, 4)
    sum_ref[...] = inner_ref[...]
    add_rows(triples_ref, taps_ref, sum_ref, 2, OUTER, False, (core == 0) & (chip == 0))
    cot = cot_ref[...].reshape(256, 128).astype(jnp.float32)
    out_ref[...] = (cot + interleaved(sum_ref, 2)).astype(jnp.bfloat16).reshape(out_ref.shape)


def grads_kernel(both_ref, triples_ref, send_ref, act_ref, edge_ref, before_ref, terms_ref):
    core, _, _, odd = place()
    pre_act = both_ref[0:512, :].astype(jnp.bfloat16).astype(jnp.float32)
    back_grad = both_ref[512:1024, :]
    sig = 1.0 / (1.0 + jnp.exp(-pre_act))
    act_grad = (back_grad * (sig * (1.0 + pre_act * (1.0 - sig)))).astype(jnp.bfloat16)
    hidden = (pre_act * sig).astype(jnp.bfloat16)
    act_ref[...] = act_grad.reshape(act_ref.shape)
    edge_ref[0:2] = act_ref[pl.ds(2 * core, 2), odd]
    edge_ref[2:4] = act_ref[pl.ds(2 - 2 * core, 2), odd]

    @pl.when(core == 0)
    def _():
        before_ref[...] = act_ref[0:2]

    @pl.when(core == 1)
    def _():
        before_ref[:, 0] = act_ref[0:2, odd]
        before_ref[:, 1] = act_ref[0:2, odd]

    @pl.when(core == 0)
    def _():
        for a in range(3):
            for b in range(3):
                start = (a * 3 + b) * 384
                terms_ref[start : start + 384, :] = contract_first(stripe(triples_ref, a, 4, b), act_grad)

    @pl.when(core == 1)
    def _():
        for a in range(3):
            for b in range(3):
                part = contract_first(hidden, stripe(triples_ref, a, 4, b))
                for d in range(3):
                    start = ((2 - a) * 9 + (2 - b) * 3 + (2 - d)) * 128
                    terms_ref[start : start + 128, :] = part[:, d * 128 : (d + 1) * 128]

    @pl.when((core == 1) & (lax.axis_index("zh") == 0) & (lax.axis_index("y") == 0))
    def _():
        for f, a in ((0, 2), (0, 1), (1, 2)):
            for b in range(3):
                part = contract_first(hidden[0:128], stripe(triples_ref, f, 1, b))
                for d in range(3):
                    start = ((2 - a) * 9 + (2 - b) * 3 + (2 - d)) * 128
                    terms_ref[start : start + 128, :] += part[:, d * 128 : (d + 1) * 128]

    for y in range(4):
        for x in range(4):
            blocks = []
            for zh in range(2):
                for c in range(2):
                    start = 54 * (((zh * 4 + y) * 2 + c) * 4 + x)
                    blocks.append(terms_ref[start : start + 54, :])
            place0, place1 = PLANES[0].index(y * 4 + x), PLANES[1].index(16 + y * 4 + x)
            rank = jnp.where(lax.axis_index("zh") == 0, place0, place1)
            send_ref[rank] = jnp.concatenate(blocks, axis=0).astype(jnp.bfloat16)


def plane_sum_kernel(got_ref, send_ref, sum_ref):
    total = got_ref[0].astype(jnp.float32)
    for k in range(1, 16):
        total = total + got_ref[k].astype(jnp.float32)
    sum_ref[0:216] = total
    sum_ref[216:224] = jnp.zeros((8, 128), jnp.float32)
    lane = lax.broadcasted_iota(jnp.int32, (8, 128), 1)
    for zh in range(2):
        for zl in range(8):
            pieces = []
            for c in range(2):
                value = (zh * 2 + c) * 54 * 128 + zl * 864
                row, shift = value // 128, value % 128
                piece = sum_ref[row : row + 8, :]
                if shift:
                    after = sum_ref[row + 1 : row + 9, :]
                    piece = jnp.where(
                        lane < 128 - shift,
                        pltpu.roll(piece, 128 - shift, 1),
                        pltpu.roll(after, 128 - shift, 1),
                    )
                pieces.append(piece)
            send_ref[LINES[0].index(zh * 8 + zl)] = jnp.concatenate(pieces, axis=0).astype(jnp.bfloat16)


def line_sum_kernel(got_ref, sum_ref):
    total = got_ref[0].astype(jnp.float32)
    for k in range(1, 16):
        total = total + got_ref[k].astype(jnp.float32)
    sum_ref[...] = total


def place_kernel(scale, shares_ref, out_ref):
    for k in range(2):
        start = pl.multiple_of(16 * k + 8 * lax.axis_index("c"), 8)
        share = shares_ref[pl.ds(start, 8), :] * scale
        for r in range(7):
            width = min(128, 864 - 128 * r)
            out_ref[k : k + 1, 128 * r : 128 * r + width] = share[r : r + 1, :width]


def call(kernel, out_shape, *args, scratch=(), flops=0, aliases=None):
    many = isinstance(out_shape, (list, tuple))
    return pl.pallas_call(
        kernel,
        out_shape=out_shape,
        in_specs=[VMEM] * len(args),
        out_specs=[VMEM] * len(out_shape) if many else VMEM,
        scratch_shapes=scratch,
        input_output_aliases=aliases or {},
        compiler_params=pltpu.CompilerParams(vmem_limit_bytes=32 * 1024 * 1024),
        cost_estimate=pl.CostEstimate(flops=flops, bytes_accessed=0, transcendentals=0) if flops else None,
    )(*args)


def shaped(shape, dtype):
    return jax.ShapeDtypeStruct(shape, dtype)


def per_device(video_clip, first_kernel, second_kernel, cotangent):
    bf16, f32 = jnp.bfloat16, jnp.float32
    core = lax.axis_index("c")
    everywhere = TM + ROWS
    first_kernel, second_kernel = first_kernel.reshape(3456, 128), second_kernel.reshape(3456, 128)
    given = jnp.where(core == 0, cotangent, video_clip)
    mine = jnp.where(core == 0, video_clip, cotangent)
    given, mine = lax.optimization_barrier((given, mine))
    both = lax.all_gather(given, "c", tiled=True)
    both, given = lax.optimization_barrier((both, given))
    beyond_far = lax.ppermute(given, TM, BEYOND_FAR)
    beyond = lax.ppermute(given, TM, BEYOND)
    edge, corner = call(
        edge_kernel,
        (shaped((6, 64, 128), bf16), shaped((2, 64, 128), bf16)),
        mine, both, beyond,
    )
    far = lax.ppermute(edge, ROWS, FAR_ROWS)
    free = lax.ppermute(corner, everywhere, CORNER_FREE)
    source, inner, corner = call(
        assemble_kernel,
        (shaped((6, 2, 64, 128), bf16), shaped((6, 64, 128), bf16), shaped((2, 64, 128), bf16)),
        mine, both, beyond, beyond_far, free,
    )
    inner, corner, second = lax.optimization_barrier((inner, corner, second_kernel))
    kernel = jnp.where(core == 0, first_kernel, second)
    near = lax.ppermute(inner, ROWS, NEAR_ROWS)
    corner = lax.ppermute(corner, everywhere, CORNER_ROWS)
    inner, triples, taps = call(
        first_inner_kernel,
        (shaped((2, 256, 128), f32), shaped((6, 4, 64, 384), bf16), shaped((9, 384, 128), bf16)),
        source, kernel,
        flops=300_000_000,
    )
    own, triples = call(
        first_outer_kernel,
        (shaped((512, 128), f32), shaped((6, 4, 64, 384), bf16)),
        inner, triples, taps, far, near, corner,
        scratch=[pltpu.VMEM((6, 64, 128), bf16), pltpu.VMEM((2, 256, 128), f32)],
        aliases={1: 1},
    )
    both = lax.all_gather(own, "c", tiled=True)
    send, act_grad, edge, before = call(
        grads_kernel,
        (
            shaped((16, 216, 128), bf16), shaped((4, 2, 64, 128), bf16),
            shaped((4, 64, 128), bf16), shaped((2, 2, 64, 128), bf16),
        ),
        both, triples,
        scratch=[pltpu.VMEM((3456, 128), f32)],
    )
    got = lax.all_to_all(send, ("zh", "y", "x"), 0, 0, axis_index_groups=PLANES, tiled=True)
    before = lax.ppermute(before, everywhere, BEFORE)
    far = lax.ppermute(edge, ROWS, FAR_ROWS)
    send = call(plane_sum_kernel, shaped((16, 16, 128), bf16), got, scratch=[pltpu.VMEM((224, 128), f32)])
    got = lax.all_to_all(send, ("zh", "zl"), 0, 0, axis_index_groups=LINES, tiled=True)
    _, before, far = lax.optimization_barrier((send, before, far))
    source, inner, corner = call(
        assemble_grad_kernel,
        (shaped((4, 2, 64, 128), bf16), shaped((4, 64, 128), bf16), shaped((2, 64, 128), bf16)),
        act_grad, before, far,
    )
    near = lax.ppermute(inner, ROWS, NEAR_ROWS)
    corner = lax.ppermute(corner, everywhere, CORNER_GRAD)
    inner, triples, taps = call(
        input_inner_kernel,
        (shaped((2, 128, 128), f32), shaped((4, 4, 64, 384), bf16), shaped((9, 384, 128), bf16)),
        source, first_kernel,
        flops=150_000_000,
    )
    input_grad, _ = call(
        input_outer_kernel,
        (shaped((2, 2, 64, 128), bf16), shaped((4, 4, 64, 384), bf16)),
        inner, taps, far, corner, near, cotangent, triples,
        scratch=[pltpu.VMEM((4, 64, 128), bf16), pltpu.VMEM((2, 128, 128), f32)],
        aliases={6: 1},
        flops=1_600_000_000,
    )
    got, input_grad = lax.optimization_barrier((got, input_grad))
    scale = 1.0 / math.sqrt(131072)
    shares = call(line_sum_kernel, shaped((16, 128), f32), got)
    shares = lax.all_gather(shares, "c", tiled=True)
    weight_grads = call(lambda *refs: place_kernel(scale, *refs), shaped((2, 864), f32), shares)
    return input_grad, weight_grads


def solution(mesh):
    fine = Mesh(np.asarray(mesh.devices).reshape(2, 4, 2, 4, 8), TM + ROWS)
    return jax.shard_map(
        per_device,
        mesh=fine,
        in_specs=(P(TM, ROWS, None, None), P(), P(), P(TM, ROWS, None, None)),
        out_specs=(P(TM, ROWS, None, None), P(None, TM + ROWS)),
        check_vma=False,
    )
```

```python
import math

import jax
import jax.numpy as jnp
import numpy as np
from jax import lax
from jax.experimental import pallas as pl
from jax.experimental.pallas import tpu as pltpu
from jax.sharding import Mesh, PartitionSpec as P

TM = ("zh", "y", "c")
ROWS = ("x", "zl")
VMEM = pl.BlockSpec(memory_space=pltpu.VMEM)


NEAR_ROWS = [(r, r ^ 1) for r in range(32)]
FAR_ROWS = [(r, r + 1) for r in range(1, 31, 2)] + [(r + 1, r) for r in range(1, 31, 2)]
ENDS = [(r, q) for r, q in FAR_ROWS if r // 8 != q // 8]
MIDDLES = [(r, q) for r, q in FAR_ROWS if r // 8 == q // 8]
ENDS_OF = [r for r, _ in ENDS]


PLANES = [
    [half * 16 + (y + 2) % 4 * 4 + (x + 2) % 4 for y in range(4) for x in range(4)] for half in range(2)
]


LINES = [[(12 + z) % 16 for z in range(16)]]


def device(chip, core, slab):
    return (2 * chip + core) * 32 + slab


BEYOND = [pair for k in (0, 1, 2, 4, 5, 6) for pair in ((2 * k + 1, 2 * k + 2), (2 * k + 2, 2 * k + 1))]
BEYOND_FAR = [(7, 8), (8, 7)]
CORNER_FREE = [(device(3, 0, r), device(4, 1, q)) for r, q in ENDS] + [
    (device(4, 1, r), device(3, 0, q)) for r, q in ENDS
]
CORNER_ROWS = [(device(k, c, r), device(k, c, q)) for k, c in ((3, 1), (4, 0)) for r, q in MIDDLES] + [
    (device(k, c, r), device(k, 1 - c, r)) for k, c in ((3, 0), (4, 1)) for r in ENDS_OF
]
BEFORE = [(device(k + 1, 0, r), device(k, 1, r)) for k in range(7) for r in range(32)] + [
    (device(4, 1, r), device(3, 0, q)) for r, q in ENDS
]
CORNER_GRAD = (
    [(device(k, 1, r), device(k, 1, q)) for k in range(7) for r, q in MIDDLES]
    + [(device(k + 1, 1, r), device(k, 1, r)) for k in (0, 1, 2, 4, 5, 6) for r in ENDS_OF]
    + [(device(3, 0, r), device(3, 1, r)) for r in ENDS_OF]
)


def place():
    core = lax.axis_index("c")
    chip = lax.axis_index("zh") * 4 + lax.axis_index("y")
    odd = lax.axis_index("zl") & 1
    end = (lax.axis_index("zl") == 0) | (lax.axis_index("zl") == 7)
    return core, chip, end, odd


def contract_first(lhs, rhs):
    return lax.dot_general(lhs, rhs, (((0,), (0,)), ((), ())), preferred_element_type=jnp.float32)


def side_by_side(cells):
    columns, chans = cells.shape
    col = lax.broadcasted_iota(jnp.int32, (columns, chans), 0)
    wide = cells.astype(jnp.float32)
    before = jnp.where(col == 0, 0.0, pltpu.roll(wide, 1, 0)).astype(cells.dtype)
    after = jnp.where(col == columns - 1, 0.0, pltpu.roll(wide, columns - 1, 0)).astype(cells.dtype)
    return jnp.concatenate([before, cells, after], axis=1)


def fill_inner(src_ref, triples_ref, frames):
    for f in range(frames):
        for r in range(2):
            triples_ref[f, r + 1] = side_by_side(src_ref[f, r])


def fill_outer(far_ref, near_ref, triples_ref, frames):
    odd = place()[3]
    for f in range(frames):
        triples_ref[f, 0] = side_by_side(jnp.where(odd == 0, far_ref[f], near_ref[f]))
        triples_ref[f, 3] = side_by_side(jnp.where(odd == 1, far_ref[f], near_ref[f]))


def stripe(triples_ref, f, count, b):
    part = triples_ref[f : f + count, b : b + 2]
    return part.reshape(count * 2 * part.shape[2], part.shape[3])


def turned(kernel_ref, a, b):
    starts = [((2 - a) * 9 + (2 - b) * 3 + (2 - d)) * 128 for d in range(3)]
    return jnp.concatenate([kernel_ref[start : start + 128, :] for start in starts], axis=1)


def stage_taps(kernel_ref, taps_ref, back):
    for a in range(3):
        for b in range(3):
            if back:
                taps_ref[a * 3 + b] = turned(kernel_ref, a, b).T
            else:
                taps_ref[a * 3 + b] = kernel_ref[(a * 3 + b) * 384 : (a * 3 + b + 1) * 384, :]


INNER = (((1, 1), (2, 2)), ((0, 1), (1, 2)))
OUTER = (((0, 0),), ((2, 3),))
TAPS = ((0, 0), (1, 1), (2, 2))
FOLD = ((0, 2), (0, 1), (1, 2))


def row_terms(triples_ref, taps_ref, frames, pairs, times):
    total = None
    for f, a in times:
        for b, row in pairs:
            part = triples_ref[f : f + frames, row].reshape(frames * 64, 384)
            term = jnp.dot(part, taps_ref[a * 3 + b], preferred_element_type=jnp.float32)
            total = term if total is None else total + term
    return total


def add_rows(triples_ref, taps_ref, sum_ref, frames, rows, fresh, fold):
    for row in range(2):
        term = row_terms(triples_ref, taps_ref, frames, rows[row], TAPS)
        sum_ref[row] = term if fresh else sum_ref[row] + term

    @pl.when(fold)
    def _():
        for row in range(2):
            sum_ref[row, 0:64, :] += row_terms(triples_ref, taps_ref, 1, rows[row], FOLD)


def interleaved(sum_ref, frames):
    rows = [sum_ref[r, f * 64 : (f + 1) * 64, :] for f in range(frames) for r in range(2)]
    return jnp.concatenate(rows, axis=0)


def edge_kernel(mine_ref, both_ref, beyond_ref, edge_ref, corner_ref):
    core, chip, _, odd = place()
    other_ref = both_ref.at[pl.ds(2 - 2 * core, 2)]
    corner_ref[...] = other_ref[:, odd]
    edge_ref[pl.ds(4 * core, 2)] = beyond_ref[:, odd]
    edge_ref[2:4] = mine_ref[:, odd]
    edge_ref[pl.ds(4 - 4 * core, 2)] = other_ref[:, odd]

    @pl.when((core == 0) & (chip == 0))
    def _():
        edge_ref[0] = mine_ref[0, odd]
        edge_ref[1] = mine_ref[0, odd]


def assemble_kernel(mine_ref, both_ref, beyond_ref, beyond_far_ref, free_ref, src_ref, inner_ref, corner_ref):
    core, chip, end, odd = place()
    src_ref[pl.ds(4 * core, 2)] = beyond_ref[...] + beyond_far_ref[...]
    src_ref[2:4] = mine_ref[...]
    src_ref[pl.ds(4 - 4 * core, 2)] = both_ref[pl.ds(2 - 2 * core, 2)]

    @pl.when((core == 0) & (chip == 0))
    def _():
        src_ref[0] = mine_ref[0]
        src_ref[1] = mine_ref[0]

    inner_ref[...] = src_ref[:, 1 - odd]
    corner_ref[...] = jnp.where(end, free_ref[...], beyond_far_ref[:, odd])


def first_inner_kernel(src_ref, kernel_ref, sum_ref, triples_ref, taps_ref):
    core, chip, _, _ = place()
    fill_inner(src_ref, triples_ref, 6)

    @pl.when(core == 0)
    def _():
        stage_taps(kernel_ref, taps_ref, False)

    @pl.when(core == 1)
    def _():
        stage_taps(kernel_ref, taps_ref, True)

    add_rows(triples_ref, taps_ref, sum_ref, 4, INNER, True, (core == 1) & (chip == 0))


def first_outer_kernel(
    inner_ref, triples_in_ref, taps_ref, far_ref, near_ref, corner_ref, out_ref, triples_ref, outer_ref, sum_ref
):
    core, chip, _, _ = place()
    outer_ref[...] = far_ref[...]
    outer_ref[pl.ds(4 * core, 2)] += corner_ref[...]
    fill_outer(outer_ref, near_ref, triples_ref, 6)
    sum_ref[...] = inner_ref[...]
    add_rows(triples_ref, taps_ref, sum_ref, 4, OUTER, False, (core == 1) & (chip == 0))
    out_ref[...] = interleaved(sum_ref, 4)


def assemble_grad_kernel(act_ref, before_ref, far_ref, src_ref, inner_ref, corner_ref):
    core, _, end, odd = place()

    @pl.when(core == 0)
    def _():
        src_ref[...] = act_ref[...]
        corner_ref[...] = before_ref[:, 0]

    @pl.when(core == 1)
    def _():
        src_ref[0:2] = act_ref[2:4]
        src_ref[2:4] = before_ref[...]
        corner_ref[...] = jnp.where(end, far_ref[2:4], before_ref[:, odd])

    inner_ref[...] = src_ref[:, 1 - odd]


def input_inner_kernel(src_ref, kernel_ref, sum_ref, triples_ref, taps_ref):
    core, chip, _, _ = place()
    fill_inner(src_ref, triples_ref, 4)
    stage_taps(kernel_ref, taps_ref, True)
    add_rows(triples_ref, taps_ref, sum_ref, 2, INNER, True, (core == 0) & (chip == 0))


def input_outer_kernel(
    inner_ref, taps_ref, far_ref, corner_ref, near_ref, cot_ref, triples_in_ref, out_ref, triples_ref, outer_ref,
    sum_ref
):
    core, chip, _, _ = place()
    outer_ref[...] = far_ref[...]

    @pl.when(core == 1)
    def _():
        outer_ref[2:4] = corner_ref[...]

    fill_outer(outer_ref, near_ref, triples_ref, 4)
    sum_ref[...] = inner_ref[...]
    add_rows(triples_ref, taps_ref, sum_ref, 2, OUTER, False, (core == 0) & (chip == 0))
    cot = cot_ref[...].reshape(256, 128).astype(jnp.float32)
    out_ref[...] = (cot + interleaved(sum_ref, 2)).astype(jnp.bfloat16).reshape(out_ref.shape)


def grads_kernel(both_ref, triples_ref, send_ref, act_ref, edge_ref, before_ref, terms_ref):
    core, _, _, odd = place()
    pre_act = both_ref[0:512, :].astype(jnp.bfloat16).astype(jnp.float32)
    back_grad = both_ref[512:1024, :]
    sig = 1.0 / (1.0 + jnp.exp(-pre_act))
    act_grad = (back_grad * (sig * (1.0 + pre_act * (1.0 - sig)))).astype(jnp.bfloat16)
    hidden = (pre_act * sig).astype(jnp.bfloat16)
    act_ref[...] = act_grad.reshape(act_ref.shape)
    edge_ref[0:2] = act_ref[pl.ds(2 * core, 2), odd]
    edge_ref[2:4] = act_ref[pl.ds(2 - 2 * core, 2), odd]

    @pl.when(core == 0)
    def _():
        before_ref[...] = act_ref[0:2]

    @pl.when(core == 1)
    def _():
        before_ref[:, 0] = act_ref[0:2, odd]
        before_ref[:, 1] = act_ref[0:2, odd]

    @pl.when(core == 0)
    def _():
        for a in range(3):
            for b in range(3):
                start = (a * 3 + b) * 384
                terms_ref[start : start + 384, :] = contract_first(stripe(triples_ref, a, 4, b), act_grad)

    @pl.when(core == 1)
    def _():
        for a in range(3):
            for b in range(3):
                part = contract_first(hidden, stripe(triples_ref, a, 4, b))
                for d in range(3):
                    start = ((2 - a) * 9 + (2 - b) * 3 + (2 - d)) * 128
                    terms_ref[start : start + 128, :] = part[:, d * 128 : (d + 1) * 128]

    @pl.when((core == 1) & (lax.axis_index("zh") == 0) & (lax.axis_index("y") == 0))
    def _():
        for f, a in ((0, 2), (0, 1), (1, 2)):
            for b in range(3):
                part = contract_first(hidden[0:128], stripe(triples_ref, f, 1, b))
                for d in range(3):
                    start = ((2 - a) * 9 + (2 - b) * 3 + (2 - d)) * 128
                    terms_ref[start : start + 128, :] += part[:, d * 128 : (d + 1) * 128]

    for y in range(4):
        for x in range(4):
            blocks = []
            for zh in range(2):
                for c in range(2):
                    start = 54 * (((zh * 4 + y) * 2 + c) * 4 + x)
                    blocks.append(terms_ref[start : start + 54, :])
            place0, place1 = PLANES[0].index(y * 4 + x), PLANES[1].index(16 + y * 4 + x)
            rank = jnp.where(lax.axis_index("zh") == 0, place0, place1)
            send_ref[rank] = jnp.concatenate(blocks, axis=0).astype(jnp.bfloat16)


def plane_sum_kernel(got_ref, send_ref, sum_ref):
    total = got_ref[0].astype(jnp.float32)
    for k in range(1, 16):
        total = total + got_ref[k].astype(jnp.float32)
    sum_ref[0:216] = total
    sum_ref[216:224] = jnp.zeros((8, 128), jnp.float32)
    lane = lax.broadcasted_iota(jnp.int32, (8, 128), 1)
    for zh in range(2):
        for zl in range(8):
            pieces = []
            for c in range(2):
                value = (zh * 2 + c) * 54 * 128 + zl * 864
                row, shift = value // 128, value % 128
                piece = sum_ref[row : row + 8, :]
                if shift:
                    after = sum_ref[row + 1 : row + 9, :]
                    piece = jnp.where(
                        lane < 128 - shift,
                        pltpu.roll(piece, 128 - shift, 1),
                        pltpu.roll(after, 128 - shift, 1),
                    )
                pieces.append(piece)
            send_ref[LINES[0].index(zh * 8 + zl)] = jnp.concatenate(pieces, axis=0).astype(jnp.bfloat16)


def line_sum_kernel(got_ref, sum_ref):
    total = got_ref[0].astype(jnp.float32)
    for k in range(1, 16):
        total = total + got_ref[k].astype(jnp.float32)
    sum_ref[...] = total


def place_kernel(scale, shares_ref, out_ref):
    for k in range(2):
        start = pl.multiple_of(16 * k + 8 * lax.axis_index("c"), 8)
        share = shares_ref[pl.ds(start, 8), :] * scale
        for r in range(7):
            width = min(128, 864 - 128 * r)
            out_ref[k : k + 1, 128 * r : 128 * r + width] = share[r : r + 1, :width]


def call(kernel, out_shape, *args, scratch=(), flops=0, aliases=None):
    many = isinstance(out_shape, (list, tuple))
    return pl.pallas_call(
        kernel,
        out_shape=out_shape,
        in_specs=[VMEM] * len(args),
        out_specs=[VMEM] * len(out_shape) if many else VMEM,
        scratch_shapes=scratch,
        input_output_aliases=aliases or {},
        compiler_params=pltpu.CompilerParams(vmem_limit_bytes=32 * 1024 * 1024),
        cost_estimate=pl.CostEstimate(flops=flops, bytes_accessed=0, transcendentals=0) if flops else None,
    )(*args)


def shaped(shape, dtype):
    return jax.ShapeDtypeStruct(shape, dtype)


def per_device(video_clip, first_kernel, second_kernel, cotangent):
    bf16, f32 = jnp.bfloat16, jnp.float32
    core = lax.axis_index("c")
    everywhere = TM + ROWS
    first_kernel, second_kernel = first_kernel.reshape(3456, 128), second_kernel.reshape(3456, 128)
    given = jnp.where(core == 0, cotangent, video_clip)
    mine = jnp.where(core == 0, video_clip, cotangent)
    given, clip, cot = lax.optimization_barrier((given, video_clip, cotangent))
    mine = jnp.where(core == 0, clip, cot)
    both = lax.all_gather(given, "c", tiled=True)
    both, given = lax.optimization_barrier((both, given))
    beyond_far = lax.ppermute(given, TM, BEYOND_FAR)
    beyond = lax.ppermute(given, TM, BEYOND)
    edge, corner = call(
        edge_kernel,
        (shaped((6, 64, 128), bf16), shaped((2, 64, 128), bf16)),
        mine, both, beyond,
    )
    far = lax.ppermute(edge, ROWS, FAR_ROWS)
    free = lax.ppermute(corner, everywhere, CORNER_FREE)
    source, inner, corner = call(
        assemble_kernel,
        (shaped((6, 2, 64, 128), bf16), shaped((6, 64, 128), bf16), shaped((2, 64, 128), bf16)),
        mine, both, beyond, beyond_far, free,
    )
    inner, corner, second = lax.optimization_barrier((inner, corner, second_kernel))
    kernel = jnp.where(core == 0, first_kernel, second)
    near = lax.ppermute(inner, ROWS, NEAR_ROWS)
    corner = lax.ppermute(corner, everywhere, CORNER_ROWS)
    inner, triples, taps = call(
        first_inner_kernel,
        (shaped((2, 256, 128), f32), shaped((6, 4, 64, 384), bf16), shaped((9, 384, 128), bf16)),
        source, kernel,
        flops=300_000_000,
    )
    own, triples = call(
        first_outer_kernel,
        (shaped((512, 128), f32), shaped((6, 4, 64, 384), bf16)),
        inner, triples, taps, far, near, corner,
        scratch=[pltpu.VMEM((6, 64, 128), bf16), pltpu.VMEM((2, 256, 128), f32)],
        aliases={1: 1},
    )
    both = lax.all_gather(own, "c", tiled=True)
    send, act_grad, edge, before = call(
        grads_kernel,
        (
            shaped((16, 216, 128), bf16), shaped((4, 2, 64, 128), bf16),
            shaped((4, 64, 128), bf16), shaped((2, 2, 64, 128), bf16),
        ),
        both, triples,
        scratch=[pltpu.VMEM((3456, 128), f32)],
    )
    got = lax.all_to_all(send, ("zh", "y", "x"), 0, 0, axis_index_groups=PLANES, tiled=True)
    before = lax.ppermute(before, everywhere, BEFORE)
    far = lax.ppermute(edge, ROWS, FAR_ROWS)
    send = call(plane_sum_kernel, shaped((16, 16, 128), bf16), got, scratch=[pltpu.VMEM((224, 128), f32)])
    got = lax.all_to_all(send, ("zh", "zl"), 0, 0, axis_index_groups=LINES, tiled=True)
    _, before, far = lax.optimization_barrier((send, before, far))
    source, inner, corner = call(
        assemble_grad_kernel,
        (shaped((4, 2, 64, 128), bf16), shaped((4, 64, 128), bf16), shaped((2, 64, 128), bf16)),
        act_grad, before, far,
    )
    near = lax.ppermute(inner, ROWS, NEAR_ROWS)
    corner = lax.ppermute(corner, everywhere, CORNER_GRAD)
    inner, triples, taps = call(
        input_inner_kernel,
        (shaped((2, 128, 128), f32), shaped((4, 4, 64, 384), bf16), shaped((9, 384, 128), bf16)),
        source, first_kernel,
        flops=150_000_000,
    )
    input_grad, _ = call(
        input_outer_kernel,
        (shaped((2, 2, 64, 128), bf16), shaped((4, 4, 64, 384), bf16)),
        inner, taps, far, corner, near, cotangent, triples,
        scratch=[pltpu.VMEM((4, 64, 128), bf16), pltpu.VMEM((2, 128, 128), f32)],
        aliases={6: 1},
        flops=1_600_000_000,
    )
    got, input_grad = lax.optimization_barrier((got, input_grad))
    scale = 1.0 / math.sqrt(131072)
    shares = call(line_sum_kernel, shaped((16, 128), f32), got)
    shares = lax.all_gather(shares, "c", tiled=True)
    weight_grads = call(lambda *refs: place_kernel(scale, *refs), shaped((2, 864), f32), shares)
    return input_grad, weight_grads


def solution(mesh):
    fine = Mesh(np.asarray(mesh.devices).reshape(2, 4, 2, 4, 8), TM + ROWS)
    return jax.shard_map(
        per_device,
        mesh=fine,
        in_specs=(P(TM, ROWS, None, None), P(), P(), P(TM, ROWS, None, None)),
        out_specs=(P(TM, ROWS, None, None), P(None, TM + ROWS)),
        check_vma=False,
    )
```

```python
import math

import jax
import jax.numpy as jnp
import numpy as np
from jax import lax
from jax.experimental import pallas as pl
from jax.experimental.pallas import tpu as pltpu
from jax.sharding import Mesh, PartitionSpec as P

TM = ("zh", "y", "c")
ROWS = ("x", "zl")
VMEM = pl.BlockSpec(memory_space=pltpu.VMEM)


NEAR_ROWS = [(r, r ^ 1) for r in range(32)]
FAR_ROWS = [(r, r + 1) for r in range(1, 31, 2)] + [(r + 1, r) for r in range(1, 31, 2)]
ENDS = [(r, q) for r, q in FAR_ROWS if r // 8 != q // 8]
MIDDLES = [(r, q) for r, q in FAR_ROWS if r // 8 == q // 8]
ENDS_OF = [r for r, _ in ENDS]


PLANES = [
    [half * 16 + (2 - y) % 4 * 4 + (x + 2) % 4 for y in range(4) for x in range(4)] for half in range(2)
]


LINES = [[(12 + z) % 16 for z in range(16)]]


def device(chip, core, slab):
    return (2 * chip + core) * 32 + slab


BEYOND = [pair for k in (0, 1, 2, 4, 5, 6) for pair in ((2 * k + 1, 2 * k + 2), (2 * k + 2, 2 * k + 1))]
BEYOND_FAR = [(7, 8), (8, 7)]
CORNER_FREE = [(device(3, 0, r), device(4, 1, q)) for r, q in ENDS] + [
    (device(4, 1, r), device(3, 0, q)) for r, q in ENDS
]
CORNER_ROWS = [(device(k, c, r), device(k, c, q)) for k, c in ((3, 1), (4, 0)) for r, q in MIDDLES] + [
    (device(k, c, r), device(k, 1 - c, r)) for k, c in ((3, 0), (4, 1)) for r in ENDS_OF
]
BEFORE = [(device(k + 1, 0, r), device(k, 1, r)) for k in range(7) for r in range(32)] + [
    (device(4, 1, r), device(3, 0, q)) for r, q in ENDS
]
CORNER_GRAD = (
    [(device(k, 1, r), device(k, 1, q)) for k in range(7) for r, q in MIDDLES]
    + [(device(k + 1, 1, r), device(k, 1, r)) for k in (0, 1, 2, 4, 5, 6) for r in ENDS_OF]
    + [(device(3, 0, r), device(3, 1, r)) for r in ENDS_OF]
)


def place():
    core = lax.axis_index("c")
    chip = lax.axis_index("zh") * 4 + lax.axis_index("y")
    odd = lax.axis_index("zl") & 1
    end = (lax.axis_index("zl") == 0) | (lax.axis_index("zl") == 7)
    return core, chip, end, odd


def contract_first(lhs, rhs):
    return lax.dot_general(lhs, rhs, (((0,), (0,)), ((), ())), preferred_element_type=jnp.float32)


def side_by_side(cells):
    columns, chans = cells.shape
    col = lax.broadcasted_iota(jnp.int32, (columns, chans), 0)
    wide = cells.astype(jnp.float32)
    before = jnp.where(col == 0, 0.0, pltpu.roll(wide, 1, 0)).astype(cells.dtype)
    after = jnp.where(col == columns - 1, 0.0, pltpu.roll(wide, columns - 1, 0)).astype(cells.dtype)
    return jnp.concatenate([before, cells, after], axis=1)


def fill_inner(src_ref, triples_ref, frames):
    for f in range(frames):
        for r in range(2):
            triples_ref[f, r + 1] = side_by_side(src_ref[f, r])


def fill_outer(far_ref, near_ref, triples_ref, frames):
    odd = place()[3]
    for f in range(frames):
        triples_ref[f, 0] = side_by_side(jnp.where(odd == 0, far_ref[f], near_ref[f]))
        triples_ref[f, 3] = side_by_side(jnp.where(odd == 1, far_ref[f], near_ref[f]))


def stripe(triples_ref, f, count, b):
    part = triples_ref[f : f + count, b : b + 2]
    return part.reshape(count * 2 * part.shape[2], part.shape[3])


def turned(kernel_ref, a, b):
    starts = [((2 - a) * 9 + (2 - b) * 3 + (2 - d)) * 128 for d in range(3)]
    return jnp.concatenate([kernel_ref[start : start + 128, :] for start in starts], axis=1)


def stage_taps(kernel_ref, taps_ref, back):
    for a in range(3):
        for b in range(3):
            if back:
                taps_ref[a * 3 + b] = turned(kernel_ref, a, b).T
            else:
                taps_ref[a * 3 + b] = kernel_ref[(a * 3 + b) * 384 : (a * 3 + b + 1) * 384, :]


INNER = (((1, 1), (2, 2)), ((0, 1), (1, 2)))
OUTER = (((0, 0),), ((2, 3),))
TAPS = ((0, 0), (1, 1), (2, 2))
FOLD = ((0, 2), (0, 1), (1, 2))


def row_terms(triples_ref, taps_ref, frames, pairs, times):
    total = None
    for f, a in times:
        for b, row in pairs:
            part = triples_ref[f : f + frames, row].reshape(frames * 64, 384)
            term = jnp.dot(part, taps_ref[a * 3 + b], preferred_element_type=jnp.float32)
            total = term if total is None else total + term
    return total


def add_rows(triples_ref, taps_ref, sum_ref, frames, rows, fresh, fold):
    for row in range(2):
        term = row_terms(triples_ref, taps_ref, frames, rows[row], TAPS)
        sum_ref[row] = term if fresh else sum_ref[row] + term

    @pl.when(fold)
    def _():
        for row in range(2):
            sum_ref[row, 0:64, :] += row_terms(triples_ref, taps_ref, 1, rows[row], FOLD)


def interleaved(sum_ref, frames):
    rows = [sum_ref[r, f * 64 : (f + 1) * 64, :] for f in range(frames) for r in range(2)]
    return jnp.concatenate(rows, axis=0)


def edge_kernel(mine_ref, both_ref, beyond_ref, edge_ref, corner_ref):
    core, chip, _, odd = place()
    other_ref = both_ref.at[pl.ds(2 - 2 * core, 2)]
    corner_ref[...] = other_ref[:, odd]
    edge_ref[pl.ds(4 * core, 2)] = beyond_ref[:, odd]
    edge_ref[2:4] = mine_ref[:, odd]
    edge_ref[pl.ds(4 - 4 * core, 2)] = other_ref[:, odd]

    @pl.when((core == 0) & (chip == 0))
    def _():
        edge_ref[0] = mine_ref[0, odd]
        edge_ref[1] = mine_ref[0, odd]


def assemble_kernel(mine_ref, both_ref, beyond_ref, beyond_far_ref, free_ref, src_ref, inner_ref, corner_ref):
    core, chip, end, odd = place()
    src_ref[pl.ds(4 * core, 2)] = beyond_ref[...] + beyond_far_ref[...]
    src_ref[2:4] = mine_ref[...]
    src_ref[pl.ds(4 - 4 * core, 2)] = both_ref[pl.ds(2 - 2 * core, 2)]

    @pl.when((core == 0) & (chip == 0))
    def _():
        src_ref[0] = mine_ref[0]
        src_ref[1] = mine_ref[0]

    inner_ref[...] = src_ref[:, 1 - odd]
    corner_ref[...] = jnp.where(end, free_ref[...], beyond_far_ref[:, odd])


def first_inner_kernel(src_ref, kernel_ref, sum_ref, triples_ref, taps_ref):
    core, chip, _, _ = place()
    fill_inner(src_ref, triples_ref, 6)

    @pl.when(core == 0)
    def _():
        stage_taps(kernel_ref, taps_ref, False)

    @pl.when(core == 1)
    def _():
        stage_taps(kernel_ref, taps_ref, True)

    add_rows(triples_ref, taps_ref, sum_ref, 4, INNER, True, (core == 1) & (chip == 0))


def first_outer_kernel(
    inner_ref, triples_in_ref, taps_ref, far_ref, near_ref, corner_ref, out_ref, triples_ref, outer_ref, sum_ref
):
    core, chip, _, _ = place()
    outer_ref[...] = far_ref[...]
    outer_ref[pl.ds(4 * core, 2)] += corner_ref[...]
    fill_outer(outer_ref, near_ref, triples_ref, 6)
    sum_ref[...] = inner_ref[...]
    add_rows(triples_ref, taps_ref, sum_ref, 4, OUTER, False, (core == 1) & (chip == 0))
    out_ref[...] = interleaved(sum_ref, 4)


def assemble_grad_kernel(act_ref, before_ref, far_ref, src_ref, inner_ref, corner_ref):
    core, _, end, odd = place()

    @pl.when(core == 0)
    def _():
        src_ref[...] = act_ref[...]
        corner_ref[...] = before_ref[:, 0]

    @pl.when(core == 1)
    def _():
        src_ref[0:2] = act_ref[2:4]
        src_ref[2:4] = before_ref[...]
        corner_ref[...] = jnp.where(end, far_ref[2:4], before_ref[:, odd])

    inner_ref[...] = src_ref[:, 1 - odd]


def input_inner_kernel(src_ref, kernel_ref, sum_ref, triples_ref, taps_ref):
    core, chip, _, _ = place()
    fill_inner(src_ref, triples_ref, 4)
    stage_taps(kernel_ref, taps_ref, True)
    add_rows(triples_ref, taps_ref, sum_ref, 2, INNER, True, (core == 0) & (chip == 0))


def input_outer_kernel(
    inner_ref, taps_ref, far_ref, corner_ref, near_ref, cot_ref, triples_in_ref, out_ref, triples_ref, outer_ref,
    sum_ref
):
    core, chip, _, _ = place()
    outer_ref[...] = far_ref[...]

    @pl.when(core == 1)
    def _():
        outer_ref[2:4] = corner_ref[...]

    fill_outer(outer_ref, near_ref, triples_ref, 4)
    sum_ref[...] = inner_ref[...]
    add_rows(triples_ref, taps_ref, sum_ref, 2, OUTER, False, (core == 0) & (chip == 0))
    cot = cot_ref[...].reshape(256, 128).astype(jnp.float32)
    out_ref[...] = (cot + interleaved(sum_ref, 2)).astype(jnp.bfloat16).reshape(out_ref.shape)


def grads_kernel(both_ref, triples_ref, send_ref, act_ref, edge_ref, before_ref, terms_ref):
    core, _, _, odd = place()
    pre_act = both_ref[0:512, :].astype(jnp.bfloat16).astype(jnp.float32)
    back_grad = both_ref[512:1024, :]
    sig = 1.0 / (1.0 + jnp.exp(-pre_act))
    act_grad = (back_grad * (sig * (1.0 + pre_act * (1.0 - sig)))).astype(jnp.bfloat16)
    hidden = (pre_act * sig).astype(jnp.bfloat16)
    act_ref[...] = act_grad.reshape(act_ref.shape)
    edge_ref[0:2] = act_ref[pl.ds(2 * core, 2), odd]
    edge_ref[2:4] = act_ref[pl.ds(2 - 2 * core, 2), odd]

    @pl.when(core == 0)
    def _():
        before_ref[...] = act_ref[0:2]

    @pl.when(core == 1)
    def _():
        before_ref[:, 0] = act_ref[0:2, odd]
        before_ref[:, 1] = act_ref[0:2, odd]

    @pl.when(core == 0)
    def _():
        for a in range(3):
            for b in range(3):
                start = (a * 3 + b) * 384
                terms_ref[start : start + 384, :] = contract_first(stripe(triples_ref, a, 4, b), act_grad)

    @pl.when(core == 1)
    def _():
        for a in range(3):
            for b in range(3):
                part = contract_first(hidden, stripe(triples_ref, a, 4, b))
                for d in range(3):
                    start = ((2 - a) * 9 + (2 - b) * 3 + (2 - d)) * 128
                    terms_ref[start : start + 128, :] = part[:, d * 128 : (d + 1) * 128]

    @pl.when((core == 1) & (lax.axis_index("zh") == 0) & (lax.axis_index("y") == 0))
    def _():
        for f, a in ((0, 2), (0, 1), (1, 2)):
            for b in range(3):
                part = contract_first(hidden[0:128], stripe(triples_ref, f, 1, b))
                for d in range(3):
                    start = ((2 - a) * 9 + (2 - b) * 3 + (2 - d)) * 128
                    terms_ref[start : start + 128, :] += part[:, d * 128 : (d + 1) * 128]

    for y in range(4):
        for x in range(4):
            blocks = []
            for zh in range(2):
                for c in range(2):
                    start = 54 * (((zh * 4 + y) * 2 + c) * 4 + x)
                    blocks.append(terms_ref[start : start + 54, :])
            place0, place1 = PLANES[0].index(y * 4 + x), PLANES[1].index(16 + y * 4 + x)
            rank = jnp.where(lax.axis_index("zh") == 0, place0, place1)
            send_ref[rank] = jnp.concatenate(blocks, axis=0).astype(jnp.bfloat16)


def plane_sum_kernel(got_ref, send_ref, sum_ref):
    total = got_ref[0].astype(jnp.float32)
    for k in range(1, 16):
        total = total + got_ref[k].astype(jnp.float32)
    sum_ref[0:216] = total
    sum_ref[216:224] = jnp.zeros((8, 128), jnp.float32)
    lane = lax.broadcasted_iota(jnp.int32, (8, 128), 1)
    for zh in range(2):
        for zl in range(8):
            pieces = []
            for c in range(2):
                value = (zh * 2 + c) * 54 * 128 + zl * 864
                row, shift = value // 128, value % 128
                piece = sum_ref[row : row + 8, :]
                if shift:
                    after = sum_ref[row + 1 : row + 9, :]
                    piece = jnp.where(
                        lane < 128 - shift,
                        pltpu.roll(piece, 128 - shift, 1),
                        pltpu.roll(after, 128 - shift, 1),
                    )
                pieces.append(piece)
            send_ref[LINES[0].index(zh * 8 + zl)] = jnp.concatenate(pieces, axis=0).astype(jnp.bfloat16)


def line_sum_kernel(got_ref, sum_ref):
    total = got_ref[0].astype(jnp.float32)
    for k in range(1, 16):
        total = total + got_ref[k].astype(jnp.float32)
    sum_ref[...] = total


def place_kernel(scale, shares_ref, out_ref):
    for k in range(2):
        start = pl.multiple_of(16 * k + 8 * lax.axis_index("c"), 8)
        share = shares_ref[pl.ds(start, 8), :] * scale
        for r in range(7):
            width = min(128, 864 - 128 * r)
            out_ref[k : k + 1, 128 * r : 128 * r + width] = share[r : r + 1, :width]


def call(kernel, out_shape, *args, scratch=(), flops=0, aliases=None):
    many = isinstance(out_shape, (list, tuple))
    return pl.pallas_call(
        kernel,
        out_shape=out_shape,
        in_specs=[VMEM] * len(args),
        out_specs=[VMEM] * len(out_shape) if many else VMEM,
        scratch_shapes=scratch,
        input_output_aliases=aliases or {},
        compiler_params=pltpu.CompilerParams(vmem_limit_bytes=32 * 1024 * 1024),
        cost_estimate=pl.CostEstimate(flops=flops, bytes_accessed=0, transcendentals=0) if flops else None,
    )(*args)


def shaped(shape, dtype):
    return jax.ShapeDtypeStruct(shape, dtype)


def per_device(video_clip, first_kernel, second_kernel, cotangent):
    bf16, f32 = jnp.bfloat16, jnp.float32
    core = lax.axis_index("c")
    everywhere = TM + ROWS
    first_kernel, second_kernel = first_kernel.reshape(3456, 128), second_kernel.reshape(3456, 128)
    given = jnp.where(core == 0, cotangent, video_clip)
    mine = jnp.where(core == 0, video_clip, cotangent)
    given, mine = lax.optimization_barrier((given, mine))
    both = lax.all_gather(given, "c", tiled=True)
    both, given = lax.optimization_barrier((both, given))
    beyond_far = lax.ppermute(given, TM, BEYOND_FAR)
    beyond = lax.ppermute(given, TM, BEYOND)
    edge, corner = call(
        edge_kernel,
        (shaped((6, 64, 128), bf16), shaped((2, 64, 128), bf16)),
        mine, both, beyond,
    )
    far = lax.ppermute(edge, ROWS, FAR_ROWS)
    free = lax.ppermute(corner, everywhere, CORNER_FREE)
    source, inner, corner = call(
        assemble_kernel,
        (shaped((6, 2, 64, 128), bf16), shaped((6, 64, 128), bf16), shaped((2, 64, 128), bf16)),
        mine, both, beyond, beyond_far, free,
    )
    inner, corner, second = lax.optimization_barrier((inner, corner, second_kernel))
    kernel = jnp.where(core == 0, first_kernel, second)
    near = lax.ppermute(inner, ROWS, NEAR_ROWS)
    corner = lax.ppermute(corner, everywhere, CORNER_ROWS)
    inner, triples, taps = call(
        first_inner_kernel,
        (shaped((2, 256, 128), f32), shaped((6, 4, 64, 384), bf16), shaped((9, 384, 128), bf16)),
        source, kernel,
        flops=300_000_000,
    )
    own, triples = call(
        first_outer_kernel,
        (shaped((512, 128), f32), shaped((6, 4, 64, 384), bf16)),
        inner, triples, taps, far, near, corner,
        scratch=[pltpu.VMEM((6, 64, 128), bf16), pltpu.VMEM((2, 256, 128), f32)],
        aliases={1: 1},
    )
    both = lax.all_gather(own, "c", tiled=True)
    send, act_grad, edge, before = call(
        grads_kernel,
        (
            shaped((16, 216, 128), bf16), shaped((4, 2, 64, 128), bf16),
            shaped((4, 64, 128), bf16), shaped((2, 2, 64, 128), bf16),
        ),
        both, triples,
        scratch=[pltpu.VMEM((3456, 128), f32)],
    )
    got = lax.all_to_all(send, ("zh", "y", "x"), 0, 0, axis_index_groups=PLANES, tiled=True)
    before = lax.ppermute(before, everywhere, BEFORE)
    far = lax.ppermute(edge, ROWS, FAR_ROWS)
    send = call(plane_sum_kernel, shaped((16, 16, 128), bf16), got, scratch=[pltpu.VMEM((224, 128), f32)])
    got = lax.all_to_all(send, ("zh", "zl"), 0, 0, axis_index_groups=LINES, tiled=True)
    _, before, far = lax.optimization_barrier((send, before, far))
    source, inner, corner = call(
        assemble_grad_kernel,
        (shaped((4, 2, 64, 128), bf16), shaped((4, 64, 128), bf16), shaped((2, 64, 128), bf16)),
        act_grad, before, far,
    )
    near = lax.ppermute(inner, ROWS, NEAR_ROWS)
    corner = lax.ppermute(corner, everywhere, CORNER_GRAD)
    inner, triples, taps = call(
        input_inner_kernel,
        (shaped((2, 128, 128), f32), shaped((4, 4, 64, 384), bf16), shaped((9, 384, 128), bf16)),
        source, first_kernel,
        flops=150_000_000,
    )
    input_grad, _ = call(
        input_outer_kernel,
        (shaped((2, 2, 64, 128), bf16), shaped((4, 4, 64, 384), bf16)),
        inner, taps, far, corner, near, cotangent, triples,
        scratch=[pltpu.VMEM((4, 64, 128), bf16), pltpu.VMEM((2, 128, 128), f32)],
        aliases={6: 1},
        flops=1_600_000_000,
    )
    got, input_grad = lax.optimization_barrier((got, input_grad))
    scale = 1.0 / math.sqrt(131072)
    shares = call(line_sum_kernel, shaped((16, 128), f32), got)
    shares = lax.all_gather(shares, "c", tiled=True)
    weight_grads = call(lambda *refs: place_kernel(scale, *refs), shaped((2, 864), f32), shares)
    return input_grad, weight_grads


def solution(mesh):
    fine = Mesh(np.asarray(mesh.devices).reshape(2, 4, 2, 4, 8), TM + ROWS)
    return jax.shard_map(
        per_device,
        mesh=fine,
        in_specs=(P(TM, ROWS, None, None), P(), P(), P(TM, ROWS, None, None)),
        out_specs=(P(TM, ROWS, None, None), P(None, TM + ROWS)),
        check_vma=False,
    )
```
